32 devices in a mesh: dp: 16 (over z, y, x), pipe: 2 (over core).
Axes of the slice: x: 2, y: 2, z: 4, core: 2. Of those that a mesh axis runs over, the one named last changes fastest.
Arguments:
- section_input: bfloat16 [2, 32, 512, 768], P('pipe', 'dp'), may hold values from -6 to 6
- visible_slot: int32 [32, 512], P('dp'), may hold values from 0 to 128, as said below
- image_of_slot: int32 [32, 512], P('dp'), may hold values from 0 to 1, as said below
- qkv_weight: bfloat16 [2, 768, 2304], P('pipe'), may hold values from -0.21875 to 0.21875
- out_weight: bfloat16 [2, 768, 768], P('pipe'), may hold values from -1.25 to 1.25
- up_weight: bfloat16 [2, 768, 3072], P('pipe'), may hold values from -0.21875 to 0.21875
- down_weight: bfloat16 [2, 3072, 768], P('pipe'), may hold values from -0.21875 to 0.21875
- norm_gain: float32 [2, 2, 768], P('pipe'), may hold values from 0.5 to 1.5
- up_bias: float32 [2, 3072], P('pipe'), may hold values from -3 to 3
- vectors: float32 [2, 7, 768], P('pipe'), may hold values from -3 to 3
Outputs:
- results: bfloat16 [2, 32, 512, 768], P('pipe', 'dp')
- qkv_weight_grad: float32 [2, 768, 2304], P('pipe', 'dp')
- out_weight_grad: float32 [2, 768, 768], P('pipe', 'dp')
- up_weight_grad: float32 [2, 768, 3072], P('pipe', 'dp')
- down_weight_grad: float32 [2, 3072, 768], P('pipe', 'dp')
- norm_gain_grad: float32 [2, 2, 768], P('pipe', None, 'dp')
- up_bias_grad: float32 [2, 3072], P('pipe', 'dp')
- vectors_grad: float32 [2, 7, 768], P('pipe', None, 'dp')
The draws below stay inside these ranges and needn't reach their ends.
Inputs may be any that keep to these rules, and one draw needn't show every extreme that they name: `visible_slot`: in each micro-batch the visible slots carry the places 0, 1, 2, ... in slot order; at least 96 slots are visible, and some micro-batch has exactly 128. `image_of_slot`: each micro-batch holds either one image on all 512 slots (all 0) or two images of 256 consecutive slots numbered 0 and 1; both kinds occur.
All inputs are finite; a program needn't handle non-finite values.
Results may differ from the reference program's by a relative error of at most 0.0095.
Values may be sent and summed in bfloat16 or wider, within the bound.
No kernel may reach another device: no remote copies, remote signals or barrier semaphores. Data moves between devices by JAX's collectives and lax.ppermute only.
A program may use at most 320 MiB of HBM per device.

```python
import math
import jax
import jax.numpy as jnp
from jax import lax

D = 768
H = 12
HD = 64
FF = 3072
S = 512
VIS = 128
MB_ALL = 32


def draw_visible_slot(key, part):
    key = jax.random.fold_in(key, 11)
    first, second, third = jax.random.split(key, 3)
    shortfall = jax.random.randint(first, (MB_ALL,), 0, VIS // 4 + 1)
    full_row = jax.random.randint(second, (), 0, MB_ALL)
    visible_count = jnp.where(jnp.arange(MB_ALL) == full_row, VIS, VIS - shortfall)
    noise = jax.random.randint(third, (MB_ALL, S), 0, 2 ** 20) * S + jnp.arange(S)[None, :]
    ranking = jnp.argsort(jnp.argsort(noise, axis=1), axis=1)
    visible = (ranking < visible_count[:, None]).astype(jnp.int32)
    placing = jnp.cumsum(visible, axis=1) - 1
    return jnp.where(visible == 1, placing, VIS).astype(jnp.int32)


def draw_image_of_slot(key, part):
    key = jax.random.fold_in(key, 12)
    first, second = jax.random.split(key, 2)
    whole = jax.random.randint(first, (MB_ALL,), 0, 2)
    picks = jax.random.randint(second, (2,), 0, MB_ALL)
    rows_all = jnp.arange(MB_ALL)
    whole = jnp.where(rows_all == picks[1], 1, whole)
    whole = jnp.where(rows_all == picks[0], 0, whole)
    halves = (jnp.arange(S) // (S // 2))[None, :]
    return jnp.where(whole[:, None] == 1, 0, halves).astype(jnp.int32)


def steps_of(stream_key, shape, shards, least, high):
    def one(axis_at, blocks):
        heights = jax.random.uniform(jax.random.fold_in(jax.random.fold_in(stream_key, 6), axis_at), (blocks,), jnp.float32, least / len(shards), high / len(shards))
        return jnp.repeat(jnp.exp(heights), shape[axis_at] // blocks).reshape((-1,) + (1,) * (len(shape) - axis_at - 1))

    loudness = one(*shards[0])
    for cut in shards[1:]:
        loudness = loudness * one(*cut)
    return loudness


def centred(key, dims, width, reach, shards=(), kind=jnp.bfloat16):
    values = jax.random.normal(key, dims, jnp.float32) * width
    if len(shards) > 0:
        values = steps_of(key, dims, shards, -0.22, 0.18) * values
    return jnp.clip(values, min=-reach, max=reach).astype(kind)


def setup_inputs(seed: int = 0) -> dict:
    arg_keys = jax.random.split(jax.random.key(seed), 11)
    return {
        "section_input": centred(arg_keys[0], (2, MB_ALL, S, D), 1.0, 6.0, ((0, 2), (1, 16))),
        "visible_slot": draw_visible_slot(jax.random.fold_in(arg_keys[10], 71), 0),
        "image_of_slot": draw_image_of_slot(jax.random.fold_in(arg_keys[10], 71), 0),
        "qkv_weight": centred(arg_keys[3], (2, D, 3 * D), D ** -0.5, 0.21875, ((0, 2),)),
        "out_weight": centred(arg_keys[4], (2, D, D), (D // 32) ** -0.5, 1.25, ((0, 2),)),
        "up_weight": centred(arg_keys[5], (2, D, FF), D ** -0.5, 0.21875, ((0, 2),)),
        "down_weight": centred(arg_keys[6], (2, FF, D), (FF // 4) ** -0.5, 0.21875, ((0, 2),)),
        "norm_gain": jnp.clip(1.0 + 0.1 * jax.random.normal(arg_keys[7], (2, 2, D), jnp.float32), 0.5, 1.5),
        "up_bias": centred(arg_keys[8], (2, FF), 0.5, 3.0, ((0, 2),), jnp.float32),
        "vectors": centred(arg_keys[9], (2, 7, D), 0.5, 3.0, ((0, 2),), jnp.float32),
    }


PRECISE = lax.Precision.HIGHEST
EPSILON = 1e-06

@jax.custom_vjp
def low(v):
    return lax.optimization_barrier(v.astype(jnp.bfloat16)).astype(jnp.float32)

@jax.custom_vjp
def low_back(v):
    return v

def low_keep(v):
    return (low(v), None)

def low_pass(kept, grad):
    return (grad,)

def back_keep(v):
    return (v, None)

def back_low(kept, grad):
    return (low(grad),)
low.defvjp(low_keep, low_pass)
low_back.defvjp(back_keep, back_low)

def matmul(left, right):
    return jnp.dot(left, right, precision=PRECISE, preferred_element_type=jnp.float32)

def layer_norm(inputs, gain_vec, shift_vec):
    row_mean = lax.optimization_barrier(jnp.mean(inputs, axis=-1, keepdims=True))
    centered = inputs - row_mean
    variance = lax.optimization_barrier(jnp.mean(centered * centered, axis=-1, keepdims=True))
    return centered * lax.rsqrt(variance + EPSILON) * gain_vec + shift_vec

def positions(slot_count, model_width):
    half_width = model_width // 2
    frequency = jnp.exp(jnp.arange(half_width, dtype=jnp.float32) * (-math.log(10000.0) / half_width))
    angles = jnp.arange(slot_count, dtype=jnp.float32)[:, None] * frequency[None, :]
    return jnp.concatenate([jnp.sin(angles), jnp.cos(angles)], axis=1)

def run_block(inputs, group_ids, w_qkv, w_out, w_up, w_down, gains, hidden_bias, vecs):
    length_rows = inputs.shape[0]
    normed = low(layer_norm(inputs, gains[0], vecs[0]))
    qkv_bias = jnp.concatenate([vecs[1], jnp.zeros_like(vecs[1]), vecs[2]])
    packed = low(low_back(matmul(normed, w_qkv) + qkv_bias))
    pieces = packed.reshape(length_rows, 3, H, HD)
    queries, keys_all, values = (pieces[:, 0], pieces[:, 1], pieces[:, 2])
    scores = low_back(jnp.einsum('qhd,khd->hqk', queries, keys_all, precision=PRECISE) * HD ** (-0.5))
    allowed = (group_ids[:, None] == group_ids[None, :])[None]
    scores = jnp.where(allowed, scores, -1e+30)
    row_top = lax.optimization_barrier(jnp.max(scores, axis=-1, keepdims=True))
    raised = jnp.exp(scores - row_top)
    probs = low(raised / lax.optimization_barrier(jnp.sum(raised, axis=-1, keepdims=True)))
    attended = jnp.einsum('hqk,khd->qhd', probs, values, precision=PRECISE).reshape(length_rows, H * HD)
    attended = low(low_back(attended))
    branch = low_back(matmul(attended, w_out) + vecs[3])
    middle = inputs + branch
    normed_two = low(layer_norm(middle, gains[1], vecs[5]))
    preact = low_back(matmul(normed_two, w_up) + hidden_bias)
    activated = low(jax.nn.gelu(preact, approximate=False))
    feed = low_back(matmul(activated, w_down) + vecs[6])
    return middle + feed

def one_batch(params, patches, slot_map, images):
    w_qkv, w_out, w_up, w_down, gains, hidden_bias, vecs = params
    slot_hit = slot_map[:, None] == jnp.arange(VIS)[None, :]
    selector = slot_hit.astype(jnp.float32)
    group_ids = jnp.where(jnp.any(slot_hit, axis=0), lax.optimization_barrier(jnp.sum(jnp.where(slot_hit, images[:, None], 0), axis=0)), -1).astype(jnp.int32)
    entry_rows = jnp.einsum('sv,sd->vd', selector, patches, precision=PRECISE) + vecs[0, 4]
    encoded = run_block(entry_rows, group_ids, w_qkv[0], w_out[0], w_up[0], w_down[0], gains[0], hidden_bias[0], vecs[0])
    sent = low_back(low(encoded))
    masked = (slot_map == VIS).astype(jnp.float32)[:, None]
    dec_input = matmul(selector, sent) + masked * vecs[1, 4] + positions(S, D)
    return run_block(dec_input, images.astype(jnp.int32), w_qkv[1], w_out[1], w_up[1], w_down[1], gains[1], hidden_bias[1], vecs[1])

def forward(params, patches, visible_slot, image_of_slot):

    def one_micro(pieces):
        return one_batch(params, pieces[0], pieces[1], pieces[2])
    return lax.map(jax.checkpoint(one_micro), (patches, visible_slot, image_of_slot))

def reference(section_input, visible_slot, image_of_slot, qkv_weight, out_weight, up_weight, down_weight, norm_gain, up_bias, vectors):
    params = (qkv_weight.astype(jnp.float32), out_weight.astype(jnp.float32), up_weight.astype(jnp.float32), down_weight.astype(jnp.float32), norm_gain.astype(jnp.float32), up_bias.astype(jnp.float32), vectors.astype(jnp.float32))
    patches = section_input[0].astype(jnp.float32)
    cotangent = section_input[1].astype(jnp.float32)
    decoded, pull_back = jax.vjp(lambda prm, pat: forward(prm, pat, visible_slot, image_of_slot), params, patches)
    grad_params, grad_patches = pull_back(cotangent)
    results = jnp.stack([grad_patches, decoded]).astype(jnp.bfloat16)
    return (results, grad_params[0], grad_params[1], grad_params[2], grad_params[3], grad_params[4], grad_params[5], grad_params[6])
```

```python
import functools
import math

import jax
import jax.numpy as jnp
import numpy as np
from jax import lax
from jax.experimental import pallas as pl
from jax.experimental.pallas import tpu as pltpu
from jax.sharding import PartitionSpec as P

D = 768
H = 12
HD = 64
FF = 3072
S = 512
VIS = 128
MICRO = 2
EPSILON = 1e-06
PAIRS = H // 2
TWO = 2 * HD
TILES = FF // D
HALF = D // 2
GROUPS = 16
GROUP_ROWS = D // GROUPS
ROWS = 16
F32 = jnp.float32
BF16 = jnp.bfloat16

SHIFT1, QBIAS, VBIAS, OBIAS, ENTRY, SHIFT2, DBIAS, GAIN1, GAIN2, UBIAS = range(10)


def contract(left, right, left_dim, right_dim):
    return lax.dot_general(
        left, right, (((left_dim,), (right_dim,)), ((), ())), preferred_element_type=F32
    )


def nn(left, right):
    return contract(left, right, 1, 0)


def nt(left, right):
    return contract(left, right, 1, 1)


def unit_rows(rows):
    centered = rows - jnp.mean(rows, axis=-1, keepdims=True)
    scale = lax.rsqrt(jnp.mean(centered * centered, axis=-1, keepdims=True) + EPSILON)
    return centered * scale, scale


def unit_rows_back(grad, unit, scale, gain):
    scaled = grad * gain
    return scale * (
        scaled
        - jnp.mean(scaled, axis=-1, keepdims=True)
        - unit * jnp.mean(scaled * unit, axis=-1, keepdims=True)
    )


def one_head(pair, which):
    lane = lax.broadcasted_iota(jnp.int32, pair.shape, 1)
    inside = lane < HD if which == 0 else lane >= HD
    return jnp.where(inside, pair, jnp.zeros_like(pair))


def hits(slots, dim):
    shape = (S, VIS) if dim == 0 else (VIS, S)
    return lax.broadcasted_iota(jnp.int32, shape, 1 - dim) == slots


def colsum(rows):
    return jnp.sum(rows, axis=0, keepdims=True)


def row(ref, index):
    return ref[index : index + 1, :]


class Pair:
    def __init__(self, refs):
        self.refs = refs

    def get(self, core):
        if len(self.refs) == 1:
            return self.refs[0][...]
        return jnp.where(core == 0, self.refs[1][...], self.refs[0][...])


def either(arrays, shape, index):
    if len(arrays) == 1:
        return [pl.BlockSpec(shape, lambda i, core: index(i))]
    zero = (0,) * len(shape)

    def on(wanted):
        def place(i, core):
            return tuple(
                jnp.where(core[0] == wanted, at, z) for at, z in zip(index(i), zero)
            )

        return place

    return [pl.BlockSpec(shape, on(1)), pl.BlockSpec(shape, on(0))]


def whole(shape):
    return pl.BlockSpec(shape, lambda i, core: (0,) * len(shape))


def struct(shape, dtype):
    return jax.ShapeDtypeStruct(shape, dtype)


def call(body, core, grid, ins, outs, scratch, name, flops):
    in_specs, args = [], []
    for specs, arrays in ins:
        in_specs += specs
        args += arrays
    out_specs = [spec for spec, _ in outs]
    out_shape = [shape for _, shape in outs]
    moved = sum(math.prod(a.shape) * a.dtype.itemsize for a in args)
    moved += sum(math.prod(a.shape) * a.dtype.itemsize for a in out_shape)
    return pl.pallas_call(
        body,
        grid_spec=pltpu.PrefetchScalarGridSpec(
            num_scalar_prefetch=1,
            grid=(grid,),
            in_specs=in_specs,
            out_specs=out_specs,
            scratch_shapes=scratch,
        ),
        out_shape=out_shape,
        compiler_params=pltpu.CompilerParams(
            vmem_limit_bytes=56 * 2**20, dimension_semantics=("arbitrary",)
        ),
        cost_estimate=pl.CostEstimate(flops=flops, bytes_accessed=moved, transcendentals=0),
        name=name,
    )(core, *args)


def attention_forward_body(n, decoder, core_ref, *refs):
    core = core_ref[0]
    refs = list(refs)
    take = lambda count: [refs.pop(0) for _ in range(count)]
    params_ref, slot_col, slot_row, img_col, img_row = take(5)
    sources = take(2 if decoder else 1)
    many = 2 if decoder else 1
    wq, wk, wv = Pair(take(many)), Pair(take(many)), Pair(take(many))
    x_ref, h_ref, qkv_ref, att_ref, lse_ref, bias_ref = refs
    j = pl.program_id(0)

    @pl.when(j == 0)
    def _():
        if decoder:
            sent_ref, pos_ref = sources
            slots = slot_col[0]
            hit = hits(slots, 0).astype(BF16)
            x = nn(hit, sent_ref[...]) + pos_ref[...]
            x = x + jnp.where(slots == VIS, row(params_ref, ENTRY), 0.0)
            x_ref[...] = x
            bias_ref[...] = jnp.where(img_col[0] == img_row[0], 0.0, -1e30)
        else:
            (patches_ref,) = sources
            cols, rows = [], []
            for micro in range(MICRO):
                hit = hits(slot_row[micro], 1)
                x_ref[micro * VIS : (micro + 1) * VIS, :] = nn(
                    hit.astype(BF16), patches_ref[micro]
                ) + row(params_ref, ENTRY)
                mark = img_row[micro] + 1
                cols.append(
                    jnp.sum(jnp.where(hit, mark, 0).astype(F32), axis=1, keepdims=True)
                    + 4.0 * micro
                )
                mark = img_col[micro] + 1
                rows.append(
                    jnp.sum(
                        jnp.where(hits(slot_col[micro], 0), mark, 0).astype(F32),
                        axis=0,
                        keepdims=True,
                    )
                    + 4.0 * micro
                )
            bias_ref[...] = jnp.where(
                jnp.concatenate(cols, axis=0) == jnp.concatenate(rows, axis=1), 0.0, -1e30
            )
        unit, _scale = unit_rows(x_ref[...])
        h_ref[...] = (unit * row(params_ref, GAIN1) + row(params_ref, SHIFT1)).astype(BF16)

    lanes = pl.ds(pl.multiple_of(j * TWO, TWO), TWO)
    h = h_ref[...]
    q = (nn(h, wq.get(core)) + params_ref[QBIAS : QBIAS + 1, lanes]).astype(BF16)
    k = nn(h, wk.get(core)).astype(BF16)
    v_wide = nn(h, wv.get(core)) + params_ref[VBIAS : VBIAS + 1, lanes]
    v = v_wide.astype(BF16)
    qkv_ref[0] = q
    qkv_ref[1] = k
    qkv_ref[2] = v
    v_across = v_wide.T.astype(BF16)
    bias = bias_ref[...]
    found = []
    for which in range(2):
        scaled = one_head(q, which) * jnp.asarray(HD**-0.5, BF16)
        scores = nt(k, scaled) + bias
        top = jnp.max(scores, axis=0, keepdims=True)
        raised = jnp.exp(scores - top)
        total = jnp.sum(raised, axis=0, keepdims=True)
        part = nn(v_across[which * HD : (which + 1) * HD, :], raised.astype(BF16))
        found.append(part * (1.0 / total))
        lse_ref[0, which : which + 1, :] = top + jnp.log(total)
    att_ref[...] = jnp.concatenate(found, axis=0).T.astype(BF16)


def attention_forward(core, n, decoder, params, marks, sources, w_qkv):
    slot_col, slot_row, img_col, img_row = marks
    m = slot_col.shape[0]
    ins = [
        ([whole((ROWS, D))], [params]),
        ([whole((m, S, 1))], [slot_col]),
        ([whole((m, 1, S))], [slot_row]),
        ([whole((m, S, 1))], [img_col]),
        ([whole((m, 1, S))], [img_row]),
    ]
    ins += [([whole(source.shape)], [source]) for source in sources]
    for part in range(3):
        ins.append(
            (either(w_qkv, (D, TWO), lambda j, part=part: (0, part * PAIRS + j)), list(w_qkv))
        )
    outs = [
        (whole((n, D)), struct((n, D), F32)),
        (whole((n, D)), struct((n, D), BF16)),
        (pl.BlockSpec((3, n, TWO), lambda j, core: (0, 0, j)), struct((3, n, D), BF16)),
        (pl.BlockSpec((n, TWO), lambda j, core: (0, j)), struct((n, D), BF16)),
        (pl.BlockSpec((1, 8, n), lambda j, core: (j, 0, 0)), struct((PAIRS, 8, n), F32)),
        (whole((n, n)), struct((n, n), F32)),
    ]
    return call(
        functools.partial(attention_forward_body, n, decoder),
        core,
        PAIRS,
        ins,
        outs,
        [],
        "attention_forward",
        2 * n * D * 3 * D + 4 * n * n * D,
    )


def feed_forward_body(many, core_ref, *refs):
    core = core_ref[0]
    refs = list(refs)
    take = lambda count: [refs.pop(0) for _ in range(count)]
    params_ref, x_ref, att_ref = take(3)
    w_out, w_up, w_down = Pair(take(many)), Pair(take(many)), Pair(take(many))
    mid_ref, h2_ref, act_ref, slope_ref, out_ref, sum_ref = refs
    t = pl.program_id(0)

    @pl.when(t == 0)
    def _():
        mid = x_ref[...] + nn(att_ref[...], w_out.get(core)) + row(params_ref, OBIAS)
        mid_ref[...] = mid
        unit, _scale = unit_rows(mid)
        h2_ref[...] = (unit * row(params_ref, GAIN2) + row(params_ref, SHIFT2)).astype(BF16)
        sum_ref[...] = mid + row(params_ref, DBIAS)

    pre = nn(h2_ref[...], w_up.get(core)) + params_ref[pl.ds(UBIAS + t, 1), :]
    below = 0.5 + 0.5 * lax.erf(pre * math.sqrt(0.5))
    act = (pre * below).astype(BF16)
    act_ref[...] = act
    density = jnp.exp(-0.5 * pre * pre) * (1.0 / math.sqrt(2.0 * math.pi))
    slope_ref[...] = (below + pre * density).astype(BF16)
    sum_ref[...] += nn(act, w_down.get(core))

    @pl.when(t == TILES - 1)
    def _():
        out_ref[...] = sum_ref[...].astype(BF16)


def feed_forward(core, n, params, x, att, w_out, w_up, w_down):
    ins = [
        ([whole((ROWS, D))], [params]),
        ([whole((n, D))], [x]),
        ([whole((n, D))], [att]),
        (either(w_out, (D, D), lambda t: (0, 0)), list(w_out)),
        (either(w_up, (D, D), lambda t: (0, t)), list(w_up)),
        (either(w_down, (D, D), lambda t: (t, 0)), list(w_down)),
    ]
    tile = pl.BlockSpec((n, D), lambda t, core: (0, t))
    outs = [
        (whole((n, D)), struct((n, D), F32)),
        (whole((n, D)), struct((n, D), BF16)),
        (tile, struct((n, FF), BF16)),
        (tile, struct((n, FF), BF16)),
        (whole((n, D)), struct((n, D), BF16)),
    ]
    return call(
        functools.partial(feed_forward_body, len(w_out)),
        core,
        TILES,
        ins,
        outs,
        [pltpu.VMEM((n, D), F32)],
        "feed_forward",
        2 * n * (D * D + 2 * D * FF),
    )


def halves(core, value):
    left, right = value[:, :HALF].astype(BF16), value[:, HALF:].astype(BF16)
    return jnp.where(core == 0, left, right), jnp.where(core == 0, right, left)


def feed_backward_body(many, core_ref, *refs):
    core = core_ref[0]
    refs = list(refs)
    take = lambda count: [refs.pop(0) for _ in range(count)]
    params_ref = take(1)[0]
    dy = Pair(take(many))
    act_ref, slope_ref, h2_ref, mid_ref, att_ref = take(5)
    w_out, w_up, w_down = Pair(take(many)), Pair(take(many)), Pair(take(many))
    up_keep, up_send, down_keep, down_send, dmid_ref, datt_ref, small_ref = take(7)
    dff_ref, h2_across, dh2_ref = refs
    t = pl.program_id(0)

    @pl.when(t == 0)
    def _():
        dff = dy.get(core)
        dff_ref[...] = dff
        h2_across[...] = h2_ref[...].T
        dh2_ref[...] = jnp.zeros_like(dh2_ref)
        small_ref[...] = jnp.zeros_like(small_ref)
        small_ref[DBIAS : DBIAS + 1, :] = colsum(dff.astype(F32))

    @pl.when(t < TILES)
    def _():
        dff = dff_ref[...]
        keep, send = halves(core, nn(act_ref[...].T, dff))
        per = D // down_keep.shape[0]
        down_keep[...] = keep.reshape(down_keep.shape)
        down_send[...] = send.reshape(down_send.shape)
        dpre_wide = nt(dff, w_down.get(core)) * slope_ref[...].astype(F32)
        dpre = dpre_wide.astype(BF16)
        small_ref[pl.ds(UBIAS + t, 1), :] = colsum(dpre.astype(F32))
        keep, send = halves(core, nn(h2_across[...], dpre))
        up_keep[...] = keep.reshape(up_keep.shape)
        up_send[...] = send.reshape(up_send.shape)
        dh2_ref[...] += nt(dpre, w_up.get(core))

    @pl.when(t == TILES)
    def _():
        dh2 = dh2_ref[...]
        unit, scale = unit_rows(mid_ref[...])
        small_ref[GAIN2 : GAIN2 + 1, :] = colsum(dh2 * unit)
        small_ref[SHIFT2 : SHIFT2 + 1, :] = colsum(dh2)
        dmid = dff_ref[...].astype(F32) + unit_rows_back(
            dh2, unit, scale, row(params_ref, GAIN2)
        )
        dmid_ref[...] = dmid
        dbranch = dmid.astype(BF16)
        small_ref[OBIAS : OBIAS + 1, :] = colsum(dbranch.astype(F32))
        keep, send = halves(core, nn(att_ref[...].T, dbranch))
        up_keep[...] = keep.reshape(up_keep.shape)
        up_send[...] = send.reshape(up_send.shape)
        datt_ref[...] = nt(dbranch, w_out.get(core)).astype(BF16)


def feed_backward(core, n, params, dy, act, slope, h2, mid, att, w_out, w_up, w_down):
    last = TILES - 1
    tile = pl.BlockSpec((n, D), lambda t, core: (0, jnp.minimum(t, last)))
    ins = [
        ([whole((ROWS, D))], [params]),
        (either(dy, (n, D), lambda t: (0, 0)), list(dy)),
        ([tile], [act]),
        ([tile], [slope]),
        ([whole((n, D))], [h2]),
        ([whole((n, D))], [mid]),
        ([whole((n, D))], [att]),
        (either(w_out, (D, D), lambda t: (0, 0)), list(w_out)),
        (either(w_up, (D, D), lambda t: (0, jnp.minimum(t, last))), list(w_up)),
        (either(w_down, (D, D), lambda t: (jnp.minimum(t, last), 0)), list(w_down)),
    ]
    up_spec = pl.BlockSpec((GROUPS, 1, GROUP_ROWS, HALF), lambda t, core: (0, t, 0, 0))
    up_shape = struct((GROUPS, TILES + 1, GROUP_ROWS, HALF), BF16)
    per = GROUPS // TILES
    down_spec = pl.BlockSpec(
        (per, D // per, HALF), lambda t, core: (jnp.minimum(t, last), 0, 0)
    )
    down_shape = struct((GROUPS, D // per, HALF), BF16)
    outs = [
        (up_spec, up_shape),
        (up_spec, up_shape),
        (down_spec, down_shape),
        (down_spec, down_shape),
        (whole((n, D)), struct((n, D), F32)),
        (whole((n, D)), struct((n, D), BF16)),
        (whole((ROWS, D)), struct((ROWS, D), F32)),
    ]
    return call(
        functools.partial(feed_backward_body, len(w_out)),
        core,
        TILES + 1,
        ins,
        outs,
        [pltpu.VMEM((n, D), BF16), pltpu.VMEM((D, n), BF16), pltpu.VMEM((n, D), F32)],
        "feed_backward",
        4 * n * (D * D + 2 * D * FF),
    )


def attention_backward_body(n, decoder, core_ref, *refs):
    core = core_ref[0]
    refs = list(refs)
    take = lambda count: [refs.pop(0) for _ in range(count)]
    many = 2 if decoder else 1
    params_ref, x_ref, h_ref, qkv_ref, att_ref, datt_ref, lse_ref, bias_ref = take(8)
    wq, wk, wv = Pair(take(many)), Pair(take(many)), Pair(take(many))
    dmid_ref, small_in, slot_col, slot_row = take(4)
    keep_ref, send_ref, small_ref, back_ref = take(4)
    h_across, dh_ref = refs
    j = pl.program_id(0)

    @pl.when(j == 0)
    def _():
        h_across[...] = h_ref[...].T
        dh_ref[...] = jnp.zeros_like(dh_ref)
        small_ref[...] = small_in[...]

    q, k, v = qkv_ref[0], qkv_ref[1], qkv_ref[2]
    datt = datt_ref[...]
    bias = bias_ref[...]
    along = (att_ref[...].astype(F32) * datt.astype(F32)).T
    k_across = k.T
    dq, dk, dv = [], 0.0, 0.0
    for which in range(2):
        scaled = one_head(q, which) * jnp.asarray(HD**-0.5, BF16)
        mine = one_head(datt, which)
        probs = jnp.exp(nt(k, scaled) + bias - lse_ref[0, which : which + 1, :])
        delta = colsum(along[which * HD : (which + 1) * HD, :])
        dscores = (probs * (nt(v, mine) - delta)).astype(BF16)
        dv = dv + nn(probs.astype(BF16), mine)
        dk = dk + nn(dscores, scaled)
        dq.append(nn(k_across[which * HD : (which + 1) * HD, :], dscores))
    dq = (jnp.concatenate(dq, axis=0) * HD**-0.5).T.astype(BF16)
    dk = dk.astype(BF16)
    dv = dv.astype(BF16)
    at = lax.rem(j + PAIRS // 2 * (1 - core), PAIRS)
    lanes = pl.ds(pl.multiple_of(at * TWO, TWO), TWO)
    small_ref[QBIAS : QBIAS + 1, lanes] = colsum(dq.astype(F32))
    small_ref[VBIAS : VBIAS + 1, lanes] = colsum(dv.astype(F32))
    across = h_across[...]
    grads = [nn(across, part).astype(BF16) for part in (dq, dk, dv)]

    @pl.when(j < PAIRS // 2)
    def _():
        for part in range(3):
            send_ref[:, part] = grads[part].reshape(GROUPS, GROUP_ROWS, TWO)

    @pl.when(j >= PAIRS // 2)
    def _():
        for part in range(3):
            keep_ref[:, part] = grads[part].reshape(GROUPS, GROUP_ROWS, TWO)

    dh_ref[...] += nt(dq, wq.get(core)) + nt(dk, wk.get(core)) + nt(dv, wv.get(core))

    @pl.when(j == PAIRS - 1)
    def _():
        dh = dh_ref[...]
        unit, scale = unit_rows(x_ref[...])
        small_ref[GAIN1 : GAIN1 + 1, :] = colsum(dh * unit)
        small_ref[SHIFT1 : SHIFT1 + 1, :] = colsum(dh)
        dx = dmid_ref[...] + unit_rows_back(dh, unit, scale, row(params_ref, GAIN1))
        low = dx.astype(BF16)
        if decoder:
            small_ref[ENTRY : ENTRY + 1, :] = colsum(jnp.where(slot_col[0] == VIS, dx, 0.0))
            back_ref[...] = nn(hits(slot_row[0], 1).astype(BF16), low).astype(BF16)
        else:
            small_ref[ENTRY : ENTRY + 1, :] = colsum(dx)
            for micro in range(MICRO):
                back_ref[micro] = nn(
                    hits(slot_col[micro], 0).astype(BF16),
                    low[micro * VIS : (micro + 1) * VIS, :],
                ).astype(BF16)


def attention_backward(
    core, n, decoder, params, x, h, qkv, att, datt, lse, bias, w_qkv, dmid, small, marks
):
    slot_col, slot_row = marks[:2]
    m = slot_col.shape[0]
    mid = PAIRS // 2

    def turn(j, core):
        return lax.rem(j + mid * (1 - core[0]), PAIRS)

    ins = [
        ([whole((ROWS, D))], [params]),
        ([whole((n, D))], [x]),
        ([whole((n, D))], [h]),
        ([pl.BlockSpec((3, n, TWO), lambda j, core: (0, 0, turn(j, core)))], [qkv]),
        ([pl.BlockSpec((n, TWO), lambda j, core: (0, turn(j, core)))], [att]),
        ([pl.BlockSpec((n, TWO), lambda j, core: (0, turn(j, core)))], [datt]),
        ([pl.BlockSpec((1, 8, n), lambda j, core: (turn(j, core), 0, 0))], [lse]),
        ([whole((n, n))], [bias]),
    ]
    for part in range(3):
        specs = []
        for wanted in (None,) if len(w_qkv) == 1 else (1, 0):

            def place(j, core, part=part, wanted=wanted):
                at = part * PAIRS + turn(j, core)
                return (0, at if wanted is None else jnp.where(core[0] == wanted, at, 0))

            specs.append(pl.BlockSpec((D, TWO), place))
        ins.append((specs, list(w_qkv)))
    ins += [
        ([whole((n, D))], [dmid]),
        ([whole((ROWS, D))], [small]),
        ([whole((m, S, 1))], [slot_col]),
        ([whole((m, 1, S))], [slot_row]),
    ]
    block = (GROUPS, 3, GROUP_ROWS, TWO)
    shape = struct((GROUPS, 3, GROUP_ROWS, HALF), BF16)
    back = (VIS, D) if decoder else (MICRO, S, D)
    outs = [
        (pl.BlockSpec(block, lambda j, core: (0, 0, 0, jnp.maximum(j - mid, 0))), shape),
        (pl.BlockSpec(block, lambda j, core: (0, 0, 0, jnp.minimum(j, mid - 1))), shape),
        (whole((ROWS, D)), struct((ROWS, D), F32)),
        (whole(back), struct(back, BF16)),
    ]
    return call(
        functools.partial(attention_backward_body, n, decoder),
        core,
        PAIRS,
        ins,
        outs,
        [pltpu.VMEM((D, n), BF16), pltpu.VMEM((n, D), F32)],
        "attention_backward",
        4 * n * D * 3 * D + 10 * n * n * D,
    )


def over_pipe(value, pairs):
    return lax.ppermute(value, "pipe", pairs)


SWAP = [(0, 1), (1, 0)]


def add(left, right, dtype):
    return (left.astype(F32) + right.astype(F32)).astype(dtype)


def exchange(piece, bits, bit, dtype=BF16):
    at = bits.index(bit)
    size = lax.axis_size("dp")
    mine = lax.rem(lax.axis_index("dp") // 2**bit, 2)
    send = lax.dynamic_index_in_dim(piece, 1 - mine, at, keepdims=False)
    keep = lax.dynamic_index_in_dim(piece, mine, at, keepdims=False)
    got = lax.ppermute(send, "dp", [(i, i ^ 2**bit) for i in range(size)])
    return add(keep, got, dtype), bits[:at] + bits[at + 1 :]


def by_device(piece):
    size = lax.axis_size("dp")
    more = size // GROUPS
    groups, slabs, rows, columns = piece.shape
    if more > 1:
        piece = piece.reshape(groups, slabs, more, rows // more, columns).transpose(0, 2, 1, 3, 4)
    count = size.bit_length() - 1
    return piece.reshape((2,) * count + (slabs * rows // more, columns)), list(
        range(count - 1, -1, -1)
    )


def scatter_sum(keep, send, first):
    piece = add(keep, over_pipe(send, SWAP), BF16)
    slabs = piece.shape[1]
    piece, bits = by_device(piece)
    order = first + [bit for bit in range(len(bits)) if bit not in first]
    for bit in order:
        piece, bits = exchange(piece, bits, bit, BF16 if len(bits) > 1 else F32)
    return piece.reshape(slabs, -1, HALF)


def everywhere(value):
    value = value + over_pipe(value, SWAP)
    size = lax.axis_size("dp")
    step = 1
    while step < size:
        value = value + lax.ppermute(value, "dp", [(i, i ^ step) for i in range(size)])
        step *= 2
    return value


def positions():
    width = D // 2
    frequency = np.exp(np.arange(width) * (-math.log(10000.0) / width))
    angles = np.arange(S)[:, None] * frequency[None, :]
    return jnp.asarray(np.concatenate([np.sin(angles), np.cos(angles)], axis=1), F32)


def on_device(
    section_input,
    visible_slot,
    image_of_slot,
    qkv_weight,
    out_weight,
    up_weight,
    down_weight,
    norm_gain,
    up_bias,
    vectors,
):
    pipe = lax.axis_index("pipe")
    first = pipe == 0
    core = pipe.astype(jnp.int32)[None]
    own = [qkv_weight[0], out_weight[0], up_weight[0], down_weight[0]]
    params = jnp.concatenate(
        [vectors[0], norm_gain[0], up_bias[0].reshape(TILES, D), jnp.zeros((3, D), F32)]
    )
    to_first, to_second = [(1, 0)], [(0, 1)]
    both = [[weight, over_pipe(weight, to_first)] for weight in own]
    dec_params = jnp.where(first, over_pipe(params, to_first), params)
    cotangent = [section_input[0, 1], over_pipe(section_input[0, 0], to_first)]

    def marks_of(slots, images):
        return (slots[:, :, None], slots[:, None, :], images[:, :, None], images[:, None, :])

    enc_marks = marks_of(visible_slot, image_of_slot)
    dec_marks = marks_of(
        lax.dynamic_index_in_dim(visible_slot, pipe, 0),
        lax.dynamic_index_in_dim(image_of_slot, pipe, 0),
    )
    rows = MICRO * VIS

    x, h, qkv, att, lse, bias = attention_forward(
        core, rows, False, params, enc_marks, [section_input[0]], [own[0]]
    )
    mid, h2, act, slope, out = feed_forward(core, rows, params, x, att, *[[w] for w in own[1:]])
    encoder = (x, h, qkv, att, lse, bias, mid, h2, act, slope)
    sent = jnp.where(first, out[:VIS], over_pipe(out[VIS:], to_second))

    def back(rows, decoder, params, dy, kept, weights, marks):
        x, h, qkv, att, lse, bias, mid, h2, act, slope = kept
        up_keep, up_send, down_keep, down_send, dmid, datt, small = feed_backward(
            core, rows, params, dy, act, slope, h2, mid, att, *weights[1:]
        )
        per = GROUPS // TILES
        down_shape = (GROUPS, 1, D // per, HALF)
        ups = scatter_sum(up_keep, up_send, [0, 1])
        downs = scatter_sum(down_keep.reshape(down_shape), down_send.reshape(down_shape), [1, 0])
        keep, send, small, returned = attention_backward(
            core, rows, decoder, params, x, h, qkv, att, datt, lse, bias, weights[0],
            dmid, small, marks,
        )
        heads = scatter_sum(keep, send, [0, 1])
        return returned, small, (ups, downs, heads)

    x, h, qkv, att, lse, bias = attention_forward(
        core, S, True, dec_params, dec_marks, [sent, positions()], both[0]
    )
    mid, h2, act, slope, out = feed_forward(core, S, dec_params, x, att, *both[1:])
    decoded = jnp.stack([over_pipe(out, to_second), out])
    kept = (x, h, qkv, att, lse, bias, mid, h2, act, slope)
    returned, dec_small, dec_grads = back(S, True, dec_params, cotangent, kept, both, dec_marks)

    other = over_pipe(returned, to_first)
    dy = jnp.where(first, jnp.concatenate([returned, other]), 0)
    returned, enc_small, enc_grads = back(
        rows, False, params, [dy], encoder, [[w] for w in own], enc_marks
    )
    results = jnp.where(first, returned, decoded)

    small = everywhere(jnp.stack([dec_small, enc_small]))
    small = jnp.where(first, small[1], small[0])
    joined = []
    for dec, enc in zip(dec_grads, enc_grads):
        got = over_pipe(jnp.where(first, dec, enc), SWAP)
        joined.append(
            jnp.concatenate(
                [jnp.where(first, enc, got), jnp.where(first, got, dec)], axis=-1
            )
        )
    ups, downs, heads = joined
    place = lax.axis_index("dp")
    width = D // lax.axis_size("dp")
    mine = lax.dynamic_slice_in_dim(small, place * width, width, 1)
    hidden = FF // lax.axis_size("dp")
    bias_grad = lax.dynamic_slice_in_dim(
        small[UBIAS : UBIAS + TILES].reshape(FF), place * hidden, hidden, 0
    )

    def wide(slabs):
        return slabs.transpose(1, 0, 2).reshape(slabs.shape[1], -1)

    return (
        results[None],
        wide(heads)[None],
        ups[TILES][None],
        wide(ups[:TILES])[None],
        downs.reshape(-1, D)[None],
        mine[GAIN1 : GAIN2 + 1][None],
        bias_grad[None],
        mine[:GAIN1][None],
    )


def solution(mesh):
    in_specs = (
        P("pipe", "dp", None, None),
        P("dp", None),
        P("dp", None),
        P("pipe", None, None),
        P("pipe", None, None),
        P("pipe", None, None),
        P("pipe", None, None),
        P("pipe", None, None),
        P("pipe", None),
        P("pipe", None, None),
    )
    out_specs = (
        P("pipe", "dp", None, None),
        P("pipe", "dp", None),
        P("pipe", "dp", None),
        P("pipe", "dp", None),
        P("pipe", "dp", None),
        P("pipe", None, "dp"),
        P("pipe", "dp"),
        P("pipe", None, "dp"),
    )
    return jax.shard_map(
        on_device, mesh=mesh, in_specs=in_specs, out_specs=out_specs, check_vma=False
    )
```

```python
import functools
import math

import jax
import jax.numpy as jnp
import numpy as np
from jax import lax
from jax.experimental import pallas as pl
from jax.experimental.pallas import tpu as pltpu
from jax.sharding import PartitionSpec as P

D = 768
H = 12
HD = 64
FF = 3072
S = 512
VIS = 128
MICRO = 2
EPSILON = 1e-06
PAIRS = H // 2
TWO = 2 * HD
TILES = FF // D
HALF = D // 2
GROUPS = 16
GROUP_ROWS = D // GROUPS
PER = GROUPS // TILES
DOWN_ROWS = FF // GROUPS
ROWS = 16
FAR = -1e30
F32 = jnp.float32
BF16 = jnp.bfloat16

SHIFT1, QBIAS, VBIAS, OBIAS, ENTRY, SHIFT2, DBIAS, GAIN1, GAIN2, UBIAS = range(10)


def contract(left, right, left_dim, right_dim):
    return lax.dot_general(
        left, right, (((left_dim,), (right_dim,)), ((), ())), preferred_element_type=F32
    )


def nn(left, right):
    return contract(left, right, 1, 0)


def nt(left, right):
    return contract(left, right, 1, 1)


def tn(left, right):
    return contract(left, right, 0, 0)


def unit_rows(rows):
    centered = rows - jnp.mean(rows, axis=-1, keepdims=True)
    scale = lax.rsqrt(jnp.mean(centered * centered, axis=-1, keepdims=True) + EPSILON)
    return centered * scale, scale


def unit_rows_back(grad, unit, scale, gain):
    scaled = grad * gain
    return scale * (
        scaled
        - jnp.mean(scaled, axis=-1, keepdims=True)
        - unit * jnp.mean(scaled * unit, axis=-1, keepdims=True)
    )


def in_head(shape, which):
    lane = lax.broadcasted_iota(jnp.int32, shape, 1)
    return lane < HD if which == 0 else lane >= HD


def one_head(pair, which):
    return jnp.where(in_head(pair.shape, which), pair, jnp.zeros_like(pair))


def colsum(rows):
    return jnp.sum(rows, axis=0, keepdims=True)


class Params:
    def __init__(self, core, own, other=None):
        self.core, self.own, self.other = core, own, other

    def __call__(self, index):
        if index >= UBIAS:
            at = (2, slice(0, 1), slice((index - UBIAS) * D, (index - UBIAS + 1) * D))
        elif index >= GAIN1:
            at = (1, 0, slice(index - GAIN1, index - GAIN1 + 1))
        else:
            at = (0, 0, slice(index, index + 1))
        return self.pick(at)

    def hidden(self, t):
        return self.pick((2, slice(0, 1), pl.ds(pl.multiple_of(t * D, D), D)))

    def pick(self, at):
        value = self.own[at[0]][at[1:]]
        if self.other is None:
            return value
        return jnp.where(self.core == 0, self.other[at[0]][at[1:]], value)


def upright(line):
    return jnp.broadcast_to(line, (8, line.shape[1])).T[:, :1]


def hits(slots):
    return lax.broadcasted_iota(jnp.int32, (VIS, S), 0).astype(F32) == slots


def hits_upright(slots):
    return lax.broadcasted_iota(jnp.int32, (S, VIS), 1).astype(F32) == slots


def marks(groups, count):
    lane = lax.broadcasted_iota(jnp.int32, (groups.shape[0], TWO), 1)
    lane = jnp.where(lane < HD, lane, lane - HD).astype(F32)
    same = lane == groups
    key_fill = jnp.where(same, 1.0, 0.0).astype(BF16)
    query_fill = jnp.where(jnp.logical_or(same, lane >= count), 0.0, FAR).astype(BF16)
    return key_fill, query_fill


class Weight:
    def __init__(self, core, refs, dst, sems, cuts):
        self.core, self.refs, self.dst, self.sems, self.cuts = core, refs, dst, sems, cuts

    def start(self, i):
        cut = self.cuts[i]

        def go(ref):
            pltpu.make_async_copy(ref.at[cut], self.dst.at[cut], self.sems.at[i]).start()

        if len(self.refs) == 1:
            go(self.refs[0])
        else:
            pl.when(self.core == 0)(lambda: go(self.refs[1]))
            pl.when(self.core != 0)(lambda: go(self.refs[0]))

    def get(self, i):
        cut = self.cuts[i]
        pltpu.make_async_copy(self.refs[0].at[cut], self.dst.at[cut], self.sems.at[i]).wait()
        return self.dst[cut]


    def take(self, i, cut):
        pltpu.make_async_copy(self.refs[0].at[cut], self.dst.at[cut], self.sems.at[i]).wait()
        return self.dst[cut]


class Out:
    def __init__(self, sems):
        self.sems, self.count, self.going = sems, 0, []

    def send(self, src, dst):
        copy = pltpu.make_async_copy(src, dst, self.sems.at[self.count])
        self.count += 1
        copy.start()
        self.going.append(copy)

    def wait(self):
        for copy in self.going:
            copy.wait()


SMEM, VMEM, HBM = pltpu.SMEM, pltpu.VMEM, pl.ANY


def struct(shape, dtype):
    return jax.ShapeDtypeStruct(shape, dtype)


def size_of(shape):
    return math.prod(shape.shape) * shape.dtype.itemsize


def call(body, ins, outs, scratch, name, flops):
    arrays = [array for array, _ in ins]
    shapes = [shape for shape, _ in outs]
    return pl.pallas_call(
        body,
        in_specs=[pl.BlockSpec(memory_space=space) for _, space in ins],
        out_specs=[pl.BlockSpec(memory_space=space) for _, space in outs],
        out_shape=shapes,
        scratch_shapes=scratch,
        compiler_params=pltpu.CompilerParams(vmem_limit_bytes=60 * 2**20),
        cost_estimate=pl.CostEstimate(
            flops=flops, bytes_accessed=sum(map(size_of, arrays + shapes)), transcendentals=0
        ),
        name=name,
    )(*arrays)


def taker(refs):
    refs = list(refs)

    def take(count):
        return [refs.pop(0) for _ in range(count)]

    return take


def columns(i):
    return (slice(None), slice(i * D, (i + 1) * D))


def positions():
    width = D // 2
    frequency = np.exp(np.arange(width) * (-math.log(10000.0) / width))
    angles = np.arange(S)[:, None] * frequency[None, :]
    return jnp.asarray(np.concatenate([np.sin(angles), np.cos(angles)], axis=1), F32)


def rows_of(i):
    return (slice(i * D, (i + 1) * D), slice(None))


def group_columns(core, decoder, slots_ref, images_ref):
    if decoder:
        return upright(images_ref[pl.ds(core, 1), :].astype(F32)), 2
    parts = []
    for micro in range(MICRO):
        hit = hits(slots_ref[micro : micro + 1, :].astype(F32))
        mark = images_ref[micro : micro + 1, :].astype(F32) + 1.0
        parts.append(jnp.sum(jnp.where(hit, mark, 0.0), axis=1, keepdims=True) + 3.0 * micro)
    return jnp.concatenate(parts, axis=0), 3 * MICRO


def project(params, weight, x_s, h_s, qkv_s, out, h_out, qkv_out):
    unit, _scale = unit_rows(x_s[...])
    h = (unit * params(GAIN1) + params(SHIFT1)).astype(BF16)
    h_s[...] = h
    out.send(h_s, h_out)
    for part, bias in enumerate((QBIAS, None, VBIAS)):
        made = nn(h, weight.get(part))
        if bias is not None:
            made = made + params(bias)
        qkv_s[part] = made.astype(BF16)
        out.send(qkv_s.at[part], qkv_out.at[part])


def attend(n, together, fills, qkv_s, att_s, lse_ref):
    key_fill, query_fill = fills
    scaling = jnp.asarray(HD**-0.5, BF16)

    def pairs(step, _):
        lanes = [
            pl.ds(pl.multiple_of((step * together + i) * TWO, TWO), TWO) for i in range(together)
        ]
        heads = [(i, which) for i in range(together) for which in range(2)]
        qs = [qkv_s[0, :, at] * scaling for at in lanes]
        ks = [qkv_s[1, :, at] for at in lanes]
        vs = [qkv_s[2, :, at].T for at in lanes]
        scores = [
            nt(
                jnp.where(in_head((n, TWO), which), ks[i], key_fill),
                jnp.where(in_head((n, TWO), which), qs[i], query_fill),
            )
            for i, which in heads
        ]
        tops = [jnp.max(score, axis=0, keepdims=True) for score in scores]
        raised = [jnp.exp(score - top) for score, top in zip(scores, tops)]
        totals = [colsum(part) for part in raised]
        found = [
            nn(vs[i][which * HD : (which + 1) * HD, :], part.astype(BF16)) * (1.0 / total)
            for (i, which), part, total in zip(heads, raised, totals)
        ]
        for i in range(together):
            att_s[lanes[i], :] = jnp.concatenate(found[2 * i : 2 * i + 2], axis=0).astype(BF16)
            lse_ref[step * together + i] = jnp.concatenate(
                [tops[at] + jnp.log(totals[at]) for at in (2 * i, 2 * i + 1)], axis=0
            )
        return 0

    lax.fori_loop(0, PAIRS // together, pairs, 0)


def feed(params, weights, x_s, att_s, mid_s, h2_s, act_s, slope_s, sum_s, out, h2_out, act_out):
    out_weight, up, down = weights
    mid = x_s[...] + tn(att_s[...], out_weight.get(0)) + params(OBIAS)
    mid_s[...] = mid
    unit, _scale = unit_rows(mid)
    h2 = (unit * params(GAIN2) + params(SHIFT2)).astype(BF16)
    h2_s[...] = h2
    out.send(h2_s, h2_out)
    sum_s[...] = mid + params(DBIAS)

    def tile(t, _):
        at = (slice(None), pl.ds(pl.multiple_of(t * D, D), D))
        pre = nn(h2_s[...], up.take(t, at)) + params.hidden(t)
        below = 0.5 + 0.5 * lax.erf(pre * math.sqrt(0.5))
        act = (pre * below).astype(BF16)
        act_s[at] = act
        density = jnp.exp(-0.5 * pre * pre) * (1.0 / math.sqrt(2.0 * math.pi))
        slope_s[at] = (below + pre * density).astype(BF16)
        sum_s[...] += nn(act, down.take(t, (at[1], slice(None))))
        return 0

    lax.fori_loop(0, TILES, tile, 0)
    out.send(act_s, act_out)


def feed_back(
    params, weights, dff, dff_ref, slope, mid, dpre_s, dh2_s, small_ref, out, dpre_out
):
    out_weight, up, down = weights
    small_ref[...] = jnp.zeros_like(small_ref)
    small_ref[DBIAS : DBIAS + 1, :] = colsum(dff.astype(F32))
    if dff_ref is not None:
        dff_ref[...] = dff
    dh2_s[...] = jnp.zeros_like(dh2_s)

    def tile(t, _):
        at = (slice(None), pl.ds(pl.multiple_of(t * D, D), D))
        dact = nt(dff_ref[...], down(t, (at[1], slice(None))))
        dpre = (dact * slope(t, at).astype(F32)).astype(BF16)
        dpre_s[at] = dpre
        small_ref[pl.ds(UBIAS + t, 1), :] = colsum(dpre.astype(F32))
        dh2_s[...] += nt(dpre, up(t, at))
        return 0

    lax.fori_loop(0, TILES, tile, 0)
    out.send(dpre_s, dpre_out)
    dh2 = dh2_s[...]
    unit, scale = unit_rows(mid())
    small_ref[GAIN2 : GAIN2 + 1, :] = colsum(dh2 * unit)
    small_ref[SHIFT2 : SHIFT2 + 1, :] = colsum(dh2)
    dmid = dff.astype(F32) + unit_rows_back(dh2, unit, scale, params(GAIN2))
    dbranch = dmid.astype(BF16)
    small_ref[OBIAS : OBIAS + 1, :] = colsum(dbranch.astype(F32))
    return dmid, dbranch, nt(dbranch, out_weight()).astype(BF16)


def attend_back(n, together, fills, qkv_ref, att_ref, datt_ref, lse_ref, dqkv_ref):
    key_fill, query_fill = fills
    scaling = jnp.asarray(HD**-0.5, BF16)

    def pairs(step, _):
        lanes = [
            pl.ds(pl.multiple_of((step * together + i) * TWO, TWO), TWO) for i in range(together)
        ]
        heads = [(i, which) for i in range(together) for which in range(2)]
        qs = [qkv_ref[0, :, at] * scaling for at in lanes]
        ks = [qkv_ref[1, :, at] for at in lanes]
        vs = [qkv_ref[2, :, at] for at in lanes]
        turned = [k.T for k in ks]
        dos = [datt_ref[:, at] for at in lanes]
        mine = [one_head(dos[i], which) for i, which in heads]
        along = [
            att_ref[at, :].astype(F32) * do.T.astype(F32) for at, do in zip(lanes, dos)
        ]
        scores = [
            nt(
                jnp.where(in_head((n, TWO), which), ks[i], key_fill),
                jnp.where(in_head((n, TWO), which), qs[i], query_fill),
            )
            for i, which in heads
        ]
        dprobs = [nt(vs[i], do) for (i, which), do in zip(heads, mine)]
        probs = [
            jnp.exp(score - lse_ref[step * together + i, which : which + 1, :])
            for (i, which), score in zip(heads, scores)
        ]
        dscores = [
            (prob * (dprob - colsum(along[i][which * HD : (which + 1) * HD, :]))).astype(BF16)
            for (i, which), prob, dprob in zip(heads, probs, dprobs)
        ]
        for i in range(together):
            a, b = 2 * i, 2 * i + 1
            dv = nn(probs[a].astype(BF16), mine[a]) + nn(probs[b].astype(BF16), mine[b])
            dk = nn(dscores[a], one_head(qs[i], 0)) + nn(dscores[b], one_head(qs[i], 1))
            dq = jnp.concatenate(
                [nn(turned[i][:HD, :], dscores[a]), nn(turned[i][HD:, :], dscores[b])], axis=0
            )
            dqkv_ref[0, :, lanes[i]] = (dq * HD**-0.5).T.astype(BF16)
            dqkv_ref[1, :, lanes[i]] = dk.astype(BF16)
            dqkv_ref[2, :, lanes[i]] = dv.astype(BF16)
        return 0

    lax.fori_loop(0, PAIRS // together, pairs, 0)


def project_back(params, weight, dqkv_ref, x, dmid, small_ref):
    dh = 0.0
    for part in range(3):
        made = dqkv_ref[part]
        if part != 1:
            bias = QBIAS if part == 0 else VBIAS
            small_ref[bias : bias + 1, :] = colsum(made.astype(F32))
        dh = dh + nt(made, weight.get(part))
    unit, scale = unit_rows(x())
    small_ref[GAIN1 : GAIN1 + 1, :] = colsum(dh * unit)
    small_ref[SHIFT1 : SHIFT1 + 1, :] = colsum(dh)
    return dmid() + unit_rows_back(dh, unit, scale, params(GAIN1))


EVERYTHING = (slice(None), slice(None))


def qkv_loads(core, refs, dst, sems):
    return Weight(core, refs, dst, sems, [columns(part) for part in range(3)])


def feed_loads(core, w_out, w_up, w_down, dsts, sems):
    return (
        Weight(core, w_out, dsts[0], sems[0], [EVERYTHING]),
        Weight(core, w_up, dsts[1], sems[1], [columns(t) for t in range(TILES)]),
        Weight(core, w_down, dsts[2], sems[2], [rows_of(t) for t in range(TILES)]),
    )


def dma(count):
    return pltpu.SemaphoreType.DMA((count,))


FEED_SCRATCH = [VMEM((D, D), BF16), VMEM((D, FF), BF16), VMEM((FF, D), BF16)]
FEED_SEMS = [dma(1), dma(TILES), dma(TILES)]
QKV_SCRATCH = [VMEM((D, 3 * D), BF16), dma(3)]


def encoder_forward_body(n, *refs):
    take = taker(refs)
    (core_ref,) = take(1)
    params = Params(core_ref[0], take(3))
    slots_ref, images_ref, patches_ref = take(3)
    w_qkv, w_out, w_up, w_down = take(1), take(1), take(1), take(1)
    x_out, h_out, qkv_out, att_out, lse_ref, mid_out, h2_out, act_out = take(8)
    slope_out, out_ref = take(2)
    x_s, h_s, qkv_s, att_s, mid_s, h2_s, act_s, slope_s, sum_s = take(9)
    wq_s, wq_sems = take(2)
    dsts, sems = take(3), take(3)
    (out_sems,) = take(1)
    core = core_ref[0]

    @pl.when(core == 0)
    def _():
        weight = qkv_loads(core, w_qkv, wq_s, wq_sems)
        weights = feed_loads(core, w_out, w_up, w_down, dsts, sems)
        for part in range(3):
            weight.start(part)
        weights[0].start(0)
        for t in range(TILES):
            weights[1].start(t)
            weights[2].start(t)
        out = Out(out_sems)
        for micro in range(MICRO):
            hit = hits(slots_ref[micro : micro + 1, :].astype(F32))
            x_s[micro * VIS : (micro + 1) * VIS, :] = nn(
                hit.astype(BF16), patches_ref[0, micro]
            ) + params(ENTRY)
        out.send(x_s, x_out)
        project(params, weight, x_s, h_s, qkv_s, out, h_out, qkv_out)
        fills = marks(*group_columns(core, False, slots_ref, images_ref))
        attend(n, 3, fills, qkv_s, att_s, lse_ref)
        out.send(att_s, att_out)
        feed(
            params, weights, x_s, att_s, mid_s, h2_s, act_s, slope_s, sum_s, out, h2_out, act_out
        )
        out.send(mid_s, mid_out)
        out.send(slope_s, slope_out)
        out_ref[...] = sum_s[...].astype(BF16)
        out.wait()


def encoder_forward(core, n, params, layout, section, weights):
    ins = [(core, SMEM)] + [(a, VMEM) for a in (*params, *layout, section)]
    ins += [(w, HBM) for w in weights]
    outs = [
        (struct((n, D), F32), HBM),
        (struct((n, D), BF16), HBM),
        (struct((3, n, D), BF16), HBM),
        (struct((D, n), BF16), HBM),
        (struct((PAIRS, 2, n), F32), VMEM),
        (struct((n, D), F32), HBM),
        (struct((n, D), BF16), HBM),
        (struct((n, FF), BF16), HBM),
        (struct((n, FF), BF16), HBM),
        (struct((n, D), BF16), VMEM),
    ]
    scratch = [
        VMEM((n, D), F32),
        VMEM((n, D), BF16),
        VMEM((3, n, D), BF16),
        VMEM((D, n), BF16),
        VMEM((n, D), F32),
        VMEM((n, D), BF16),
        VMEM((n, FF), BF16),
        VMEM((n, FF), BF16),
        VMEM((n, D), F32),
        *QKV_SCRATCH,
        *FEED_SCRATCH,
        *FEED_SEMS,
        dma(10),
    ]
    return call(
        functools.partial(encoder_forward_body, n),
        ins,
        outs,
        scratch,
        "encoder_forward",
        2 * n * (4 * D * D + 2 * D * FF),
    )


def decoder_body(n, *refs):
    take = taker(refs)
    (core_ref,) = take(1)
    core = core_ref[0]
    params = Params(core, take(3), take(3))
    slots_ref, images_ref, pos_ref, sent_ref, other_sent_ref, dff_ref, other_dff_ref = take(7)
    w_qkv, w_out, w_up, w_down = take(2), take(2), take(2), take(2)
    x_out, h_out, qkv_out, att_out, lse_ref, h2_out, act_out, out_ref = take(8)
    dpre_out, dbranch_ref, dmid_ref, datt_ref, small_ref = take(5)
    x_s, h_s, qkv_s, att_s, mid_s, h2_s, act_s, slope_s, sum_s, dpre_s, dff_s = take(11)
    wq_s, wq_sems = take(2)
    dsts, sems = take(3), take(3)
    out_sems, dff_sem = take(2)
    weight = qkv_loads(core, w_qkv, wq_s, wq_sems)
    weights = feed_loads(core, w_out, w_up, w_down, dsts, sems)
    for part in range(3):
        weight.start(part)
    weights[0].start(0)
    for t in range(TILES):
        weights[1].start(t)
        weights[2].start(t)
    dff = Weight(core, [dff_ref.at[0, 1], other_dff_ref], dff_s, dff_sem, [EVERYTHING])
    dff.start(0)
    out = Out(out_sems)
    slots = upright(slots_ref[pl.ds(core, 1), :].astype(F32))
    sent = jnp.where(core == 0, sent_ref[:VIS, :], other_sent_ref[VIS:, :])
    x = nn(hits_upright(slots).astype(BF16), sent) + pos_ref[...]
    x_s[...] = x + jnp.where(slots == VIS, params(ENTRY), 0.0)
    out.send(x_s, x_out)
    project(params, weight, x_s, h_s, qkv_s, out, h_out, qkv_out)
    fills = marks(*group_columns(core, True, slots_ref, images_ref))
    attend(n, 2, fills, qkv_s, att_s, lse_ref)
    out.send(att_s, att_out)
    feed(params, weights, x_s, att_s, mid_s, h2_s, act_s, slope_s, sum_s, out, h2_out, act_out)
    out_ref[...] = sum_s[...].astype(BF16)
    dmid_ref[...], dbranch_ref[...], datt_ref[...] = feed_back(
        params,
        (
            lambda: weights[0].dst[...],
            lambda t, at: weights[1].dst[at],
            lambda t, at: weights[2].dst[at],
        ),
        dff.get(0),
        dff_s,
        lambda t, at: slope_s[at],
        lambda: mid_s[...],
        dpre_s,
        sum_s,
        small_ref,
        out,
        dpre_out,
    )
    out.wait()


def decoder(core, n, params, other_params, layout, sent, other_sent, section, other_dff, weights):
    ins = [(core, SMEM)] + [(a, VMEM) for a in (*params, *other_params, *layout, positions())]
    ins += [(sent, VMEM), (other_sent, VMEM), (section, HBM), (other_dff, HBM)]
    ins += [(w, HBM) for pair in weights for w in pair]
    outs = [
        (struct((n, D), F32), HBM),
        (struct((n, D), BF16), HBM),
        (struct((3, n, D), BF16), HBM),
        (struct((D, n), BF16), HBM),
        (struct((PAIRS, 2, n), F32), VMEM),
        (struct((n, D), BF16), HBM),
        (struct((n, FF), BF16), HBM),
        (struct((n, D), BF16), VMEM),
        (struct((n, FF), BF16), HBM),
        (struct((n, D), BF16), VMEM),
        (struct((n, D), F32), VMEM),
        (struct((n, D), BF16), VMEM),
        (struct((ROWS, D), F32), VMEM),
    ]
    scratch = [
        VMEM((n, D), F32),
        VMEM((n, D), BF16),
        VMEM((3, n, D), BF16),
        VMEM((D, n), BF16),
        VMEM((n, D), F32),
        VMEM((n, D), BF16),
        VMEM((n, FF), BF16),
        VMEM((n, FF), BF16),
        VMEM((n, D), F32),
        VMEM((n, FF), BF16),
        VMEM((n, D), BF16),
        *QKV_SCRATCH,
        *FEED_SCRATCH,
        *FEED_SEMS,
        dma(9),
        dma(1),
    ]
    return call(
        functools.partial(decoder_body, n),
        ins,
        outs,
        scratch,
        "decoder",
        2 * n * (5 * D * D + 4 * D * FF) + 4 * n * n * D,
    )


def decoder_back_body(n, *refs):
    take = taker(refs)
    (core_ref,) = take(1)
    core = core_ref[0]
    params = Params(core, take(3), take(3))
    slots_ref, images_ref, qkv_ref, att_ref, datt_ref, lse_ref, small_in = take(7)
    x_in, dmid_in = take(2)
    w_qkv = take(2)
    dqkv_ref, small_ref, back_ref = take(3)
    x_s, dmid_s, wq_s, wq_sems, in_sems = take(5)
    weight = qkv_loads(core, w_qkv, wq_s, wq_sems)
    x = Weight(core, [x_in], x_s, in_sems, [EVERYTHING])
    dmid = Weight(core, [dmid_in], dmid_s, in_sems.at[pl.ds(1, 1)], [EVERYTHING])
    for part in range(3):
        weight.start(part)
    x.start(0)
    dmid.start(0)
    fills = marks(*group_columns(core, True, slots_ref, images_ref))
    attend_back(n, 1, fills, qkv_ref, att_ref, datt_ref, lse_ref, dqkv_ref)
    small_ref[...] = small_in[...]
    dx = project_back(
        params, weight, dqkv_ref, lambda: x.get(0), lambda: dmid.get(0), small_ref
    )
    slots = slots_ref[pl.ds(core, 1), :].astype(F32)
    small_ref[ENTRY : ENTRY + 1, :] = colsum(jnp.where(upright(slots) == VIS, dx, 0.0))
    back_ref[...] = nn(hits(slots).astype(BF16), dx.astype(BF16)).astype(BF16)


def decoder_back(
    core, n, params, other_params, layout, qkv, att, datt, lse, small, x, dmid, w_qkv
):
    ins = [(core, SMEM)] + [(a, VMEM) for a in (*params, *other_params, *layout)]
    ins += [(a, VMEM) for a in (qkv, att, datt, lse, small)] + [(x, HBM), (dmid, HBM)]
    ins += [(w, HBM) for w in w_qkv]
    outs = [
        (struct((3, n, D), BF16), VMEM),
        (struct((ROWS, D), F32), VMEM),
        (struct((VIS, D), BF16), VMEM),
    ]
    scratch = [VMEM((n, D), F32), VMEM((n, D), F32), *QKV_SCRATCH, dma(2)]
    return call(
        functools.partial(decoder_back_body, n),
        ins,
        outs,
        scratch,
        "decoder_back",
        2 * n * D * 3 * D + 10 * n * n * D,
    )


def encoder_back_body(n, *refs):
    take = taker(refs)
    (core_ref,) = take(1)
    core = core_ref[0]
    params = Params(core, take(3))
    slots_ref, images_ref, dy_ref, other_dy_ref, att_ref, lse_ref = take(6)
    slope_in, mid_in, qkv_in, x_in, decoded_in, other_decoded_in = take(6)
    w_qkv, w_out, w_up, w_down = take(1), take(1), take(1), take(1)
    dpre_out, dbranch_out, dqkv_out, small_ref, results_out = take(5)
    slope_s, mid_s, qkv_s, x_s, dpre_s, dh2_s, dbranch_s, datt_s, dqkv_s, back_s = take(10)
    wq_s, wq_sems = take(2)
    dsts, sems = take(3), take(3)
    in_sems, out_sems = take(2)

    @pl.when(core != 0)
    def _():
        parts = [
            Weight(core, [ref], back_s.at[at], in_sems.at[pl.ds(at, 1)], [EVERYTHING])
            for at, ref in enumerate((other_decoded_in, decoded_in))
        ]
        out = Out(out_sems)
        for part in parts:
            part.start(0)
        for at, part in enumerate(parts):
            part.get(0)
            out.send(back_s.at[at], results_out.at[at])
        out.wait()

    @pl.when(core == 0)
    def _():
        weight = qkv_loads(core, w_qkv, wq_s, wq_sems)
        weights = feed_loads(core, w_out, w_up, w_down, dsts, sems)
        out_weight, up, down = weights
        slope = Weight(core, [slope_in], slope_s, in_sems, [columns(t) for t in range(TILES)])
        mid = Weight(core, [mid_in], mid_s, in_sems.at[pl.ds(TILES, 1)], [EVERYTHING])
        qkv = Weight(
            core, [qkv_in], qkv_s, in_sems.at[pl.ds(TILES + 1, 1)], [(slice(None),) * 3]
        )
        x = Weight(core, [x_in], x_s, in_sems.at[pl.ds(TILES + 2, 1)], [EVERYTHING])
        for t in range(TILES):
            down.start(t)
            slope.start(t)
            up.start(t)
        mid.start(0)
        out_weight.start(0)
        qkv.start(0)
        for part in range(3):
            weight.start(part)
        x.start(0)
        out = Out(out_sems)
        dff = jnp.concatenate([dy_ref[...], other_dy_ref[...]], axis=0)
        dmid, dbranch, datt = feed_back(
            params, (lambda: out_weight.get(0), up.take, down.take), dff, dbranch_s, slope.take,
            lambda: mid.get(0), dpre_s, dh2_s, small_ref, out, dpre_out,
        )
        dh2_s[...] = dmid
        dbranch_s[...] = dbranch
        out.send(dbranch_s, dbranch_out)
        datt_s[...] = datt
        fills = marks(*group_columns(core, False, slots_ref, images_ref))
        qkv.get(0)
        attend_back(n, 2, fills, qkv_s, att_ref, datt_s, lse_ref, dqkv_s)
        out.send(dqkv_s, dqkv_out)
        dx = project_back(params, weight, dqkv_s, lambda: x.get(0), lambda: dh2_s[...], small_ref)
        low = dx.astype(BF16)
        small_ref[ENTRY : ENTRY + 1, :] = colsum(dx)
        for micro in range(MICRO):
            slots = upright(slots_ref[micro : micro + 1, :].astype(F32))
            back_s[micro] = nn(
                hits_upright(slots).astype(BF16), low[micro * VIS : (micro + 1) * VIS, :]
            ).astype(BF16)
        out.send(back_s, results_out)
        out.wait()


def encoder_back(
    core, n, params, layout, dy, other_dy, att, lse, slope, mid, qkv, x, decoded, other_decoded,
    weights,
):
    ins = [(core, SMEM)] + [(a, VMEM) for a in (*params, *layout, dy, other_dy, att, lse)]
    ins += [(a, HBM) for a in (slope, mid, qkv, x, decoded, other_decoded, *weights)]
    outs = [
        (struct((n, FF), BF16), HBM),
        (struct((n, D), BF16), HBM),
        (struct((3, n, D), BF16), HBM),
        (struct((ROWS, D), F32), VMEM),
        (struct((MICRO, S, D), BF16), HBM),
    ]
    scratch = [
        VMEM((n, FF), BF16),
        VMEM((n, D), F32),
        VMEM((3, n, D), BF16),
        VMEM((n, D), F32),
        VMEM((n, FF), BF16),
        VMEM((n, D), F32),
        VMEM((n, D), BF16),
        VMEM((n, D), BF16),
        VMEM((3, n, D), BF16),
        VMEM((MICRO, S, D), BF16),
        *QKV_SCRATCH,
        *FEED_SCRATCH,
        *FEED_SEMS,
        dma(TILES + 3),
        dma(4),
    ]
    return call(
        functools.partial(encoder_back_body, n),
        ins,
        outs,
        scratch,
        "encoder_back",
        2 * n * (4 * D * D + 2 * D * FF),
    )


def put(core_ref, bit, made, out_refs, at=slice(None)):
    if bit is None:
        out_refs[0][:, at, :] = made
        return
    groups, rows, width = made.shape
    made = made.reshape(groups // 2 ** (bit + 1), 2, 2**bit, rows, width)
    mine = core_ref[1 + bit]
    low, high = made[:, 0], made[:, 1]
    for out_ref, other in zip(out_refs, (True, False)):
        chosen = jnp.where((mine == 0) != other, low, high)
        out_ref[:, at, :] = chosen.reshape(groups // 2, rows, width)


def grad_call(body, core, dec, enc, out, bit, name):
    def only(wanted, index):
        def place(i, core):
            return tuple(jnp.where(core[0] == wanted, at, 0) for at in index(i))

        return place

    specs = [pl.BlockSpec(block, only(1, index)) for _, block, index in dec]
    specs += [pl.BlockSpec(block, only(0, index)) for _, block, index in enc]
    arrays = [a for a, _, _ in (*dec, *enc)]
    rows, block, index = out
    parts = 1 if bit is None else 2
    out_spec = pl.BlockSpec((block[0] // parts, *block[1:]), lambda i, core: index(i))
    return pl.pallas_call(
        functools.partial(body, bit),
        grid_spec=pltpu.PrefetchScalarGridSpec(
            num_scalar_prefetch=1, grid=(TILES,), in_specs=specs, out_specs=[out_spec] * parts
        ),
        out_shape=[struct((GROUPS // parts, rows, D), BF16)] * parts,
        compiler_params=pltpu.CompilerParams(
            vmem_limit_bytes=60 * 2**20, dimension_semantics=("arbitrary",)
        ),
        cost_estimate=pl.CostEstimate(
            flops=4 * S * FF * D, bytes_accessed=sum(map(size_of, arrays)), transcendentals=0
        ),
        name=name,
    )(core, *arrays)


def down_grad_body(bit, core_ref, a0, a1, b0, b1, c, d0, d1, *out_refs):
    def give(made):
        put(core_ref, bit, made.astype(BF16).reshape(PER, DOWN_ROWS, D), out_refs)

    @pl.when(core_ref[0] != 0)
    def _():
        give(tn(a0[...], b0[0]) + tn(a1[...], b1[0]))

    @pl.when(core_ref[0] == 0)
    def _():
        give(tn(c[...], jnp.concatenate([d0[...], d1[...]], axis=0)))


def down_grad(core, bit, acts, section, enc_act, dys):
    tile = lambda i: (0, i)
    zero = lambda i: (0, 0)
    dec = [(a, (a.shape[0], D), tile) for a in acts]
    dec += [(section, (1, S, D), lambda i, m=m: (m, 0, 0)) for m in (1, 0)]
    enc = [(enc_act, (enc_act.shape[0], D), tile)] + [(dy, dy.shape, zero) for dy in dys]
    return grad_call(
        down_grad_body, core, dec, enc,
        (DOWN_ROWS, (PER, DOWN_ROWS, D), lambda i: (i, 0, 0)), bit, "down_grad",
    )


def up_grad_body(bit, core_ref, a0, a1, b0, b1, c, d, *out_refs):
    def give(made):
        put(core_ref, bit, made.astype(BF16).reshape(GROUPS, GROUP_ROWS, D), out_refs)

    @pl.when(core_ref[0] != 0)
    def _():
        give(tn(a0[...], b0[...]) + tn(a1[...], b1[...]))

    @pl.when(core_ref[0] == 0)
    def _():
        give(tn(c[...], d[...]))


def up_grad(core, bit, h2s, dpres, enc_h2, enc_dpre):
    tile = lambda i: (0, i)
    zero = lambda i: (0, 0)
    dec = [(a, a.shape, zero) for a in h2s] + [(b, (b.shape[0], D), tile) for b in dpres]
    enc = [(enc_h2, enc_h2.shape, zero), (enc_dpre, (enc_dpre.shape[0], D), tile)]
    return grad_call(
        up_grad_body, core, dec, enc,
        (TILES * GROUP_ROWS, (GROUPS, GROUP_ROWS, D), lambda i: (0, i, 0)), bit, "up_grad",
    )


def heads_grad_body(bit, core_ref, *refs):
    take = taker(refs)
    hs, atts, dqkvs, dbranches, smalls = take(2), take(2), take(2), take(2), take(2)
    enc_h, enc_att, enc_dqkv, enc_dbranch, enc_small = take(5)
    out_refs = refs[15:]
    step = pl.program_id(0)

    def give(part, made):
        made = made.astype(BF16).reshape(GROUPS, GROUP_ROWS, D)
        put(core_ref, bit, made, out_refs, slice(part * GROUP_ROWS, (part + 1) * GROUP_ROWS))

    def extra(small):
        for out_ref in out_refs:
            shape = (out_ref.shape[0], ROWS, D)
            out_ref[:, TILES * GROUP_ROWS :, :] = jnp.broadcast_to(small.astype(BF16), shape)

    for part in range(3):

        @pl.when(jnp.logical_and(step == part, core_ref[0] != 0))
        def _():
            give(part, tn(hs[0][...], dqkvs[0][0]) + tn(hs[1][...], dqkvs[1][0]))

        @pl.when(jnp.logical_and(step == part, core_ref[0] == 0))
        def _():
            give(part, tn(enc_h[...], enc_dqkv[0]))

    @pl.when(jnp.logical_and(step == 3, core_ref[0] != 0))
    def _():
        give(3, nn(atts[0][...], dbranches[0][...]) + nn(atts[1][...], dbranches[1][...]))
        extra(smalls[0][...] + smalls[1][...])

    @pl.when(jnp.logical_and(step == 3, core_ref[0] == 0))
    def _():
        give(3, nn(enc_att[...], enc_dbranch[...]))
        extra(enc_small[...])


def heads_grad(core, bit, dec, enc):
    zero = lambda i: (0, 0)

    def specs(h, att, dqkv, dbranch, small):
        part = lambda i: (jnp.minimum(i, 2), 0, 0)
        return [
            (h, h.shape, zero),
            (att, att.shape, zero),
            (dqkv, (1, *dqkv.shape[1:]), part),
            (dbranch, dbranch.shape, zero),
            (small, small.shape, zero),
        ]

    dec = [one for pair in zip(*[specs(*operands) for operands in dec]) for one in pair]
    rows = TILES * GROUP_ROWS + ROWS
    return grad_call(
        heads_grad_body, core, dec, specs(*enc),
        (rows, (GROUPS, rows, D), lambda i: (0, 0, 0)), bit, "heads_grad",
    )


def swapped(value):
    return lax.ppermute(value, "pipe", [(0, 1), (1, 0)])


def across(value, bit):
    size = lax.axis_size("dp")
    return lax.ppermute(value, "dp", [(i, i ^ 2**bit) for i in range(size)])


def dp_bit(bit):
    return lax.rem(lax.axis_index("dp") // 2**bit, 2)


class Order:
    def __init__(self):
        self.last = None

    def __call__(self, step, *operands):
        if self.last is not None:
            operands, _ = lax.optimization_barrier((operands, self.last))
        made = step(*operands)
        self.last = jax.tree.leaves(made)[0]
        return made


class Sum:
    def __init__(self, arrays, order):
        go, self.stay = arrays
        self.order = list(order)
        bit = self.order.pop(0)
        self.bits = [b for b in range(GROUPS.bit_length() - 2, -1, -1) if b != bit]
        self.got = across(go, bit)

    def step(self, run):
        if not self.order:
            self.value = run(
                lambda stay, got: (stay.astype(F32) + got.astype(F32))[0], self.stay, self.got
            )
            return
        bit = self.order.pop(0)
        shape = self.stay.shape
        at = self.bits.index(bit)
        self.bits.remove(bit)
        left = 2 ** len(self.bits)

        def half(which):
            def make(stay, got):
                made = (stay.astype(F32) + got.astype(F32)).astype(BF16)
                made = made.reshape(2**at, 2, left // 2**at, *shape[1:])
                chosen = lax.dynamic_index_in_dim(made, which, 1, keepdims=False)
                return chosen.reshape(left, *shape[1:])

            return make

        mine = dp_bit(bit)
        go = run(half(1 - mine), self.stay, self.got)
        stay = run(half(mine), self.stay, self.got)
        self.got, self.stay = across(go, bit), stay


class PlainSum:
    def __init__(self, arrays, slabs):
        (whole,) = arrays
        size = lax.axis_size("dp")
        rows = whole.shape[1] // slabs // ROWS * ROWS
        extra = whole[0, slabs * rows :] if slabs * rows < whole.shape[1] else None
        grad = whole[:, : slabs * rows].reshape(GROUPS, slabs, rows, D).transpose(0, 2, 1, 3)
        grad = grad.reshape(GROUPS * rows, slabs * D).astype(F32)
        mine = lax.psum_scatter(grad, "dp", scatter_dimension=0, tiled=True)
        mine = mine.reshape(-1, slabs, D).transpose(1, 0, 2).reshape(-1, D)
        if extra is not None:
            mine = jnp.concatenate([mine, lax.psum(extra.astype(F32), "dp")])
        self.value = mine

    def step(self, run):
        pass


DOWN_ORDER = (0, 1, 2, 3)
UP_ORDER = (1, 0, 2, 3)
HEADS_ORDER = (2, 0, 1, 3)


def on_device(
    section_input,
    visible_slot,
    image_of_slot,
    qkv_weight,
    out_weight,
    up_weight,
    down_weight,
    norm_gain,
    up_bias,
    vectors,
):
    pipe = lax.axis_index("pipe")
    size = lax.axis_size("dp")
    halving = size == GROUPS
    core = jnp.stack([pipe] + [dp_bit(bit) for bit in range(GROUPS.bit_length() - 1)])
    own = [qkv_weight[0], out_weight[0], up_weight[0], down_weight[0]]
    params = [vectors, norm_gain, up_bias]
    layout = (visible_slot, image_of_slot)
    rows = MICRO * VIS
    run = Order()
    both = [[weight, swapped(weight)] for weight in own]
    other_params = [swapped(value) for value in params]
    other_dff = swapped(section_input[0, 0])

    enc_x, enc_h, enc_qkv, enc_att, enc_lse, enc_mid, enc_h2, enc_act, enc_slope, sent = run(
        lambda section, *w: encoder_forward(core, rows, params, layout, section, w),
        section_input, *own,
    )
    other_sent = swapped(sent)
    x, h, qkv, att, lse, h2, act, decoded, dpre, dbranch, dmid, datt, small = run(
        lambda sent, other_sent, other_dff, *w: decoder(
            core, S, params, other_params, layout, sent, other_sent, section_input, other_dff,
            [w[2 * i : 2 * i + 2] for i in range(4)],
        ),
        sent, other_sent, other_dff, *[w for pair in both for w in pair],
    )
    other_act = swapped(act)
    other_dpre, other_h2, other_decoded = map(swapped, (dpre, h2, decoded))
    dqkv, small, returned = run(
        lambda qkv, att, datt, lse, small, x, dmid: decoder_back(
            core, S, params, other_params, layout, qkv, att, datt, lse, small, x, dmid, both[0]
        ),
        qkv, att, datt, lse, small, x, dmid,
    )
    other_returned = swapped(returned)
    other_dqkv, other_small = swapped(dqkv), swapped(small)
    other_h, other_att, other_dbranch = map(swapped, (h, att, dbranch))

    def begin(arrays, order, slabs):
        return Sum(arrays, order) if halving else PlainSum(arrays, slabs)

    def first_of(order):
        return order[0] if halving else None

    down = run(
        lambda *a: down_grad(
            core, first_of(DOWN_ORDER), a[:2], section_input[0], enc_act, a[2:4]
        ),
        act, other_act, returned, other_returned,
        other_dpre, other_h2, other_decoded, other_dqkv, other_small, other_h, other_att,
        other_dbranch,
    )
    down = begin(down, DOWN_ORDER, 1)
    enc_dpre, enc_dbranch, enc_dqkv, enc_small, results = run(
        lambda dy, other_dy, other_decoded: encoder_back(
            core, rows, params, layout, dy, other_dy, enc_att, enc_lse, enc_slope, enc_mid,
            enc_qkv, enc_x, decoded, other_decoded, own,
        ),
        returned, other_returned, other_decoded,
    )
    up = run(
        lambda *a: up_grad(core, first_of(UP_ORDER), a[:2], a[2:4], enc_h2, a[4]),
        h2, other_h2, dpre, other_dpre, enc_dpre,
    )
    up = begin(up, UP_ORDER, 4)
    heads = run(
        lambda *a: heads_grad(
            core, first_of(HEADS_ORDER), (a[0:5], a[5:10]), (enc_h, enc_att, *a[10:])
        ),
        h, att, dqkv, dbranch, small,
        other_h, other_att, other_dqkv, other_dbranch, other_small,
        enc_dqkv, enc_dbranch, enc_small,
    )
    heads = begin(heads, HEADS_ORDER, 4)
    for _ in range(len(DOWN_ORDER)):
        for one in (down, up, heads):
            one.step(run)
    width = D // size
    down, up, heads = down.value, up.value, heads.value

    def wide(slabs):
        return jnp.concatenate(
            [slabs[i * width : (i + 1) * width] for i in range(slabs.shape[0] // width)], axis=1
        )

    small = heads[TILES * width :]
    heads = heads[: TILES * width]
    place = lax.axis_index("dp")
    mine = lax.dynamic_slice_in_dim(small, place * width, width, 1)
    hidden = FF // size
    bias_grad = lax.dynamic_slice_in_dim(
        small[UBIAS : UBIAS + TILES].reshape(FF), place * hidden, hidden, 0
    )
    return (
        results[None],
        wide(heads[: 3 * width])[None],
        heads[3 * width :][None],
        wide(up)[None],
        down[None],
        mine[GAIN1 : GAIN2 + 1][None],
        bias_grad[None],
        mine[:GAIN1][None],
    )


def solution(mesh):
    in_specs = (
        P("pipe", "dp", None, None),
        P("dp", None),
        P("dp", None),
        P("pipe", None, None),
        P("pipe", None, None),
        P("pipe", None, None),
        P("pipe", None, None),
        P("pipe", None, None),
        P("pipe", None),
        P("pipe", None, None),
    )
    out_specs = (
        P("pipe", "dp", None, None),
        P("pipe", "dp", None),
        P("pipe", "dp", None),
        P("pipe", "dp", None),
        P("pipe", "dp", None),
        P("pipe", None, "dp"),
        P("pipe", "dp"),
        P("pipe", None, "dp"),
    )
    return jax.shard_map(
        on_device, mesh=mesh, in_specs=in_specs, out_specs=out_specs, check_vma=False
    )
```

```python
import functools
import math

import jax
import jax.numpy as jnp
import numpy as np
from jax import lax
from jax.experimental import pallas as pl
from jax.experimental.pallas import tpu as pltpu
from jax.sharding import PartitionSpec as P

D = 768
H = 12
HD = 64
FF = 3072
S = 512
VIS = 128
MICRO = 2
EPSILON = 1e-06
PAIRS = H // 2
TWO = 2 * HD
TILES = FF // D
WIDE = 2 * D
LOADS = FF // WIDE
HALF = D // 2
GROUPS = 16
GROUP_ROWS = D // GROUPS
PER = GROUPS // TILES
DOWN_ROWS = FF // GROUPS
ROWS = 16
FAR = -1e30
F32 = jnp.float32
BF16 = jnp.bfloat16

SHIFT1, QBIAS, VBIAS, OBIAS, ENTRY, SHIFT2, DBIAS, GAIN1, GAIN2, UBIAS = range(10)


def contract(left, right, left_dim, right_dim):
    return lax.dot_general(
        left, right, (((left_dim,), (right_dim,)), ((), ())), preferred_element_type=F32
    )


def nn(left, right):
    return contract(left, right, 1, 0)


def nt(left, right):
    return contract(left, right, 1, 1)


def tn(left, right):
    return contract(left, right, 0, 0)


def unit_rows(rows):
    centered = rows - jnp.mean(rows, axis=-1, keepdims=True)
    scale = lax.rsqrt(jnp.mean(centered * centered, axis=-1, keepdims=True) + EPSILON)
    return centered * scale, scale


def unit_rows_back(grad, unit, scale, gain):
    scaled = grad * gain
    return scale * (
        scaled
        - jnp.mean(scaled, axis=-1, keepdims=True)
        - unit * jnp.mean(scaled * unit, axis=-1, keepdims=True)
    )


def in_head(shape, which):
    lane = lax.broadcasted_iota(jnp.int32, shape, 1)
    return lane < HD if which == 0 else lane >= HD


def one_head(pair, which):
    return jnp.where(in_head(pair.shape, which), pair, jnp.zeros_like(pair))


def colsum(rows):
    return jnp.sum(rows, axis=0, keepdims=True)


class Params:
    def __init__(self, core, refs):
        self.core, self.refs = core, refs

    def hidden(self, t):
        if len(self.refs) == 3:
            return self.refs[2][:, pl.ds(pl.multiple_of(t * WIDE, WIDE), WIDE)]
        each = WIDE // D
        return jnp.concatenate(
            [self.pick(pl.ds(UBIAS + t * each + part, 1)) for part in range(each)], axis=1
        )

    def __call__(self, index):
        at = slice(index, index + 1)
        if len(self.refs) < 3:
            return self.pick(at)
        if index < GAIN1:
            return self.refs[0][index]
        return self.refs[1][0, index - GAIN1 : index - GAIN1 + 1]

    def pick(self, at):
        return jnp.where(self.core == 0, self.refs[1][at], self.refs[0][at])


def upright(line):
    return jnp.broadcast_to(line, (8, line.shape[1])).T[:, :1]


def hits(slots):
    return lax.broadcasted_iota(jnp.int32, (VIS, S), 0).astype(F32) == slots


def hits_upright(slots):
    return lax.broadcasted_iota(jnp.int32, (S, VIS), 1).astype(F32) == slots


def marks(groups, count):
    lane = lax.broadcasted_iota(jnp.int32, (groups.shape[0], TWO), 1)
    lane = jnp.where(lane < HD, lane, lane - HD).astype(F32)
    same = lane == groups
    key_fill = jnp.where(same, 1.0, 0.0).astype(BF16)
    query_fill = jnp.where(jnp.logical_or(same, lane >= count), 0.0, FAR).astype(BF16)
    return key_fill, query_fill


class Weight:
    def __init__(self, core, refs, dst, sems, cuts):
        self.core, self.refs, self.dst, self.sems, self.cuts = core, refs, dst, sems, cuts

    def start(self, i):
        cut = self.cuts[i]

        def go(ref):
            pltpu.make_async_copy(ref.at[cut], self.dst.at[cut], self.sems.at[i]).start()

        if len(self.refs) == 1:
            go(self.refs[0])
        else:
            pl.when(self.core == 0)(lambda: go(self.refs[1]))
            pl.when(self.core != 0)(lambda: go(self.refs[0]))

    def get(self, i):
        cut = self.cuts[i]
        pltpu.make_async_copy(self.refs[0].at[cut], self.dst.at[cut], self.sems.at[i]).wait()
        return self.dst[cut]


    def take(self, i, cut):
        pltpu.make_async_copy(self.refs[0].at[cut], self.dst.at[cut], self.sems.at[i]).wait()
        return self.dst[cut]


class Either:
    def __init__(self, core, on_first, on_second, dst, sem):
        self.copy = pltpu.make_async_copy(on_first, dst, sem)
        self.dst = dst
        pl.when(core == 0)(self.copy.start)
        pl.when(core != 0)(lambda: pltpu.make_async_copy(on_second, dst, sem).start())

    def get(self):
        self.copy.wait()
        return self.dst[...]


class Out:
    def __init__(self, sems):
        self.sems, self.count, self.going = sems, 0, []

    def send(self, src, dst):
        copy = pltpu.make_async_copy(src, dst, self.sems.at[self.count])
        self.count += 1
        copy.start()
        self.going.append(copy)

    def wait(self):
        for copy in self.going:
            copy.wait()


SMEM, VMEM, HBM = pltpu.SMEM, pltpu.VMEM, pl.ANY


def struct(shape, dtype):
    return jax.ShapeDtypeStruct(shape, dtype)


def size_of(shape):
    return math.prod(shape.shape) * shape.dtype.itemsize


def call(body, ins, outs, scratch, name, flops):
    arrays = [array for array, _ in ins]
    shapes = [shape for shape, _ in outs]
    return pl.pallas_call(
        body,
        in_specs=[pl.BlockSpec(memory_space=space) for _, space in ins],
        out_specs=[pl.BlockSpec(memory_space=space) for _, space in outs],
        out_shape=shapes,
        scratch_shapes=scratch,
        compiler_params=pltpu.CompilerParams(vmem_limit_bytes=60 * 2**20),
        cost_estimate=pl.CostEstimate(flops=1, bytes_accessed=1, transcendentals=0),
        name=name,
    )(*arrays)


def taker(refs):
    refs = list(refs)

    def take(count):
        return [refs.pop(0) for _ in range(count)]

    return take


def columns(i):
    return (slice(None), slice(i * D, (i + 1) * D))


def positions():
    width = D // 2
    frequency = np.exp(np.arange(width) * (-math.log(10000.0) / width))
    angles = np.arange(S)[:, None] * frequency[None, :]
    return jnp.asarray(np.concatenate([np.sin(angles), np.cos(angles)], axis=1), F32)


def section(i):
    return columns(i)


def group_columns(core, decoder, slots_ref, images_ref):
    if decoder:
        return upright(images_ref[pl.ds(core, 1), :].astype(F32)), 2
    parts = []
    for micro in range(MICRO):
        hit = hits(slots_ref[micro : micro + 1, :].astype(F32))
        mark = images_ref[micro : micro + 1, :].astype(F32) + 1.0
        parts.append(jnp.sum(jnp.where(hit, mark, 0.0), axis=1, keepdims=True) + 3.0 * micro)
    return jnp.concatenate(parts, axis=0), 3 * MICRO


def project(params, weight, x_s, h_s, qkv_s, out, h_out, qkv_out):
    unit, _scale = unit_rows(x_s[...])
    h = (unit * params(GAIN1) + params(SHIFT1)).astype(BF16)
    h_s[...] = h
    out.send(h_s, h_out)
    for part, bias in enumerate((QBIAS, None, VBIAS)):
        made = nn(h, weight.get(part))
        if bias is not None:
            made = made + params(bias)
        qkv_s[part] = made.astype(BF16)
        out.send(qkv_s.at[part], qkv_out.at[part])


def attend(n, together, fills, qkv_s, att_s, lse_ref):
    key_fill, query_fill = fills
    scaling = jnp.asarray(HD**-0.5, BF16)

    def pairs(step, _):
        lanes = [
            pl.ds(pl.multiple_of((step * together + i) * TWO, TWO), TWO) for i in range(together)
        ]
        heads = [(i, which) for i in range(together) for which in range(2)]
        qs = [qkv_s[0, :, at] * scaling for at in lanes]
        ks = [qkv_s[1, :, at] for at in lanes]
        vs = [qkv_s[2, :, at].T for at in lanes]
        scores = [
            nt(
                jnp.where(in_head((n, TWO), which), ks[i], key_fill),
                jnp.where(in_head((n, TWO), which), qs[i], query_fill),
            )
            for i, which in heads
        ]
        tops = [jnp.max(score, axis=0, keepdims=True) for score in scores]
        raised = [jnp.exp(score - top) for score, top in zip(scores, tops)]
        totals = [colsum(part) for part in raised]
        found = [
            nn(vs[i][which * HD : (which + 1) * HD, :], part.astype(BF16)) * (1.0 / total)
            for (i, which), part, total in zip(heads, raised, totals)
        ]
        for i in range(together):
            att_s[:, lanes[i]] = jnp.concatenate(found[2 * i : 2 * i + 2], axis=0).T.astype(BF16)
            lse_ref[step * together + i] = jnp.concatenate(
                [tops[at] + jnp.log(totals[at]) for at in (2 * i, 2 * i + 1)], axis=0
            )
        return 0

    lax.fori_loop(0, PAIRS // together, pairs, 0)


def feed(params, weights, x_s, att_s, mid_s, h2_s, act_s, slope_s, sum_s, out, h2_out, act_out):
    out_weight, up, down = weights
    mid = x_s[...] + nn(att_s[...], out_weight.get(0)) + params(OBIAS)
    mid_s[...] = mid
    unit, _scale = unit_rows(mid)
    h2 = (unit * params(GAIN2) + params(SHIFT2)).astype(BF16)
    h2_s[...] = h2
    out.send(h2_s, h2_out)
    sum_s[...] = mid + params(DBIAS)

    def tile(t, _):
        at = (slice(None), pl.ds(pl.multiple_of(t * WIDE, WIDE), WIDE))
        pre = nn(h2_s[...], up.take(t, at)) + params.hidden(t)
        below = 0.5 + 0.5 * lax.erf(pre * math.sqrt(0.5))
        act = (pre * below).astype(BF16)
        act_s[at] = act
        density = jnp.exp(-0.5 * pre * pre) * (1.0 / math.sqrt(2.0 * math.pi))
        slope_s[at] = (below + pre * density).astype(BF16)
        sum_s[...] += nn(act, down.take(t, (at[1], slice(None))))
        return 0

    lax.fori_loop(0, LOADS, tile, 0)
    out.send(act_s, act_out)


def feed_back(
    params, weights, dff, dff_ref, slope, mid, dpre_s, dh2_s, small_ref, out, dpre_out, width
):
    out_weight, up, down = weights
    small_ref[...] = jnp.zeros_like(small_ref)
    small_ref[DBIAS : DBIAS + 1, :] = colsum(dff.astype(F32))
    if dff_ref is not None:
        dff_ref[...] = dff
    dh2_s[...] = jnp.zeros_like(dh2_s)

    def tile(t, _):
        at = (slice(None), pl.ds(pl.multiple_of(t * width, width), width))
        dact = nt(dff_ref[...], down(t, (at[1], slice(None))))
        dpre = (dact * slope(t, at).astype(F32)).astype(BF16)
        dpre_s[at] = dpre
        sums = colsum(dpre.astype(F32))
        for part in range(width // D):
            small_ref[pl.ds(UBIAS + t * (width // D) + part, 1), :] = sums[columns(part)]
        dh2_s[...] += nt(dpre, up(t, at))
        return 0

    lax.fori_loop(0, FF // width, tile, 0)
    out.send(dpre_s, dpre_out)
    dh2 = dh2_s[...]
    unit, scale = unit_rows(mid())
    small_ref[GAIN2 : GAIN2 + 1, :] = colsum(dh2 * unit)
    small_ref[SHIFT2 : SHIFT2 + 1, :] = colsum(dh2)
    dmid = dff.astype(F32) + unit_rows_back(dh2, unit, scale, params(GAIN2))
    dbranch = dmid.astype(BF16)
    small_ref[OBIAS : OBIAS + 1, :] = colsum(dbranch.astype(F32))
    return dmid, dbranch, nt(dbranch, out_weight()).astype(BF16)


def attend_back(n, together, fills, qkv_ref, att_ref, datt_ref, lse_ref, dqkv_ref):
    key_fill, query_fill = fills
    scaling = jnp.asarray(HD**-0.5, BF16)

    def pairs(step, _):
        lanes = [
            pl.ds(pl.multiple_of((step * together + i) * TWO, TWO), TWO) for i in range(together)
        ]
        heads = [(i, which) for i in range(together) for which in range(2)]
        qs = [qkv_ref[0, :, at] * scaling for at in lanes]
        ks = [qkv_ref[1, :, at] for at in lanes]
        vs = [qkv_ref[2, :, at] for at in lanes]
        turned = [k.T for k in ks]
        dos = [datt_ref[:, at] for at in lanes]
        mine = [one_head(dos[i], which) for i, which in heads]
        along = [
            (att_ref[:, at].astype(F32) * do.astype(F32)).T for at, do in zip(lanes, dos)
        ]
        scores = [
            nt(
                jnp.where(in_head((n, TWO), which), ks[i], key_fill),
                jnp.where(in_head((n, TWO), which), qs[i], query_fill),
            )
            for i, which in heads
        ]
        dprobs = [nt(vs[i], do) for (i, which), do in zip(heads, mine)]
        probs = [
            jnp.exp(score - lse_ref[step * together + i, which : which + 1, :])
            for (i, which), score in zip(heads, scores)
        ]
        dscores = [
            (prob * (dprob - colsum(along[i][which * HD : (which + 1) * HD, :]))).astype(BF16)
            for (i, which), prob, dprob in zip(heads, probs, dprobs)
        ]
        for i in range(together):
            a, b = 2 * i, 2 * i + 1
            dv = nn(probs[a].astype(BF16), mine[a]) + nn(probs[b].astype(BF16), mine[b])
            dk = nn(dscores[a], one_head(qs[i], 0)) + nn(dscores[b], one_head(qs[i], 1))
            dq = jnp.concatenate(
                [nn(turned[i][:HD, :], dscores[a]), nn(turned[i][HD:, :], dscores[b])], axis=0
            )
            dqkv_ref[:, pl.ds(0 * D + lanes[i].start, TWO)] = (dq * HD**-0.5).T.astype(BF16)
            dqkv_ref[:, pl.ds(1 * D + lanes[i].start, TWO)] = dk.astype(BF16)
            dqkv_ref[:, pl.ds(2 * D + lanes[i].start, TWO)] = dv.astype(BF16)
        return 0

    lax.fori_loop(0, PAIRS // together, pairs, 0)


def project_back(params, weight, dqkv_ref, x, dmid, small_ref):
    dh = 0.0
    for part in range(3):
        made = dqkv_ref[columns(part)]
        if part != 1:
            bias = QBIAS if part == 0 else VBIAS
            small_ref[bias : bias + 1, :] = colsum(made.astype(F32))
        dh = dh + nt(made, weight.get(part))
    unit, scale = unit_rows(x())
    small_ref[GAIN1 : GAIN1 + 1, :] = colsum(dh * unit)
    small_ref[SHIFT1 : SHIFT1 + 1, :] = colsum(dh)
    return dmid() + unit_rows_back(dh, unit, scale, params(GAIN1))


EVERYTHING = (slice(None), slice(None))


def qkv_loads(core, refs, dst, sems):
    return Weight(core, refs, dst, sems, [columns(part) for part in range(3)])


def feed_loads(core, w_out, w_up, w_down, dsts, sems, width):
    parts = [slice(i, i + width) for i in range(0, FF, width)]
    return (
        Weight(core, w_out, dsts[0], sems[0], [EVERYTHING]),
        Weight(core, w_up, dsts[1], sems[1], [(slice(None), part) for part in parts]),
        Weight(core, w_down, dsts[2], sems[2], [(part, slice(None)) for part in parts]),
    )


def dma(count):
    return pltpu.SemaphoreType.DMA((count,))


FEED_SCRATCH = [VMEM((D, D), BF16), VMEM((D, FF), BF16), VMEM((FF, D), BF16)]
FEED_SEMS = [dma(1), dma(LOADS), dma(LOADS)]
QKV_SCRATCH = [VMEM((D, 3 * D), BF16), dma(3)]


DEC_DPRE, DEC_H2, DEC_SECTIONS = TILES, 2 * TILES, 2 * TILES + 1
LATE_H, LATE_ATT, LATE_DBRANCH, LATE_OUT, LATE_SECTIONS = range(5)
ENC_H, ENC_H2, ENC_ATT, ENC_SECTIONS = range(TILES, TILES + 4)
ENC_DBRANCH, ENC_DQKV, ENC_BACK_SECTIONS = TILES, TILES + 1, TILES + 4


def sections(first, count):
    return (slice(None), slice(first * D, (first + count) * D))


def encoder_forward_body(n, *refs):
    take = taker(refs)
    given = take(3)
    core = lax.axis_index("pipe")
    params = Params(core, given)
    slots_ref, images_ref, section_ref = take(3)
    w_qkv, w_out, w_up, w_down = take(1), take(1), take(1), take(1)
    x_out, factors_out, qkv_out, lse_ref, mid_out, slope_out, sent_ref, params_ref = take(8)
    x_s, h_s, qkv_s, att_s, mid_s, h2_s, act_s, slope_s, sum_s = take(9)
    wq_s, wq_sems = take(2)
    dsts, sems = take(3), take(3)
    (out_sems,) = take(1)
    for i in range(GAIN1):
        params_ref[i : i + 1, :] = given[0][i]
    params_ref[GAIN1:UBIAS, :] = given[1][0]
    for t in range(TILES):
        params_ref[UBIAS + t : UBIAS + t + 1, :] = given[2][columns(t)]

    @pl.when(core != 0)
    def _():
        sent_ref[n:, :] = section_ref[0, 0]

    @pl.when(core == 0)
    def _():
        weight = qkv_loads(core, w_qkv, wq_s, wq_sems)
        weights = feed_loads(core, w_out, w_up, w_down, dsts, sems, WIDE)
        for part in range(3):
            weight.start(part)
        weights[0].start(0)
        for t in range(LOADS):
            weights[1].start(t)
            weights[2].start(t)
        out = Out(out_sems)
        for micro in range(MICRO):
            hit = hits(slots_ref[micro : micro + 1, :].astype(F32))
            x_s[micro * VIS : (micro + 1) * VIS, :] = nn(
                hit.astype(BF16), section_ref[0, micro]
            ) + params(ENTRY)
        out.send(x_s, x_out)
        project(params, weight, x_s, h_s, qkv_s, out, factors_out.at[section(ENC_H)], qkv_out)
        fills = marks(*group_columns(core, False, slots_ref, images_ref))
        attend(n, 3, fills, qkv_s, att_s, lse_ref)
        out.send(att_s, factors_out.at[section(ENC_ATT)])
        feed(
            params, weights, x_s, att_s, mid_s, h2_s, act_s, slope_s, sum_s, out,
            factors_out.at[section(ENC_H2)], factors_out.at[sections(0, TILES)],
        )
        out.send(mid_s, mid_out)
        out.send(slope_s, slope_out)
        sent_ref[:n, :] = sum_s[...].astype(BF16)
        out.wait()


def encoder_forward(n, params, layout, section, weights):
    ins = [(a, VMEM) for a in (*params, *layout, section)]
    ins += [(w, HBM) for w in weights]
    outs = [
        (struct((n, D), F32), HBM),
        (struct((n, ENC_SECTIONS * D), BF16), HBM),
        (struct((3, n, D), BF16), HBM),
        (struct((PAIRS, 2, n), F32), VMEM),
        (struct((n, D), F32), HBM),
        (struct((n, FF), BF16), HBM),
        (struct((n + S, D), BF16), VMEM),
        (struct((ROWS, D), F32), VMEM),
    ]
    scratch = [
        VMEM((n, D), F32),
        VMEM((n, D), BF16),
        VMEM((3, n, D), BF16),
        VMEM((n, D), BF16),
        VMEM((n, D), F32),
        VMEM((n, D), BF16),
        VMEM((n, FF), BF16),
        VMEM((n, FF), BF16),
        VMEM((n, D), F32),
        *QKV_SCRATCH,
        *FEED_SCRATCH,
        *FEED_SEMS,
        dma(10),
    ]
    return call(
        functools.partial(encoder_forward_body, n),
        ins,
        outs,
        scratch,
        "encoder_forward",
        2 * n * (4 * D * D + 2 * D * FF),
    )


def decoder_body(n, *refs):
    take = taker(refs)
    core = lax.axis_index("pipe")
    params = Params(core, take(2))
    slots_ref, images_ref, pos_ref, sent_ref, other_sent_ref, section_ref = take(6)
    w_qkv, w_out, w_up, w_down = take(2), take(2), take(2), take(2)
    x_out, factors_out, late_out, qkv_out, lse_ref, dmid_ref, datt_ref, small_ref = take(8)
    x_s, h_s, qkv_s, att_s, mid_s, h2_s, act_s, slope_s, sum_s, dpre_s, dff_s = take(11)
    sent_s, dbranch_s, decoded_s = take(3)
    wq_s, wq_sems = take(2)
    dsts, sems = take(3), take(3)
    out_sems, in_sems = take(2)
    rows = MICRO * VIS
    sent = Either(
        core, sent_ref.at[:VIS], other_sent_ref.at[rows - VIS : rows], sent_s, in_sems.at[0]
    )
    weight = qkv_loads(core, w_qkv, wq_s, wq_sems)
    weights = feed_loads(core, w_out, w_up, w_down, dsts, sems, WIDE)
    for part in range(3):
        weight.start(part)
    weights[0].start(0)
    for t in range(LOADS):
        weights[1].start(t)
        weights[2].start(t)
    dff = Either(core, other_sent_ref.at[rows:], section_ref.at[0, 1], dff_s, in_sems.at[1])
    out = Out(out_sems)
    slots = upright(slots_ref[pl.ds(core, 1), :].astype(F32))
    x = nn(hits_upright(slots).astype(BF16), sent.get()) + pos_ref[...]
    x_s[...] = x + jnp.where(slots == VIS, params(ENTRY), 0.0)
    out.send(x_s, x_out)
    project(params, weight, x_s, h_s, qkv_s, out, late_out.at[section(LATE_H)], qkv_out)
    fills = marks(*group_columns(core, True, slots_ref, images_ref))
    attend(n, 2, fills, qkv_s, att_s, lse_ref)
    out.send(att_s, late_out.at[section(LATE_ATT)])
    feed(
        params, weights, x_s, att_s, mid_s, h2_s, act_s, slope_s, sum_s, out,
        factors_out.at[section(DEC_H2)], factors_out.at[sections(0, TILES)],
    )
    decoded_s[...] = sum_s[...].astype(BF16)
    out.send(decoded_s, late_out.at[section(LATE_OUT)])
    dmid_ref[...], dbranch_s[...], datt_ref[...] = feed_back(
        params,
        (
            lambda: weights[0].dst[...],
            lambda t, at: weights[1].dst[at],
            lambda t, at: weights[2].dst[at],
        ),
        dff.get(),
        dff_s,
        lambda t, at: slope_s[at],
        lambda: mid_s[...],
        dpre_s,
        sum_s,
        small_ref,
        out,
        factors_out.at[sections(DEC_DPRE, TILES)],
        WIDE,
    )
    out.send(dbranch_s, late_out.at[section(LATE_DBRANCH)])
    out.wait()


def decoder(n, params, other_params, layout, sent, other_sent, section, weights):
    ins = [(a, VMEM) for a in (params, other_params, *layout, positions())]
    ins += [(a, HBM) for a in (sent, other_sent, section)]
    ins += [(w, HBM) for pair in weights for w in pair]
    outs = [
        (struct((n, D), F32), HBM),
        (struct((n, DEC_SECTIONS * D), BF16), HBM),
        (struct((n, LATE_SECTIONS * D), BF16), HBM),
        (struct((3, n, D), BF16), HBM),
        (struct((PAIRS, 2, n), F32), VMEM),
        (struct((n, D), F32), VMEM),
        (struct((n, D), BF16), VMEM),
        (struct((ROWS, D), F32), VMEM),
    ]
    scratch = [
        VMEM((n, D), F32),
        VMEM((n, D), BF16),
        VMEM((3, n, D), BF16),
        VMEM((n, D), BF16),
        VMEM((n, D), F32),
        VMEM((n, D), BF16),
        VMEM((n, FF), BF16),
        VMEM((n, FF), BF16),
        VMEM((n, D), F32),
        VMEM((n, FF), BF16),
        VMEM((n, D), BF16),
        VMEM((VIS, D), BF16),
        VMEM((n, D), BF16),
        VMEM((n, D), BF16),
        *QKV_SCRATCH,
        *FEED_SCRATCH,
        *FEED_SEMS,
        dma(12),
        dma(2),
    ]
    return call(
        functools.partial(decoder_body, n),
        ins,
        outs,
        scratch,
        "decoder",
        2 * n * (5 * D * D + 4 * D * FF) + 4 * n * n * D,
    )


def decoder_back_body(n, *refs):
    take = taker(refs)
    core = lax.axis_index("pipe")
    params = Params(core, take(2))
    slots_ref, images_ref, qkv_ref, datt_ref, lse_ref, small_in = take(6)
    x_in, dmid_in, factors_in = take(3)
    w_qkv = take(2)
    dqkv_out, back_ref = take(2)
    dqkv_s, x_s, dmid_s, att_s, small_s, wq_s, wq_sems, in_sems, out_sems = take(9)
    att = pltpu.make_async_copy(factors_in.at[section(LATE_ATT)], att_s, in_sems.at[2])
    att.start()
    weight = qkv_loads(core, w_qkv, wq_s, wq_sems)
    x = Weight(core, [x_in], x_s, in_sems, [EVERYTHING])
    dmid = Weight(core, [dmid_in], dmid_s, in_sems.at[pl.ds(1, 1)], [EVERYTHING])
    for part in range(3):
        weight.start(part)
    x.start(0)
    dmid.start(0)
    fills = marks(*group_columns(core, True, slots_ref, images_ref))
    att.wait()
    attend_back(n, 1, fills, qkv_ref, att_s, datt_ref, lse_ref, dqkv_s)
    out = Out(out_sems)
    out.send(dqkv_s, dqkv_out)
    small_s[...] = small_in[...]
    dx = project_back(
        params, weight, dqkv_s, lambda: x.get(0), lambda: dmid.get(0), small_s
    )
    slots = slots_ref[pl.ds(core, 1), :].astype(F32)
    small_s[ENTRY : ENTRY + 1, :] = colsum(jnp.where(upright(slots) == VIS, dx, 0.0))
    back_ref[:VIS, :] = nn(hits(slots).astype(BF16), dx.astype(BF16)).astype(BF16)
    back_ref[VIS:, :] = small_s[...].astype(BF16)
    out.wait()


def decoder_back(
    n, params, other_params, layout, qkv, datt, lse, small, x, dmid, factors, w_qkv
):
    ins = [(a, VMEM) for a in (params, other_params, *layout)]
    ins += [(a, VMEM) for a in (qkv, datt, lse, small)]
    ins += [(a, HBM) for a in (x, dmid, factors, *w_qkv)]
    outs = [
        (struct((n, 3 * D), BF16), HBM),
        (struct((VIS + ROWS, D), BF16), VMEM),
    ]
    scratch = [
        VMEM((n, 3 * D), BF16),
        VMEM((n, D), F32),
        VMEM((n, D), F32),
        VMEM((n, D), BF16),
        VMEM((ROWS, D), F32),
        *QKV_SCRATCH,
        dma(3),
        dma(1),
    ]
    return call(
        functools.partial(decoder_back_body, n),
        ins,
        outs,
        scratch,
        "decoder_back",
        2 * n * D * 3 * D + 10 * n * n * D,
    )


def encoder_back_body(n, *refs):
    take = taker(refs)
    core = lax.axis_index("pipe")
    params = Params(core, take(3))
    slots_ref, images_ref, dy_ref, other_dy_ref, lse_ref = take(5)
    slope_in, mid_in, qkv_in, x_in, enc_in = take(5)
    w_qkv, w_out, w_up, w_down = take(1), take(1), take(1), take(1)
    factors_out, small_ref, results_out = take(3)
    slope_s, mid_s, qkv_s, x_s, att_s, dpre_s, dh2_s, dbranch_s, datt_s, dqkv_s, back_s = take(11)
    wq_s, wq_sems = take(2)
    dsts, sems = take(3), take(3)
    in_sems, out_sems = take(2)

    @pl.when(core == 0)
    def _():
        weight = qkv_loads(core, w_qkv, wq_s, wq_sems)
        weights = feed_loads(core, w_out, w_up, w_down, dsts, sems, D)
        out_weight, up, down = weights
        slope = Weight(core, [slope_in], slope_s, in_sems, [columns(t) for t in range(TILES)])
        mid = Weight(core, [mid_in], mid_s, in_sems.at[pl.ds(TILES, 1)], [EVERYTHING])
        qkv = Weight(
            core, [qkv_in], qkv_s, in_sems.at[pl.ds(TILES + 1, 1)], [(slice(None),) * 3]
        )
        x = Weight(core, [x_in], x_s, in_sems.at[pl.ds(TILES + 2, 1)], [EVERYTHING])
        att = pltpu.make_async_copy(
            enc_in.at[section(ENC_ATT)], att_s, in_sems.at[TILES + 3]
        )
        for t in range(TILES):
            down.start(t)
            slope.start(t)
            up.start(t)
        mid.start(0)
        out_weight.start(0)
        qkv.start(0)
        att.start()
        for part in range(3):
            weight.start(part)
        x.start(0)
        out = Out(out_sems)
        dff = jnp.concatenate([dy_ref[:VIS, :], other_dy_ref[:VIS, :]], axis=0)
        dmid, dbranch, datt = feed_back(
            params, (lambda: out_weight.get(0), up.take, down.take), dff, datt_s, slope.take,
            lambda: mid.get(0), dpre_s, dh2_s, small_ref, out,
            factors_out.at[sections(0, TILES)], D,
        )
        dh2_s[...] = dmid
        dbranch_s[...] = dbranch
        out.send(dbranch_s, factors_out.at[section(ENC_DBRANCH)])
        datt_s[...] = datt
        fills = marks(*group_columns(core, False, slots_ref, images_ref))
        qkv.get(0)
        att.wait()
        attend_back(n, 2, fills, qkv_s, att_s, datt_s, lse_ref, dqkv_s)
        out.send(dqkv_s, factors_out.at[sections(ENC_DQKV, 3)])
        dx = project_back(params, weight, dqkv_s, lambda: x.get(0), lambda: dh2_s[...], small_ref)
        low = dx.astype(BF16)
        small_ref[ENTRY : ENTRY + 1, :] = colsum(dx)
        for micro in range(MICRO):
            slots = upright(slots_ref[micro : micro + 1, :].astype(F32))
            back_s[micro] = nn(
                hits_upright(slots).astype(BF16), low[micro * VIS : (micro + 1) * VIS, :]
            ).astype(BF16)
        out.send(back_s, results_out)
        out.wait()


def encoder_back(
    n, params, layout, dy, other_dy, lse, slope, mid, qkv, x, enc, weights
):
    ins = [(a, VMEM) for a in (*params, *layout, dy, other_dy, lse)]
    ins += [(a, HBM) for a in (slope, mid, qkv, x, enc, *weights)]
    outs = [
        (struct((n, ENC_BACK_SECTIONS * D), BF16), HBM),
        (struct((ROWS, D), F32), VMEM),
        (struct((MICRO, S, D), BF16), HBM),
    ]
    scratch = [
        VMEM((n, FF), BF16),
        VMEM((n, D), F32),
        VMEM((3, n, D), BF16),
        VMEM((n, D), F32),
        VMEM((n, D), BF16),
        VMEM((n, FF), BF16),
        VMEM((n, D), F32),
        VMEM((n, D), BF16),
        VMEM((n, D), BF16),
        VMEM((n, 3 * D), BF16),
        VMEM((MICRO, S, D), BF16),
        *QKV_SCRATCH,
        *FEED_SCRATCH,
        dma(1),
        dma(TILES),
        dma(TILES),
        dma(TILES + 4),
        dma(4),
    ]
    return call(
        functools.partial(encoder_back_body, n),
        ins,
        outs,
        scratch,
        "encoder_back",
        2 * n * (4 * D * D + 2 * D * FF),
    )


def place_body(core_ref, _, dec_in, other_dec_in, results_out, back_s, in_sems, out_sems):
    @pl.when(core_ref[0] != 0)
    def _():
        parts = [
            pltpu.make_async_copy(ref.at[section(LATE_OUT)], back_s.at[at], in_sems.at[at])
            for at, ref in enumerate((other_dec_in, dec_in))
        ]
        out = Out(out_sems)
        for part in parts:
            part.start()
        for at, part in enumerate(parts):
            part.wait()
            out.send(back_s.at[at], results_out.at[at])
        out.wait()


def place_results(core, results, dec, other_dec):
    return pl.pallas_call(
        place_body,
        in_specs=[pl.BlockSpec(memory_space=SMEM)] + [pl.BlockSpec(memory_space=HBM)] * 3,
        out_specs=pl.BlockSpec(memory_space=HBM),
        out_shape=struct(results.shape, BF16),
        scratch_shapes=[VMEM((MICRO, S, D), BF16), dma(2), dma(2)],
        input_output_aliases={1: 0},
        name="place_results",
    )(core, results, dec, other_dec)


def put(core_ref, bit, made, out_refs, at=slice(None)):
    if bit is None:
        out_refs[0][:, at, :] = made
        return
    groups, rows, width = made.shape
    made = made.reshape(groups // 2 ** (bit + 1), 2, 2**bit, rows, width)
    mine = core_ref[1 + bit]
    low, high = made[:, 0], made[:, 1]
    for out_ref, other in zip(out_refs, (True, False)):
        chosen = jnp.where((mine == 0) != other, low, high)
        out_ref[:, at, :] = chosen.reshape(groups // 2, rows, width)


def grad_call(body, core, dec, enc, outs, bits, name):
    def only(wanted, index):
        def place(i, core):
            return tuple(jnp.where(core[0] == wanted, at, 0) for at in index(i))

        return place

    specs = [pl.BlockSpec(block, only(1, index)) for _, block, index in dec]
    specs += [pl.BlockSpec(block, only(0, index)) for _, block, index in enc]
    arrays = [a for a, _, _ in (*dec, *enc)]
    ways = 1 if bits is None else 2
    out_specs, shapes = [], []
    for rows, block, index in outs:
        spec = pl.BlockSpec((block[0] // ways, *block[1:]), lambda i, core, index=index: index(i))
        out_specs += [spec] * ways
        shapes += [struct((GROUPS // ways, rows, D), BF16)] * ways
    made = pl.pallas_call(
        functools.partial(body, bits or (None, None), ways),
        grid_spec=pltpu.PrefetchScalarGridSpec(
            num_scalar_prefetch=1, grid=(TILES,), in_specs=specs, out_specs=out_specs
        ),
        out_shape=shapes,
        compiler_params=pltpu.CompilerParams(
            vmem_limit_bytes=60 * 2**20, dimension_semantics=("arbitrary",)
        ),
        cost_estimate=pl.CostEstimate(flops=1, bytes_accessed=1, transcendentals=0),
        name=name,
    )(core, *arrays)
    return made[:ways], made[ways:]


def on_either(core_ref, dec, enc):
    pl.when(core_ref[0] != 0)(dec)
    pl.when(core_ref[0] == 0)(enc)


def down_grad_body(bits, ways, core_ref, a0, a1, b0, b1, c, d0, d1, *out_refs):
    step = pl.program_id(0)

    def give(made):
        made = made.astype(BF16).reshape(PER, 2, DOWN_ROWS // 2, D)
        for part, bit in enumerate(bits):
            refs = out_refs[part * ways : (part + 1) * ways]
            if bit != 2:
                put(core_ref, bit, made[:, part], refs)
                continue
            stays = lax.rem(step, 2) == core_ref[1 + bit]

            @pl.when(stays)
            def _():
                refs[1][...] = made[:, part]

            @pl.when(jnp.logical_not(stays))
            def _():
                refs[0][...] = made[:, part]

    on_either(
        core_ref,
        lambda: give(tn(a0[...], b0[0]) + tn(a1[...], b1[0])),
        lambda: give(tn(c[...], jnp.concatenate([d0[:VIS, :], d1[:VIS, :]], axis=0))),
    )


def down_grad(core, bits, factors, section, enc, dys):
    tile = lambda i: (0, i)
    zero = lambda i: (0, 0)
    dec = [(a, (a.shape[0], D), tile) for a in factors]
    dec += [(section, (1, S, D), lambda i, m=m: (m, 0, 0)) for m in (1, 0)]
    enc = [(enc, (enc.shape[0], D), tile)] + [(dy, dy.shape, zero) for dy in dys]
    rows = DOWN_ROWS // 2
    outs = []
    for bit in bits or (None, None):
        if bit == 2:
            outs.append((rows, (2 * PER, rows, D), lambda i: (i // 2, 0, 0)))
        else:
            outs.append((rows, (PER, rows, D), lambda i: (i, 0, 0)))
    return grad_call(down_grad_body, core, dec, enc, outs, bits, "down_grad")


def put_slab(core_ref, bits, ways, out_refs, step, made):
    made = made.astype(BF16).reshape(GROUPS, GROUP_ROWS, D)
    for part in range(2):

        @pl.when(step // 2 == part)
        def _():
            put(core_ref, bits[part], made, out_refs[part * ways : (part + 1) * ways])


def up_grad_body(bits, ways, core_ref, a0, a1, b0, b1, c, d, *out_refs):
    give = functools.partial(put_slab, core_ref, bits, ways, out_refs, pl.program_id(0))
    on_either(
        core_ref,
        lambda: give(tn(a0[...], b0[...]) + tn(a1[...], b1[...])),
        lambda: give(tn(c[...], d[...])),
    )


SLABS = (
    (2 * GROUP_ROWS, (GROUPS, GROUP_ROWS, D), lambda i: (0, jnp.minimum(i, 1), 0)),
    (2 * GROUP_ROWS, (GROUPS, GROUP_ROWS, D), lambda i: (0, jnp.maximum(i - 2, 0), 0)),
)


def up_grad(core, bits, factors, enc, enc_back):
    at = lambda place: (lambda i: (0, place))
    after = lambda place: (lambda i: (0, place + i))
    dec = [(a, (a.shape[0], D), at(DEC_H2)) for a in factors]
    dec += [(b, (b.shape[0], D), after(DEC_DPRE)) for b in factors]
    enc = [(enc, (enc.shape[0], D), at(ENC_H2)), (enc_back, (enc.shape[0], D), after(0))]
    return grad_call(up_grad_body, core, dec, enc, SLABS, bits, "up_grad")


def heads_grad_body(bits, ways, core_ref, a0, a1, b0, b1, c0, c1, s0, s1, d, e, small, *out_refs):
    step = pl.program_id(0)
    last = 2 * GROUP_ROWS

    def give(made):
        made = made.astype(BF16).reshape(GROUPS, GROUP_ROWS, D)
        for at in range(4):

            @pl.when(step == at)
            def _():
                part = at // 2
                rows = slice(at % 2 * GROUP_ROWS, (at % 2 + 1) * GROUP_ROWS)
                refs = out_refs[part * ways : (part + 1) * ways]
                if part == 0:
                    put(core_ref, bits[0], made, refs)
                else:
                    put(core_ref, bits[1], made, refs, rows)

    def dec():
        rights = [jnp.where(step == 3, c[...], b[...]) for b, c in ((b0, c0), (b1, c1))]
        give(tn(a0[...], rights[0]) + tn(a1[...], rights[1]))

    on_either(core_ref, dec, lambda: give(tn(d[...], e[...])))

    @pl.when(step == 3)
    def _():
        given = [s[VIS:, :].astype(F32) for s in (s0, s1)]
        extra = jnp.where(core_ref[0] == 0, small[...], given[0] + given[1]).astype(BF16)
        for out_ref in out_refs[ways:]:
            out_ref[:, last:, :] = jnp.broadcast_to(extra, (out_ref.shape[0], ROWS, D))


def heads_grad(core, bits, lates, dqkvs, backs, enc, enc_back, small):
    zero = lambda i: (0, 0)
    n, m = lates[0].shape[0], enc.shape[0]
    dec = [(a, (n, D), lambda i: (0, jnp.where(i < 3, LATE_H, LATE_ATT))) for a in lates]
    dec += [(b, (n, D), lambda i: (0, jnp.minimum(i, 2))) for b in dqkvs]
    dec += [(c, (n, D), lambda i: (0, LATE_DBRANCH)) for c in lates]
    dec += [(s, s.shape, zero) for s in backs]
    enc = [
        (enc, (m, D), lambda i: (0, jnp.where(i < 3, ENC_H, ENC_ATT))),
        (enc_back, (m, D), lambda i: (0, jnp.where(i < 3, ENC_DQKV + i, ENC_DBRANCH))),
        (small, small.shape, zero),
    ]
    rows = 2 * GROUP_ROWS + ROWS
    outs = (SLABS[0], (rows, (GROUPS, rows, D), lambda i: (0, 0, 0)))
    return grad_call(heads_grad_body, core, dec, enc, outs, bits, "heads_grad")


def swapped(value):
    return lax.ppermute(value, "pipe", [(0, 1), (1, 0)])


def across(value, bit):
    size = lax.axis_size("dp")
    return lax.ppermute(value, "dp", [(i, i ^ 2**bit) for i in range(size)])


def dp_bit(bit):
    return lax.rem(lax.axis_index("dp") // 2**bit, 2)


class Order:
    def __init__(self):
        self.last = None

    def __call__(self, step, *operands):
        if self.last is not None:
            operands, _ = lax.optimization_barrier((operands, self.last))
        made = step(*operands)
        self.last = jax.tree.leaves(made)[0]
        return made


class Sum:
    def __init__(self, arrays, order):
        go, self.stay = arrays
        self.value = None
        self.order = list(order)
        bit = self.order.pop(0)
        self.bits = [b for b in range(GROUPS.bit_length() - 2, -1, -1) if b != bit]
        self.got = across(go, bit)

    def step(self, run):
        if not self.order:
            self.value = run(
                lambda stay, got: (stay.astype(F32) + got.astype(F32))[0], self.stay, self.got
            )
            return
        bit = self.order.pop(0)
        shape = self.stay.shape
        at = self.bits.index(bit)
        self.bits.remove(bit)
        left = 2 ** len(self.bits)

        def half(which):
            def part(value):
                value = value.reshape(2**at, 2, left // 2**at, *shape[1:])
                chosen = lax.dynamic_index_in_dim(value, which, 1, keepdims=False)
                return chosen.reshape(left, *shape[1:]).astype(F32)

            return lambda stay, got: (part(stay) + part(got)).astype(BF16)

        mine = dp_bit(bit)
        go = run(half(1 - mine), self.stay, self.got)
        stay = run(half(mine), self.stay, self.got)
        self.got, self.stay = across(go, bit), stay


class PlainSum:
    def __init__(self, parts, slabs):
        whole = jnp.concatenate([part for (part,) in parts], axis=1)
        size = lax.axis_size("dp")
        rows = whole.shape[1] // slabs // ROWS * ROWS
        extra = whole[0, slabs * rows :] if slabs * rows < whole.shape[1] else None
        grad = whole[:, : slabs * rows].reshape(GROUPS, slabs, rows, D).transpose(0, 2, 1, 3)
        grad = grad.reshape(GROUPS * rows, slabs * D).astype(F32)
        mine = lax.psum_scatter(grad, "dp", scatter_dimension=0, tiled=True)
        mine = mine.reshape(-1, slabs, D).transpose(1, 0, 2).reshape(-1, D)
        if extra is not None:
            mine = jnp.concatenate([mine, lax.psum(extra.astype(F32), "dp")])
        self.value = mine

    def step(self, run):
        pass


ORDERS = {
    "down": ((2, 1, 0, 3), (1, 3, 0, 2)),
    "up": ((1, 2, 0, 3), (0, 1, 3, 2)),
    "heads": ((2, 0, 1, 3), (0, 1, 2, 3)),
}
EARLY_STEPS = ()
STEPS = (("down", 0), ("down", 1), ("down", 0), ("up", 1), ("up", 0), ("heads", 0), ("down", 0), ("heads", 1), ("up", 1), ("down", 0), ("up", 0), ("heads", 0), ("up", 0), ("heads", 1), ("down", 1), ("heads", 0), ("up", 1), ("heads", 1), ("down", 1), ("heads", 0), ("up", 1), ("up", 0), ("heads", 1), ("down", 1),)


def on_device(
    section_input,
    visible_slot,
    image_of_slot,
    qkv_weight,
    out_weight,
    up_weight,
    down_weight,
    norm_gain,
    up_bias,
    vectors,
):
    pipe = lax.axis_index("pipe")
    size = lax.axis_size("dp")
    halving = size == GROUPS
    core = jnp.stack([pipe] + [dp_bit(bit) for bit in range(GROUPS.bit_length() - 1)])
    own = [qkv_weight[0], out_weight[0], up_weight[0], down_weight[0]]
    params = [vectors.transpose(1, 0, 2), norm_gain, up_bias]
    layout = (visible_slot, image_of_slot)
    rows = MICRO * VIS
    run = Order()
    both = [[weight, swapped(weight)] for weight in own]

    enc_x, enc, enc_qkv, enc_lse, enc_mid, enc_slope, sent, packed = run(
        lambda section, first, *w: encoder_forward(rows, params, layout, section, w),
        section_input, both[1][1], *own,
    )
    other_sent, other_packed = swapped(sent), swapped(packed)
    x, dec, late, qkv, lse, dmid, datt, small = run(
        lambda sent, other_sent, packed, other_packed, *w: decoder(
            S, packed, other_packed, layout, sent, other_sent, section_input,
            [w[2 * i : 2 * i + 2] for i in range(4)],
        ),
        sent, other_sent, packed, other_packed, *[w for pair in both for w in pair],
    )
    other_dec = swapped(dec)
    dqkv, back = run(
        lambda *a: decoder_back(S, packed, other_packed, layout, *a, both[0]),
        qkv, datt, lse, small, x, dmid, late,
    )
    other_back = swapped(back)
    (late, dqkv), _ = lax.optimization_barrier(((late, dqkv), other_back))
    other_dqkv, other_late = swapped(dqkv), swapped(late)
    sums = {}

    def begin(name, parts, slabs):
        if halving:
            for i, (arrays, order) in enumerate(zip(parts, ORDERS[name])):
                sums[name, i] = Sum(arrays, order)
        else:
            sums[name, 0] = PlainSum(parts, slabs)

    def bits_of(name):
        return tuple(order[0] for order in ORDERS[name]) if halving else None

    parts = run(
        lambda *a: down_grad(core, bits_of("down"), a[:2], section_input[0], enc, a[2:]),
        dec, other_dec, back, other_back,
    )
    begin("down", parts, 1)
    enc_back, small, results = run(
        lambda dy, other_dy, *_: encoder_back(
            rows, params, layout, dy, other_dy, enc_lse, enc_slope, enc_mid, enc_qkv, enc_x, enc,
            own,
        ),
        back, other_back, other_dqkv, other_late,
    )
    parts = run(
        lambda *a: up_grad(core, bits_of("up"), a[:2], enc, a[2]), dec, other_dec, enc_back
    )
    begin("up", parts, 4)
    if halving:
        for name, i in EARLY_STEPS:
            sums[name, i].step(run)
    parts = run(
        lambda *a: heads_grad(core, bits_of("heads"), a[:2], a[2:4], a[4:6], enc, *a[6:]),
        late, other_late, dqkv, other_dqkv, back, other_back, enc_back, small,
    )
    begin("heads", parts, 4)
    results = run(lambda *a: place_results(core, *a), results, late, other_late)
    if halving:
        for name, i in STEPS:
            sums[name, i].step(run)
        waiting = [one for one in sums.values() if one.value is None]
        while waiting:
            for one in waiting:
                one.step(run)
            waiting = [one for one in waiting if one.value is None]

    def whole(name):
        values = [one.value for (kind, _), one in sums.items() if kind == name]
        return jnp.concatenate(values) if len(values) > 1 else values[0]

    down, up, heads = map(whole, ("down", "up", "heads"))
    width = D // size

    def wide(slabs):
        return jnp.concatenate(
            [slabs[i * width : (i + 1) * width] for i in range(slabs.shape[0] // width)], axis=1
        )

    small = heads[TILES * width :]
    heads = heads[: TILES * width]
    place = lax.axis_index("dp")
    mine = lax.dynamic_slice_in_dim(small, place * width, width, 1)
    hidden = FF // size
    bias_grad = lax.dynamic_slice_in_dim(
        small[UBIAS : UBIAS + TILES].reshape(FF), place * hidden, hidden, 0
    )
    return (
        results[None],
        wide(heads[: 3 * width])[None],
        heads[3 * width :][None],
        wide(up)[None],
        down[None],
        mine[GAIN1 : GAIN2 + 1][None],
        bias_grad[None],
        mine[:GAIN1][None],
    )


def solution(mesh):
    in_specs = (
        P("pipe", "dp", None, None),
        P("dp", None),
        P("dp", None),
        P("pipe", None, None),
        P("pipe", None, None),
        P("pipe", None, None),
        P("pipe", None, None),
        P("pipe", None, None),
        P("pipe", None),
        P("pipe", None, None),
    )
    out_specs = (
        P("pipe", "dp", None, None),
        P("pipe", "dp", None),
        P("pipe", "dp", None),
        P("pipe", "dp", None),
        P("pipe", "dp", None),
        P("pipe", None, "dp"),
        P("pipe", "dp"),
        P("pipe", None, "dp"),
    )
    return jax.shard_map(
        on_device, mesh=mesh, in_specs=in_specs, out_specs=out_specs, check_vma=False
    )
```

```python
import functools
import math

import jax
import jax.numpy as jnp
import numpy as np
from jax import lax
from jax.experimental import pallas as pl
from jax.experimental.pallas import tpu as pltpu
from jax.sharding import PartitionSpec as P

D = 768
H = 12
HD = 64
FF = 3072
S = 512
VIS = 128
MICRO = 2
EPSILON = 1e-06
PAIRS = H // 2
TWO = 2 * HD
TILES = FF // D
WIDE = 2 * D
LOADS = FF // WIDE
HALF = D // 2
GROUPS = 16
GROUP_ROWS = D // GROUPS
PER = GROUPS // TILES
DOWN_ROWS = FF // GROUPS
ROWS = 16
FAR = -1e30
F32 = jnp.float32
BF16 = jnp.bfloat16

SHIFT1, QBIAS, VBIAS, OBIAS, ENTRY, SHIFT2, DBIAS, GAIN1, GAIN2, UBIAS = range(10)


def contract(left, right, left_dim, right_dim):
    return lax.dot_general(
        left, right, (((left_dim,), (right_dim,)), ((), ())), preferred_element_type=F32
    )


def nn(left, right):
    return contract(left, right, 1, 0)


def nt(left, right):
    return contract(left, right, 1, 1)


def tn(left, right):
    return contract(left, right, 0, 0)


def unit_rows(rows):
    centered = rows - jnp.mean(rows, axis=-1, keepdims=True)
    scale = lax.rsqrt(jnp.mean(centered * centered, axis=-1, keepdims=True) + EPSILON)
    return centered * scale, scale


def unit_rows_back(grad, unit, scale, gain):
    scaled = grad * gain
    return scale * (
        scaled
        - jnp.mean(scaled, axis=-1, keepdims=True)
        - unit * jnp.mean(scaled * unit, axis=-1, keepdims=True)
    )


def in_head(shape, which):
    lane = lax.broadcasted_iota(jnp.int32, shape, 1)
    return lane < HD if which == 0 else lane >= HD


def one_head(pair, which):
    return jnp.where(in_head(pair.shape, which), pair, jnp.zeros_like(pair))


def colsum(rows):
    return jnp.sum(rows, axis=0, keepdims=True)


class Params:
    def __init__(self, core, refs):
        self.core, self.refs = core, refs

    def hidden(self, t):
        if len(self.refs) == 3:
            return self.refs[2][:, pl.ds(pl.multiple_of(t * WIDE, WIDE), WIDE)]
        each = WIDE // D
        return jnp.concatenate(
            [self.pick(pl.ds(UBIAS + t * each + part, 1)) for part in range(each)], axis=1
        )

    def __call__(self, index):
        at = slice(index, index + 1)
        if len(self.refs) < 3:
            return self.pick(at)
        if index < GAIN1:
            return self.refs[0][index]
        return self.refs[1][0, index - GAIN1 : index - GAIN1 + 1]

    def pick(self, at):
        return jnp.where(self.core == 0, self.refs[1][at], self.refs[0][at])


def upright(line):
    return jnp.broadcast_to(line, (8, line.shape[1])).T[:, :1]


def hits(slots):
    return lax.broadcasted_iota(jnp.int32, (VIS, S), 0).astype(F32) == slots


def hits_upright(slots):
    return lax.broadcasted_iota(jnp.int32, (S, VIS), 1).astype(F32) == slots


def marks(groups, count):
    lane = lax.broadcasted_iota(jnp.int32, (groups.shape[0], TWO), 1)
    lane = jnp.where(lane < HD, lane, lane - HD).astype(F32)
    same = lane == groups
    key_fill = jnp.where(same, 1.0, 0.0).astype(BF16)
    query_fill = jnp.where(jnp.logical_or(same, lane >= count), 0.0, FAR).astype(BF16)
    return key_fill, query_fill


class Weight:
    def __init__(self, core, refs, dst, sems, cuts):
        self.core, self.refs, self.dst, self.sems, self.cuts = core, refs, dst, sems, cuts

    def start(self, i):
        cut = self.cuts[i]

        def go(ref):
            pltpu.make_async_copy(ref.at[cut], self.dst.at[cut], self.sems.at[i]).start()

        if len(self.refs) == 1:
            go(self.refs[0])
        else:
            pl.when(self.core == 0)(lambda: go(self.refs[1]))
            pl.when(self.core != 0)(lambda: go(self.refs[0]))

    def get(self, i):
        cut = self.cuts[i]
        pltpu.make_async_copy(self.refs[0].at[cut], self.dst.at[cut], self.sems.at[i]).wait()
        return self.dst[cut]


    def take(self, i, cut):
        pltpu.make_async_copy(self.refs[0].at[cut], self.dst.at[cut], self.sems.at[i]).wait()
        return self.dst[cut]


class Either:
    def __init__(self, core, on_first, on_second, dst, sem):
        self.copy = pltpu.make_async_copy(on_first, dst, sem)
        self.dst = dst
        pl.when(core == 0)(self.copy.start)
        pl.when(core != 0)(lambda: pltpu.make_async_copy(on_second, dst, sem).start())

    def get(self):
        self.copy.wait()
        return self.dst[...]


class Out:
    def __init__(self, sems):
        self.sems, self.count, self.going = sems, 0, []

    def send(self, src, dst):
        copy = pltpu.make_async_copy(src, dst, self.sems.at[self.count])
        self.count += 1
        copy.start()
        self.going.append(copy)

    def wait(self):
        for copy in self.going:
            copy.wait()


SMEM, VMEM, HBM = pltpu.SMEM, pltpu.VMEM, pl.ANY


def struct(shape, dtype):
    return jax.ShapeDtypeStruct(shape, dtype)


def size_of(shape):
    return math.prod(shape.shape) * shape.dtype.itemsize


def call(body, ins, outs, scratch, name, flops):
    arrays = [array for array, _ in ins]
    shapes = [shape for shape, _ in outs]
    return pl.pallas_call(
        body,
        in_specs=[pl.BlockSpec(memory_space=space) for _, space in ins],
        out_specs=[pl.BlockSpec(memory_space=space) for _, space in outs],
        out_shape=shapes,
        scratch_shapes=scratch,
        compiler_params=pltpu.CompilerParams(vmem_limit_bytes=60 * 2**20),
        cost_estimate=pl.CostEstimate(flops=1, bytes_accessed=1, transcendentals=0),
        name=name,
    )(*arrays)


def taker(refs):
    refs = list(refs)

    def take(count):
        return [refs.pop(0) for _ in range(count)]

    return take


def columns(i):
    return (slice(None), slice(i * D, (i + 1) * D))


def positions():
    width = D // 2
    frequency = np.exp(np.arange(width) * (-math.log(10000.0) / width))
    angles = np.arange(S)[:, None] * frequency[None, :]
    return jnp.asarray(np.concatenate([np.sin(angles), np.cos(angles)], axis=1), F32)


def section(i):
    return columns(i)


def group_columns(core, decoder, slots_ref, images_ref):
    if decoder:
        return upright(images_ref[pl.ds(core, 1), :].astype(F32)), 2
    parts = []
    for micro in range(MICRO):
        hit = hits(slots_ref[micro : micro + 1, :].astype(F32))
        mark = images_ref[micro : micro + 1, :].astype(F32) + 1.0
        parts.append(jnp.sum(jnp.where(hit, mark, 0.0), axis=1, keepdims=True) + 3.0 * micro)
    return jnp.concatenate(parts, axis=0), 3 * MICRO


def project(params, weight, x_s, h_s, qkv_s, out, h_out, qkv_out):
    unit, _scale = unit_rows(x_s[...])
    h = (unit * params(GAIN1) + params(SHIFT1)).astype(BF16)
    h_s[...] = h
    out.send(h_s, h_out)
    for part, bias in enumerate((QBIAS, None, VBIAS)):
        made = nn(h, weight.get(part))
        if bias is not None:
            made = made + params(bias)
        qkv_s[part] = made.astype(BF16)
        out.send(qkv_s.at[part], qkv_out.at[part])


def attend(n, together, fills, qkv_s, att_s, lse_ref):
    key_fill, query_fill = fills
    scaling = jnp.asarray(HD**-0.5, BF16)

    def pairs(step, _):
        lanes = [
            pl.ds(pl.multiple_of((step * together + i) * TWO, TWO), TWO) for i in range(together)
        ]
        heads = [(i, which) for i in range(together) for which in range(2)]
        qs = [qkv_s[0, :, at] * scaling for at in lanes]
        ks = [qkv_s[1, :, at] for at in lanes]
        vs = [qkv_s[2, :, at].T for at in lanes]
        scores = [
            nt(
                jnp.where(in_head((n, TWO), which), ks[i], key_fill),
                jnp.where(in_head((n, TWO), which), qs[i], query_fill),
            )
            for i, which in heads
        ]
        tops = [jnp.max(score, axis=0, keepdims=True) for score in scores]
        raised = [jnp.exp(score - top) for score, top in zip(scores, tops)]
        totals = [colsum(part) for part in raised]
        found = [
            nn(vs[i][which * HD : (which + 1) * HD, :], part.astype(BF16)) * (1.0 / total)
            for (i, which), part, total in zip(heads, raised, totals)
        ]
        for i in range(together):
            att_s[:, lanes[i]] = jnp.concatenate(found[2 * i : 2 * i + 2], axis=0).T.astype(BF16)
            lse_ref[step * together + i] = jnp.concatenate(
                [tops[at] + jnp.log(totals[at]) for at in (2 * i, 2 * i + 1)], axis=0
            )
        return 0

    lax.fori_loop(0, PAIRS // together, pairs, 0)


def feed(params, weights, x_s, att_s, mid_s, h2_s, act_s, slope_s, sum_s, out, h2_out, act_out):
    out_weight, up, down = weights
    mid = x_s[...] + nn(att_s[...], out_weight.get(0)) + params(OBIAS)
    mid_s[...] = mid
    unit, _scale = unit_rows(mid)
    h2 = (unit * params(GAIN2) + params(SHIFT2)).astype(BF16)
    h2_s[...] = h2
    out.send(h2_s, h2_out)
    sum_s[...] = mid + params(DBIAS)

    def tile(t, _):
        at = (slice(None), pl.ds(pl.multiple_of(t * WIDE, WIDE), WIDE))
        pre = nn(h2_s[...], up.take(t, at)) + params.hidden(t)
        below = 0.5 + 0.5 * lax.erf(pre * math.sqrt(0.5))
        act = (pre * below).astype(BF16)
        act_s[at] = act
        density = jnp.exp(-0.5 * pre * pre) * (1.0 / math.sqrt(2.0 * math.pi))
        slope_s[at] = (below + pre * density).astype(BF16)
        sum_s[...] += nn(act, down.take(t, (at[1], slice(None))))
        return 0

    lax.fori_loop(0, LOADS, tile, 0)
    out.send(act_s, act_out)


def feed_back(
    params, weights, dff, dff_ref, slope, mid, dpre_s, dh2_s, small_ref, out, dpre_out, width
):
    out_weight, up, down = weights
    small_ref[...] = jnp.zeros_like(small_ref)
    small_ref[DBIAS : DBIAS + 1, :] = colsum(dff.astype(F32))
    if dff_ref is not None:
        dff_ref[...] = dff
    dh2_s[...] = jnp.zeros_like(dh2_s)

    def tile(t, _):
        at = (slice(None), pl.ds(pl.multiple_of(t * width, width), width))
        dact = nt(dff_ref[...], down(t, (at[1], slice(None))))
        dpre = (dact * slope(t, at).astype(F32)).astype(BF16)
        dpre_s[at] = dpre
        sums = colsum(dpre.astype(F32))
        for part in range(width // D):
            small_ref[pl.ds(UBIAS + t * (width // D) + part, 1), :] = sums[columns(part)]
        dh2_s[...] += nt(dpre, up(t, at))
        return 0

    lax.fori_loop(0, FF // width, tile, 0)
    out.send(dpre_s, dpre_out)
    dh2 = dh2_s[...]
    unit, scale = unit_rows(mid())
    small_ref[GAIN2 : GAIN2 + 1, :] = colsum(dh2 * unit)
    small_ref[SHIFT2 : SHIFT2 + 1, :] = colsum(dh2)
    dmid = dff.astype(F32) + unit_rows_back(dh2, unit, scale, params(GAIN2))
    dbranch = dmid.astype(BF16)
    small_ref[OBIAS : OBIAS + 1, :] = colsum(dbranch.astype(F32))
    return dmid, dbranch, nt(dbranch, out_weight()).astype(BF16)


def attend_back(n, together, fills, qkv_ref, att_ref, datt_ref, lse_ref, dqkv_ref):
    key_fill, query_fill = fills
    scaling = jnp.asarray(HD**-0.5, BF16)

    def pairs(step, _):
        lanes = [
            pl.ds(pl.multiple_of((step * together + i) * TWO, TWO), TWO) for i in range(together)
        ]
        heads = [(i, which) for i in range(together) for which in range(2)]
        qs = [qkv_ref[0, :, at] * scaling for at in lanes]
        ks = [qkv_ref[1, :, at] for at in lanes]
        vs = [qkv_ref[2, :, at] for at in lanes]
        turned = [k.T for k in ks]
        dos = [datt_ref[:, at] for at in lanes]
        mine = [one_head(dos[i], which) for i, which in heads]
        along = [
            (att_ref[:, at].astype(F32) * do.astype(F32)).T for at, do in zip(lanes, dos)
        ]
        scores = [
            nt(
                jnp.where(in_head((n, TWO), which), ks[i], key_fill),
                jnp.where(in_head((n, TWO), which), qs[i], query_fill),
            )
            for i, which in heads
        ]
        dprobs = [nt(vs[i], do) for (i, which), do in zip(heads, mine)]
        probs = [
            jnp.exp(score - lse_ref[step * together + i, which : which + 1, :])
            for (i, which), score in zip(heads, scores)
        ]
        dscores = [
            (prob * (dprob - colsum(along[i][which * HD : (which + 1) * HD, :]))).astype(BF16)
            for (i, which), prob, dprob in zip(heads, probs, dprobs)
        ]
        for i in range(together):
            a, b = 2 * i, 2 * i + 1
            dv = nn(probs[a].astype(BF16), mine[a]) + nn(probs[b].astype(BF16), mine[b])
            dk = nn(dscores[a], one_head(qs[i], 0)) + nn(dscores[b], one_head(qs[i], 1))
            dq = jnp.concatenate(
                [nn(turned[i][:HD, :], dscores[a]), nn(turned[i][HD:, :], dscores[b])], axis=0
            )
            dqkv_ref[:, pl.ds(0 * D + lanes[i].start, TWO)] = (dq * HD**-0.5).T.astype(BF16)
            dqkv_ref[:, pl.ds(1 * D + lanes[i].start, TWO)] = dk.astype(BF16)
            dqkv_ref[:, pl.ds(2 * D + lanes[i].start, TWO)] = dv.astype(BF16)
        return 0

    lax.fori_loop(0, PAIRS // together, pairs, 0)


def project_back(params, weight, dqkv_ref, x, dmid, small_ref):
    dh = 0.0
    for part in range(3):
        made = dqkv_ref[columns(part)]
        if part != 1:
            bias = QBIAS if part == 0 else VBIAS
            small_ref[bias : bias + 1, :] = colsum(made.astype(F32))
        dh = dh + nt(made, weight.get(part))
    unit, scale = unit_rows(x())
    small_ref[GAIN1 : GAIN1 + 1, :] = colsum(dh * unit)
    small_ref[SHIFT1 : SHIFT1 + 1, :] = colsum(dh)
    return dmid() + unit_rows_back(dh, unit, scale, params(GAIN1))


EVERYTHING = (slice(None), slice(None))


def qkv_loads(core, refs, dst, sems):
    return Weight(core, refs, dst, sems, [columns(part) for part in range(3)])


def feed_loads(core, w_out, w_up, w_down, dsts, sems, width):
    parts = [slice(i, i + width) for i in range(0, FF, width)]
    return (
        Weight(core, w_out, dsts[0], sems[0], [EVERYTHING]),
        Weight(core, w_up, dsts[1], sems[1], [(slice(None), part) for part in parts]),
        Weight(core, w_down, dsts[2], sems[2], [(part, slice(None)) for part in parts]),
    )


def dma(count):
    return pltpu.SemaphoreType.DMA((count,))


FEED_SCRATCH = [VMEM((D, D), BF16), VMEM((D, FF), BF16), VMEM((FF, D), BF16)]
FEED_SEMS = [dma(1), dma(LOADS), dma(LOADS)]
QKV_SCRATCH = [VMEM((D, 3 * D), BF16), dma(3)]


DEC_DPRE, DEC_H2, DEC_SECTIONS = TILES, 2 * TILES, 2 * TILES + 1
LATE_H, LATE_ATT, LATE_DBRANCH, LATE_OUT, LATE_SECTIONS = range(5)
ENC_H, ENC_H2, ENC_ATT, ENC_SECTIONS = range(TILES, TILES + 4)
ENC_DBRANCH, ENC_DQKV, ENC_BACK_SECTIONS = TILES, TILES + 1, TILES + 4


def sections(first, count):
    return (slice(None), slice(first * D, (first + count) * D))


def encoder_forward_body(n, *refs):
    take = taker(refs)
    given = take(3)
    core = lax.axis_index("pipe")
    params = Params(core, given)
    slots_ref, images_ref, section_ref = take(3)
    w_qkv, w_out, w_up, w_down = take(1), take(1), take(1), take(1)
    x_out, factors_out, qkv_out, lse_ref, mid_out, slope_out, sent_ref, params_ref = take(8)
    x_s, h_s, qkv_s, att_s, mid_s, h2_s, act_s, slope_s, sum_s = take(9)
    wq_s, wq_sems = take(2)
    dsts, sems = take(3), take(3)
    (out_sems,) = take(1)
    for i in range(GAIN1):
        params_ref[i : i + 1, :] = given[0][i]
    params_ref[GAIN1:UBIAS, :] = given[1][0]
    for t in range(TILES):
        params_ref[UBIAS + t : UBIAS + t + 1, :] = given[2][columns(t)]

    @pl.when(core != 0)
    def _():
        sent_ref[n:, :] = section_ref[0, 0]

    @pl.when(core == 0)
    def _():
        weight = qkv_loads(core, w_qkv, wq_s, wq_sems)
        weights = feed_loads(core, w_out, w_up, w_down, dsts, sems, WIDE)
        for part in range(3):
            weight.start(part)
        weights[0].start(0)
        for t in range(LOADS):
            weights[1].start(t)
            weights[2].start(t)
        out = Out(out_sems)
        for micro in range(MICRO):
            hit = hits(slots_ref[micro : micro + 1, :].astype(F32))
            x_s[micro * VIS : (micro + 1) * VIS, :] = nn(
                hit.astype(BF16), section_ref[0, micro]
            ) + params(ENTRY)
        out.send(x_s, x_out)
        project(params, weight, x_s, h_s, qkv_s, out, factors_out.at[section(ENC_H)], qkv_out)
        fills = marks(*group_columns(core, False, slots_ref, images_ref))
        attend(n, 3, fills, qkv_s, att_s, lse_ref)
        out.send(att_s, factors_out.at[section(ENC_ATT)])
        feed(
            params, weights, x_s, att_s, mid_s, h2_s, act_s, slope_s, sum_s, out,
            factors_out.at[section(ENC_H2)], factors_out.at[sections(0, TILES)],
        )
        out.send(mid_s, mid_out)
        out.send(slope_s, slope_out)
        sent_ref[:n, :] = sum_s[...].astype(BF16)
        out.wait()


def encoder_forward(n, params, layout, section, weights):
    ins = [(a, VMEM) for a in (*params, *layout, section)]
    ins += [(w, HBM) for w in weights]
    outs = [
        (struct((n, D), F32), HBM),
        (struct((n, ENC_SECTIONS * D), BF16), HBM),
        (struct((3, n, D), BF16), HBM),
        (struct((PAIRS, 2, n), F32), VMEM),
        (struct((n, D), F32), HBM),
        (struct((n, FF), BF16), HBM),
        (struct((n + S, D), BF16), VMEM),
        (struct((ROWS, D), F32), VMEM),
    ]
    scratch = [
        VMEM((n, D), F32),
        VMEM((n, D), BF16),
        VMEM((3, n, D), BF16),
        VMEM((n, D), BF16),
        VMEM((n, D), F32),
        VMEM((n, D), BF16),
        VMEM((n, FF), BF16),
        VMEM((n, FF), BF16),
        VMEM((n, D), F32),
        *QKV_SCRATCH,
        *FEED_SCRATCH,
        *FEED_SEMS,
        dma(10),
    ]
    return call(
        functools.partial(encoder_forward_body, n),
        ins,
        outs,
        scratch,
        "encoder_forward",
        2 * n * (4 * D * D + 2 * D * FF),
    )


def decoder_body(n, *refs):
    take = taker(refs)
    core = lax.axis_index("pipe")
    params = Params(core, take(2))
    slots_ref, images_ref, pos_ref, sent_ref, other_sent_ref, section_ref = take(6)
    w_qkv, w_out, w_up, w_down = take(2), take(2), take(2), take(2)
    x_out, factors_out, late_out, qkv_out, lse_ref, dmid_ref, datt_ref, small_ref = take(8)
    x_s, h_s, qkv_s, att_s, mid_s, h2_s, act_s, slope_s, sum_s, dpre_s, dff_s = take(11)
    dbranch_s, decoded_s = take(2)
    wq_s, wq_sems = take(2)
    dsts, sems = take(3), take(3)
    out_sems, in_sems = take(2)
    rows = MICRO * VIS
    weight = qkv_loads(core, w_qkv, wq_s, wq_sems)
    weights = feed_loads(core, w_out, w_up, w_down, dsts, sems, WIDE)
    for part in range(3):
        weight.start(part)
    weights[0].start(0)
    for t in range(LOADS):
        weights[1].start(t)
        weights[2].start(t)
    dff = Either(core, other_sent_ref.at[rows:], section_ref.at[0, 1], dff_s, in_sems.at[0])
    out = Out(out_sems)
    slots = upright(slots_ref[pl.ds(core, 1), :].astype(F32))
    sent = jnp.where(core == 0, sent_ref[:VIS, :], other_sent_ref[rows - VIS : rows, :])
    x = nn(hits_upright(slots).astype(BF16), sent) + pos_ref[...]
    x_s[...] = x + jnp.where(slots == VIS, params(ENTRY), 0.0)
    out.send(x_s, x_out)
    project(params, weight, x_s, h_s, qkv_s, out, late_out.at[section(LATE_H)], qkv_out)
    fills = marks(*group_columns(core, True, slots_ref, images_ref))
    attend(n, 2, fills, qkv_s, att_s, lse_ref)
    out.send(att_s, late_out.at[section(LATE_ATT)])
    feed(
        params, weights, x_s, att_s, mid_s, h2_s, act_s, slope_s, sum_s, out,
        factors_out.at[section(DEC_H2)], factors_out.at[sections(0, TILES)],
    )
    decoded_s[...] = sum_s[...].astype(BF16)
    out.send(decoded_s, late_out.at[section(LATE_OUT)])
    dmid_ref[...], dbranch_s[...], datt_ref[...] = feed_back(
        params,
        (
            lambda: weights[0].dst[...],
            lambda t, at: weights[1].dst[at],
            lambda t, at: weights[2].dst[at],
        ),
        dff.get(),
        dff_s,
        lambda t, at: slope_s[at],
        lambda: mid_s[...],
        dpre_s,
        sum_s,
        small_ref,
        out,
        factors_out.at[sections(DEC_DPRE, TILES)],
        WIDE,
    )
    out.send(dbranch_s, late_out.at[section(LATE_DBRANCH)])
    out.wait()


def decoder(n, params, other_params, layout, sent, other_sent, section, weights):
    ins = [(a, VMEM) for a in (params, other_params, *layout, positions())]
    ins += [(sent, VMEM), (other_sent, VMEM), (section, HBM)]
    ins += [(w, HBM) for pair in weights for w in pair]
    outs = [
        (struct((n, D), F32), HBM),
        (struct((n, DEC_SECTIONS * D), BF16), HBM),
        (struct((n, LATE_SECTIONS * D), BF16), HBM),
        (struct((3, n, D), BF16), HBM),
        (struct((PAIRS, 2, n), F32), VMEM),
        (struct((n, D), F32), VMEM),
        (struct((n, D), BF16), VMEM),
        (struct((ROWS, D), F32), VMEM),
    ]
    scratch = [
        VMEM((n, D), F32),
        VMEM((n, D), BF16),
        VMEM((3, n, D), BF16),
        VMEM((n, D), BF16),
        VMEM((n, D), F32),
        VMEM((n, D), BF16),
        VMEM((n, FF), BF16),
        VMEM((n, FF), BF16),
        VMEM((n, D), F32),
        VMEM((n, FF), BF16),
        VMEM((n, D), BF16),
        VMEM((n, D), BF16),
        VMEM((n, D), BF16),
        *QKV_SCRATCH,
        *FEED_SCRATCH,
        *FEED_SEMS,
        dma(12),
        dma(1),
    ]
    return call(
        functools.partial(decoder_body, n),
        ins,
        outs,
        scratch,
        "decoder",
        2 * n * (5 * D * D + 4 * D * FF) + 4 * n * n * D,
    )


def decoder_back_body(n, *refs):
    take = taker(refs)
    core = lax.axis_index("pipe")
    params = Params(core, take(2))
    slots_ref, images_ref, qkv_ref, datt_ref, lse_ref, small_in = take(6)
    x_in, dmid_in, factors_in = take(3)
    w_qkv = take(2)
    dqkv_out, back_ref = take(2)
    dqkv_s, x_s, dmid_s, att_s, small_s, wq_s, wq_sems, in_sems, out_sems = take(9)
    att = pltpu.make_async_copy(factors_in.at[section(LATE_ATT)], att_s, in_sems.at[2])
    att.start()
    weight = qkv_loads(core, w_qkv, wq_s, wq_sems)
    x = Weight(core, [x_in], x_s, in_sems, [EVERYTHING])
    dmid = Weight(core, [dmid_in], dmid_s, in_sems.at[pl.ds(1, 1)], [EVERYTHING])
    for part in range(3):
        weight.start(part)
    x.start(0)
    dmid.start(0)
    fills = marks(*group_columns(core, True, slots_ref, images_ref))
    att.wait()
    attend_back(n, 1, fills, qkv_ref, att_s, datt_ref, lse_ref, dqkv_s)
    out = Out(out_sems)
    out.send(dqkv_s, dqkv_out)
    small_s[...] = small_in[...]
    dx = project_back(
        params, weight, dqkv_s, lambda: x.get(0), lambda: dmid.get(0), small_s
    )
    slots = slots_ref[pl.ds(core, 1), :].astype(F32)
    small_s[ENTRY : ENTRY + 1, :] = colsum(jnp.where(upright(slots) == VIS, dx, 0.0))
    back_ref[:VIS, :] = nn(hits(slots).astype(BF16), dx.astype(BF16)).astype(BF16)
    back_ref[VIS:, :] = small_s[...].astype(BF16)
    out.wait()


def decoder_back(
    n, params, other_params, layout, qkv, datt, lse, small, x, dmid, factors, w_qkv
):
    ins = [(a, VMEM) for a in (params, other_params, *layout)]
    ins += [(a, VMEM) for a in (qkv, datt, lse, small)]
    ins += [(a, HBM) for a in (x, dmid, factors, *w_qkv)]
    outs = [
        (struct((n, 3 * D), BF16), HBM),
        (struct((VIS + ROWS, D), BF16), VMEM),
    ]
    scratch = [
        VMEM((n, 3 * D), BF16),
        VMEM((n, D), F32),
        VMEM((n, D), F32),
        VMEM((n, D), BF16),
        VMEM((ROWS, D), F32),
        *QKV_SCRATCH,
        dma(3),
        dma(1),
    ]
    return call(
        functools.partial(decoder_back_body, n),
        ins,
        outs,
        scratch,
        "decoder_back",
        2 * n * D * 3 * D + 10 * n * n * D,
    )


def encoder_back_body(n, *refs):
    take = taker(refs)
    core = lax.axis_index("pipe")
    params = Params(core, take(3))
    slots_ref, images_ref, dy_ref, other_dy_ref, lse_ref = take(5)
    slope_in, mid_in, qkv_in, x_in, enc_in = take(5)
    w_qkv, w_out, w_up, w_down = take(1), take(1), take(1), take(1)
    factors_out, small_ref, results_out = take(3)
    slope_s, mid_s, qkv_s, x_s, att_s, dpre_s, dh2_s, dbranch_s, datt_s, dqkv_s, back_s = take(11)
    wq_s, wq_sems = take(2)
    dsts, sems = take(3), take(3)
    in_sems, out_sems = take(2)

    @pl.when(core == 0)
    def _():
        weight = qkv_loads(core, w_qkv, wq_s, wq_sems)
        weights = feed_loads(core, w_out, w_up, w_down, dsts, sems, D)
        out_weight, up, down = weights
        slope = Weight(core, [slope_in], slope_s, in_sems, [columns(t) for t in range(TILES)])
        mid = Weight(core, [mid_in], mid_s, in_sems.at[pl.ds(TILES, 1)], [EVERYTHING])
        qkv = Weight(
            core, [qkv_in], qkv_s, in_sems.at[pl.ds(TILES + 1, 1)], [(slice(None),) * 3]
        )
        x = Weight(core, [x_in], x_s, in_sems.at[pl.ds(TILES + 2, 1)], [EVERYTHING])
        att = pltpu.make_async_copy(
            enc_in.at[section(ENC_ATT)], att_s, in_sems.at[TILES + 3]
        )
        for t in range(TILES):
            down.start(t)
            slope.start(t)
            up.start(t)
        mid.start(0)
        out_weight.start(0)
        qkv.start(0)
        att.start()
        for part in range(3):
            weight.start(part)
        x.start(0)
        out = Out(out_sems)
        dff = jnp.concatenate([dy_ref[:VIS, :], other_dy_ref[:VIS, :]], axis=0)
        dmid, dbranch, datt = feed_back(
            params, (lambda: out_weight.get(0), up.take, down.take), dff, datt_s, slope.take,
            lambda: mid.get(0), dpre_s, dh2_s, small_ref, out,
            factors_out.at[sections(0, TILES)], D,
        )
        dh2_s[...] = dmid
        dbranch_s[...] = dbranch
        out.send(dbranch_s, factors_out.at[section(ENC_DBRANCH)])
        datt_s[...] = datt
        fills = marks(*group_columns(core, False, slots_ref, images_ref))
        qkv.get(0)
        att.wait()
        attend_back(n, 2, fills, qkv_s, att_s, datt_s, lse_ref, dqkv_s)
        out.send(dqkv_s, factors_out.at[sections(ENC_DQKV, 3)])
        dx = project_back(params, weight, dqkv_s, lambda: x.get(0), lambda: dh2_s[...], small_ref)
        low = dx.astype(BF16)
        small_ref[ENTRY : ENTRY + 1, :] = colsum(dx)
        for micro in range(MICRO):
            slots = upright(slots_ref[micro : micro + 1, :].astype(F32))
            back_s[micro] = nn(
                hits_upright(slots).astype(BF16), low[micro * VIS : (micro + 1) * VIS, :]
            ).astype(BF16)
        out.send(back_s, results_out)
        out.wait()


def encoder_back(
    n, params, layout, dy, other_dy, lse, slope, mid, qkv, x, enc, weights
):
    ins = [(a, VMEM) for a in (*params, *layout, dy, other_dy, lse)]
    ins += [(a, HBM) for a in (slope, mid, qkv, x, enc, *weights)]
    outs = [
        (struct((n, ENC_BACK_SECTIONS * D), BF16), HBM),
        (struct((ROWS, D), F32), VMEM),
        (struct((MICRO, S, D), BF16), HBM),
    ]
    scratch = [
        VMEM((n, FF), BF16),
        VMEM((n, D), F32),
        VMEM((3, n, D), BF16),
        VMEM((n, D), F32),
        VMEM((n, D), BF16),
        VMEM((n, FF), BF16),
        VMEM((n, D), F32),
        VMEM((n, D), BF16),
        VMEM((n, D), BF16),
        VMEM((n, 3 * D), BF16),
        VMEM((MICRO, S, D), BF16),
        *QKV_SCRATCH,
        *FEED_SCRATCH,
        dma(1),
        dma(TILES),
        dma(TILES),
        dma(TILES + 4),
        dma(4),
    ]
    return call(
        functools.partial(encoder_back_body, n),
        ins,
        outs,
        scratch,
        "encoder_back",
        2 * n * (4 * D * D + 2 * D * FF),
    )


def place_body(core_ref, _, dec_in, other_dec_in, results_out, back_s, in_sems, out_sems):
    @pl.when(core_ref[0] != 0)
    def _():
        parts = [
            pltpu.make_async_copy(ref.at[section(LATE_OUT)], back_s.at[at], in_sems.at[at])
            for at, ref in enumerate((other_dec_in, dec_in))
        ]
        out = Out(out_sems)
        for part in parts:
            part.start()
        for at, part in enumerate(parts):
            part.wait()
            out.send(back_s.at[at], results_out.at[at])
        out.wait()


def place_results(core, results, dec, other_dec):
    return pl.pallas_call(
        place_body,
        in_specs=[pl.BlockSpec(memory_space=SMEM)] + [pl.BlockSpec(memory_space=HBM)] * 3,
        out_specs=pl.BlockSpec(memory_space=HBM),
        out_shape=struct(results.shape, BF16),
        scratch_shapes=[VMEM((MICRO, S, D), BF16), dma(2), dma(2)],
        input_output_aliases={1: 0},
        name="place_results",
    )(core, results, dec, other_dec)


def put(core_ref, bit, made, out_refs, at=slice(None)):
    if bit is None:
        out_refs[0][:, at, :] = made
        return
    groups, rows, width = made.shape
    made = made.reshape(groups // 2 ** (bit + 1), 2, 2**bit, rows, width)
    mine = core_ref[1 + bit]
    low, high = made[:, 0], made[:, 1]
    for out_ref, other in zip(out_refs, (True, False)):
        chosen = jnp.where((mine == 0) != other, low, high)
        out_ref[:, at, :] = chosen.reshape(groups // 2, rows, width)


def grad_call(body, core, dec, enc, outs, bits, name):
    def only(wanted, index):
        def place(i, core):
            return tuple(jnp.where(core[0] == wanted, at, 0) for at in index(i))

        return place

    specs = [pl.BlockSpec(block, only(1, index)) for _, block, index in dec]
    specs += [pl.BlockSpec(block, only(0, index)) for _, block, index in enc]
    arrays = [a for a, _, _ in (*dec, *enc)]
    ways = 1 if bits is None else 2
    out_specs, shapes = [], []
    for rows, block, index in outs:
        spec = pl.BlockSpec((block[0] // ways, *block[1:]), lambda i, core, index=index: index(i))
        out_specs += [spec] * ways
        shapes += [struct((GROUPS // ways, rows, D), BF16)] * ways
    made = pl.pallas_call(
        functools.partial(body, bits or (None, None), ways),
        grid_spec=pltpu.PrefetchScalarGridSpec(
            num_scalar_prefetch=1, grid=(TILES,), in_specs=specs, out_specs=out_specs
        ),
        out_shape=shapes,
        compiler_params=pltpu.CompilerParams(
            vmem_limit_bytes=60 * 2**20, dimension_semantics=("arbitrary",)
        ),
        cost_estimate=pl.CostEstimate(flops=1, bytes_accessed=1, transcendentals=0),
        name=name,
    )(core, *arrays)
    return made[:ways], made[ways:]


def on_either(core_ref, dec, enc):
    pl.when(core_ref[0] != 0)(dec)
    pl.when(core_ref[0] == 0)(enc)


def down_grad_body(bits, ways, core_ref, a0, a1, b0, b1, c, d0, d1, *out_refs):
    step = pl.program_id(0)

    def give(made):
        made = made.astype(BF16).reshape(PER, 2, DOWN_ROWS // 2, D)
        for part, bit in enumerate(bits):
            refs = out_refs[part * ways : (part + 1) * ways]
            if bit != 2:
                put(core_ref, bit, made[:, part], refs)
                continue
            stays = lax.rem(step, 2) == core_ref[1 + bit]

            @pl.when(stays)
            def _():
                refs[1][...] = made[:, part]

            @pl.when(jnp.logical_not(stays))
            def _():
                refs[0][...] = made[:, part]

    on_either(
        core_ref,
        lambda: give(tn(a0[...], b0[0]) + tn(a1[...], b1[0])),
        lambda: give(tn(c[...], jnp.concatenate([d0[:VIS, :], d1[:VIS, :]], axis=0))),
    )


def down_grad(core, bits, factors, section, enc, dys):
    tile = lambda i: (0, i)
    zero = lambda i: (0, 0)
    dec = [(a, (a.shape[0], D), tile) for a in factors]
    dec += [(section, (1, S, D), lambda i, m=m: (m, 0, 0)) for m in (1, 0)]
    enc = [(enc, (enc.shape[0], D), tile)] + [(dy, dy.shape, zero) for dy in dys]
    rows = DOWN_ROWS // 2
    outs = []
    for bit in bits or (None, None):
        if bit == 2:
            outs.append((rows, (2 * PER, rows, D), lambda i: (i // 2, 0, 0)))
        else:
            outs.append((rows, (PER, rows, D), lambda i: (i, 0, 0)))
    return grad_call(down_grad_body, core, dec, enc, outs, bits, "down_grad")


def put_slab(core_ref, bits, ways, out_refs, step, made):
    made = made.astype(BF16).reshape(GROUPS, GROUP_ROWS, D)
    for part in range(2):

        @pl.when(step // 2 == part)
        def _():
            put(core_ref, bits[part], made, out_refs[part * ways : (part + 1) * ways])


def up_grad_body(bits, ways, core_ref, a0, a1, b0, b1, c, d, *out_refs):
    give = functools.partial(put_slab, core_ref, bits, ways, out_refs, pl.program_id(0))
    on_either(
        core_ref,
        lambda: give(tn(a0[...], b0[...]) + tn(a1[...], b1[...])),
        lambda: give(tn(c[...], d[...])),
    )


SLABS = (
    (2 * GROUP_ROWS, (GROUPS, GROUP_ROWS, D), lambda i: (0, jnp.minimum(i, 1), 0)),
    (2 * GROUP_ROWS, (GROUPS, GROUP_ROWS, D), lambda i: (0, jnp.maximum(i - 2, 0), 0)),
)


def up_grad(core, bits, factors, enc, enc_back):
    at = lambda place: (lambda i: (0, place))
    after = lambda place: (lambda i: (0, place + i))
    dec = [(a, (a.shape[0], D), at(DEC_H2)) for a in factors]
    dec += [(b, (b.shape[0], D), after(DEC_DPRE)) for b in factors]
    enc = [(enc, (enc.shape[0], D), at(ENC_H2)), (enc_back, (enc.shape[0], D), after(0))]
    return grad_call(up_grad_body, core, dec, enc, SLABS, bits, "up_grad")


def heads_grad_body(bits, ways, core_ref, a0, a1, b0, b1, c0, c1, s0, s1, d, e, small, *out_refs):
    step = pl.program_id(0)
    last = 2 * GROUP_ROWS

    def give(made):
        made = made.astype(BF16).reshape(GROUPS, GROUP_ROWS, D)
        for at in range(4):

            @pl.when(step == at)
            def _():
                part = at // 2
                rows = slice(at % 2 * GROUP_ROWS, (at % 2 + 1) * GROUP_ROWS)
                refs = out_refs[part * ways : (part + 1) * ways]
                if part == 0:
                    put(core_ref, bits[0], made, refs)
                else:
                    put(core_ref, bits[1], made, refs, rows)

    def dec():
        rights = [jnp.where(step == 3, c[...], b[...]) for b, c in ((b0, c0), (b1, c1))]
        give(tn(a0[...], rights[0]) + tn(a1[...], rights[1]))

    on_either(core_ref, dec, lambda: give(tn(d[...], e[...])))

    @pl.when(step == 3)
    def _():
        given = [s[VIS:, :].astype(F32) for s in (s0, s1)]
        extra = jnp.where(core_ref[0] == 0, small[...], given[0] + given[1]).astype(BF16)
        for out_ref in out_refs[ways:]:
            out_ref[:, last:, :] = jnp.broadcast_to(extra, (out_ref.shape[0], ROWS, D))


def heads_grad(core, bits, lates, dqkvs, backs, enc, enc_back, small):
    zero = lambda i: (0, 0)
    n, m = lates[0].shape[0], enc.shape[0]
    dec = [(a, (n, D), lambda i: (0, jnp.where(i < 3, LATE_H, LATE_ATT))) for a in lates]
    dec += [(b, (n, D), lambda i: (0, jnp.minimum(i, 2))) for b in dqkvs]
    dec += [(c, (n, D), lambda i: (0, LATE_DBRANCH)) for c in lates]
    dec += [(s, s.shape, zero) for s in backs]
    enc = [
        (enc, (m, D), lambda i: (0, jnp.where(i < 3, ENC_H, ENC_ATT))),
        (enc_back, (m, D), lambda i: (0, jnp.where(i < 3, ENC_DQKV + i, ENC_DBRANCH))),
        (small, small.shape, zero),
    ]
    rows = 2 * GROUP_ROWS + ROWS
    outs = (SLABS[0], (rows, (GROUPS, rows, D), lambda i: (0, 0, 0)))
    return grad_call(heads_grad_body, core, dec, enc, outs, bits, "heads_grad")


def swapped(value):
    return lax.ppermute(value, "pipe", [(0, 1), (1, 0)])


def across(value, bit):
    size = lax.axis_size("dp")
    return lax.ppermute(value, "dp", [(i, i ^ 2**bit) for i in range(size)])


def dp_bit(bit):
    return lax.rem(lax.axis_index("dp") // 2**bit, 2)


class Order:
    def __init__(self):
        self.last = None

    def __call__(self, step, *operands):
        if self.last is not None:
            operands, _ = lax.optimization_barrier((operands, self.last))
        made = step(*operands)
        self.last = jax.tree.leaves(made)[0]
        return made


def half_sum(stay, got, at, which, left):
    def part(value):
        rest = value.shape[1:]
        value = value.reshape(2**at, 2, left // 2**at, *rest)
        chosen = lax.dynamic_index_in_dim(value, which, 1, keepdims=False)
        return chosen.reshape(left, *rest).astype(F32)

    return (part(stay) + part(got)).astype(BF16)


class Sum:
    def __init__(self, arrays, order):
        go, self.stay = arrays
        self.value = None
        self.order = list(order)
        bit = self.order.pop(0)
        self.bits = [b for b in range(GROUPS.bit_length() - 2, -1, -1) if b != bit]
        self.got = across(go, bit)

    def step(self, run):
        if not self.order:
            self.value = run(
                lambda stay, got: (stay.astype(F32) + got.astype(F32))[0], self.stay, self.got
            )
            return
        bit = self.order.pop(0)
        shape = self.stay.shape
        at = self.bits.index(bit)
        self.bits.remove(bit)
        left = 2 ** len(self.bits)

        def half(which):
            return lambda stay, got: half_sum(stay, got, at, which, left)

        mine = dp_bit(bit)
        go = run(half(1 - mine), self.stay, self.got)
        stay = run(half(mine), self.stay, self.got)
        self.got, self.stay = across(go, bit), stay


class Joined(Sum):
    def __init__(self, one, two):
        self.parts, self.cut = (one, two), one.stay.shape[1]
        self.order, self.bits = one.order, one.bits
        self.value, self.apart = None, True

    def step(self, run):
        if not self.apart:
            super().step(run)
            if self.value is not None:
                self.parts[0].value = self.value[: self.cut]
                self.parts[1].value = self.value[self.cut :]
            return
        self.apart = False
        bit = self.order.pop(0)
        at = self.bits.index(bit)
        self.bits = [b for b in self.bits if b != bit]
        left = 2 ** len(self.bits)

        def both(which):
            def make(*values):
                pairs = zip(values[:2], values[2:])
                return jnp.concatenate(
                    [half_sum(stay, got, at, which, left) for stay, got in pairs], axis=1
                )

            return make

        operands = [one.stay for one in self.parts] + [one.got for one in self.parts]
        mine = dp_bit(bit)
        go = run(both(1 - mine), *operands)
        self.stay = run(both(mine), *operands)
        self.got = across(go, bit)


class PlainSum:
    def __init__(self, parts, slabs):
        whole = jnp.concatenate([part for (part,) in parts], axis=1)
        size = lax.axis_size("dp")
        rows = whole.shape[1] // slabs // ROWS * ROWS
        extra = whole[0, slabs * rows :] if slabs * rows < whole.shape[1] else None
        grad = whole[:, : slabs * rows].reshape(GROUPS, slabs, rows, D).transpose(0, 2, 1, 3)
        grad = grad.reshape(GROUPS * rows, slabs * D).astype(F32)
        mine = lax.psum_scatter(grad, "dp", scatter_dimension=0, tiled=True)
        mine = mine.reshape(-1, slabs, D).transpose(1, 0, 2).reshape(-1, D)
        if extra is not None:
            mine = jnp.concatenate([mine, lax.psum(extra.astype(F32), "dp")])
        self.value = mine

    def step(self, run):
        pass


ORDERS = {
    "down": ((2, 1, 0, 3), (1, 2, 0, 3)),
    "up": ((0, 1, 2, 3), (1, 0, 2, 3)),
    "heads": ((2, 1, 0, 3), (0, 1, 2, 3)),
}
EARLY_STEPS = ()
STEPS = (("down", 0), ("down", 1), ("up", 0), ("up", 1), ("J1", ("down", 0), ("down", 1)), ("heads", 0), ("heads", 1), ("J1", 0), ("J2", ("up", 0), ("up", 1)), ("J2", 0), ("J1", 0), ("heads", 0), ("heads", 1), ("J2", 0), ("J1", 0), ("heads", 0), ("heads", 1), ("J2", 0), ("heads", 0), ("heads", 1),)


def on_device(
    section_input,
    visible_slot,
    image_of_slot,
    qkv_weight,
    out_weight,
    up_weight,
    down_weight,
    norm_gain,
    up_bias,
    vectors,
):
    pipe = lax.axis_index("pipe")
    size = lax.axis_size("dp")
    halving = size == GROUPS
    core = jnp.stack([pipe] + [dp_bit(bit) for bit in range(GROUPS.bit_length() - 1)])
    own = [qkv_weight[0], out_weight[0], up_weight[0], down_weight[0]]
    params = [vectors.transpose(1, 0, 2), norm_gain, up_bias]
    layout = (visible_slot, image_of_slot)
    rows = MICRO * VIS
    run = Order()
    both = [[weight, swapped(weight)] for weight in own]

    enc_x, enc, enc_qkv, enc_lse, enc_mid, enc_slope, sent, packed = run(
        lambda section, *w: encoder_forward(rows, params, layout, section, w),
        section_input, *own,
    )
    other_sent, other_packed = swapped(sent), swapped(packed)
    core, sent = lax.optimization_barrier((core, sent))
    x, dec, late, qkv, lse, dmid, datt, small = run(
        lambda sent, other_sent, packed, other_packed, *w: decoder(
            S, packed, other_packed, layout, sent, other_sent, section_input,
            [w[2 * i : 2 * i + 2] for i in range(4)],
        ),
        sent, other_sent, packed, other_packed, *[w for pair in both for w in pair],
    )
    other_dec = swapped(dec)
    dqkv, back = run(
        lambda *a: decoder_back(S, packed, other_packed, layout, *a, both[0]),
        qkv, datt, lse, small, x, dmid, late,
    )
    other_back = swapped(back)
    (late, dqkv), _ = lax.optimization_barrier(((late, dqkv), other_back))
    other_dqkv, other_late = swapped(dqkv), swapped(late)
    sums = {}

    def begin(name, parts, slabs):
        if halving:
            for i, (arrays, order) in enumerate(zip(parts, ORDERS[name])):
                sums[name, i] = Sum(arrays, order)
        else:
            sums[name, 0] = PlainSum(parts, slabs)

    def bits_of(name):
        return tuple(order[0] for order in ORDERS[name]) if halving else None

    parts = run(
        lambda *a: down_grad(core, bits_of("down"), a[:2], section_input[0], enc, a[2:]),
        dec, other_dec, back, other_back,
    )
    begin("down", parts, 1)
    ready = lax.optimization_barrier((back, other_back, other_dqkv, other_late))
    enc_back, small, results = run(
        lambda dy, other_dy: encoder_back(
            rows, params, layout, dy, other_dy, enc_lse, enc_slope, enc_mid, enc_qkv, enc_x, enc,
            own,
        ),
        *ready[:2],
    )
    other_dqkv, other_late = ready[2:]
    parts = run(
        lambda *a: up_grad(core, bits_of("up"), a[:2], enc, a[2]), dec, other_dec, enc_back
    )
    begin("up", parts, 4)
    if halving:
        for name, i in EARLY_STEPS:
            sums[name, i].step(run)
    parts = run(
        lambda *a: heads_grad(core, bits_of("heads"), a[:2], a[2:4], a[4:6], enc, *a[6:]),
        late, other_late, dqkv, other_dqkv, back, other_back, enc_back, small,
    )
    begin("heads", parts, 4)
    results = run(lambda *a: place_results(core, *a), results, late, other_late)
    width = D // size
    hidden = FF // size

    def wide(slabs):
        return jnp.concatenate(
            [slabs[i * width : (i + 1) * width] for i in range(slabs.shape[0] // width)], axis=1
        )

    def finish(name, *values):
        grad = jnp.concatenate(values) if len(values) > 1 else values[0]
        if name == "down":
            return grad
        if name == "up":
            return wide(grad)
        small = grad[TILES * width :]
        at = lax.axis_index("dp")
        mine = lax.dynamic_slice_in_dim(small, at * width, width, 1)
        bias = lax.dynamic_slice_in_dim(
            small[UBIAS : UBIAS + TILES].reshape(FF), at * hidden, hidden, 0
        )
        return wide(grad[: 3 * width]), grad[3 * width : TILES * width], mine, bias

    finished = {}
    if halving:
        joined = {}
        for step in STEPS:
            if len(step) == 3:
                joined[step[0]] = Joined(sums[step[1]], sums[step[2]])
            elif step[0] in joined:
                joined[step[0]].step(run)
            else:
                sums[step].step(run)
    for name in ORDERS:
        finished[name] = finish(
            name, *[one.value for (kind, _), one in sums.items() if kind == name]
        )
    down, up = finished["down"], finished["up"]
    qkv_grad, out_grad, mine, bias_grad = finished["heads"]
    return (
        results[None],
        qkv_grad[None],
        out_grad[None],
        up[None],
        down[None],
        mine[GAIN1 : GAIN2 + 1][None],
        bias_grad[None],
        mine[:GAIN1][None],
    )


def solution(mesh):
    in_specs = (
        P("pipe", "dp", None, None),
        P("dp", None),
        P("dp", None),
        P("pipe", None, None),
        P("pipe", None, None),
        P("pipe", None, None),
        P("pipe", None, None),
        P("pipe", None, None),
        P("pipe", None),
        P("pipe", None, None),
    )
    out_specs = (
        P("pipe", "dp", None, None),
        P("pipe", "dp", None),
        P("pipe", "dp", None),
        P("pipe", "dp", None),
        P("pipe", "dp", None),
        P("pipe", None, "dp"),
        P("pipe", "dp"),
        P("pipe", None, "dp"),
    )
    return jax.shard_map(
        on_device, mesh=mesh, in_specs=in_specs, out_specs=out_specs, check_vma=False
    )
```

```python
import functools
import math

import jax
import jax.numpy as jnp
import numpy as np
from jax import lax
from jax.experimental import pallas as pl
from jax.experimental.pallas import tpu as pltpu
from jax.sharding import PartitionSpec as P

D = 768
H = 12
HD = 64
FF = 3072
S = 512
VIS = 128
MICRO = 2
EPSILON = 1e-06
PAIRS = H // 2
TWO = 2 * HD
TILES = FF // D
WIDE = 2 * D
LOADS = FF // WIDE
HALF = D // 2
GROUPS = 16
GROUP_ROWS = D // GROUPS
PER = GROUPS // TILES
DOWN_ROWS = FF // GROUPS
ROWS = 16
FAR = -1e30
F32 = jnp.float32
BF16 = jnp.bfloat16

SHIFT1, QBIAS, VBIAS, OBIAS, ENTRY, SHIFT2, DBIAS, GAIN1, GAIN2, UBIAS = range(10)


def contract(left, right, left_dim, right_dim):
    return lax.dot_general(
        left, right, (((left_dim,), (right_dim,)), ((), ())), preferred_element_type=F32
    )


def nn(left, right):
    return contract(left, right, 1, 0)


def nt(left, right):
    return contract(left, right, 1, 1)


def tn(left, right):
    return contract(left, right, 0, 0)


def unit_rows(rows):
    centered = rows - jnp.mean(rows, axis=-1, keepdims=True)
    scale = lax.rsqrt(jnp.mean(centered * centered, axis=-1, keepdims=True) + EPSILON)
    return centered * scale, scale


def unit_rows_back(grad, unit, scale, gain):
    scaled = grad * gain
    return scale * (
        scaled
        - jnp.mean(scaled, axis=-1, keepdims=True)
        - unit * jnp.mean(scaled * unit, axis=-1, keepdims=True)
    )


def in_head(shape, which):
    lane = lax.broadcasted_iota(jnp.int32, shape, 1)
    return lane < HD if which == 0 else lane >= HD


def one_head(pair, which):
    return jnp.where(in_head(pair.shape, which), pair, jnp.zeros_like(pair))


def colsum(rows):
    return jnp.sum(rows, axis=0, keepdims=True)


class Params:
    def __init__(self, core, refs):
        self.core, self.refs = core, refs

    def hidden(self, t):
        if len(self.refs) == 3:
            return self.refs[2][:, pl.ds(pl.multiple_of(t * WIDE, WIDE), WIDE)]
        each = WIDE // D
        return jnp.concatenate(
            [self.pick(pl.ds(UBIAS + t * each + part, 1)) for part in range(each)], axis=1
        )

    def __call__(self, index):
        at = slice(index, index + 1)
        if len(self.refs) < 3:
            return self.pick(at)
        if index < GAIN1:
            return self.refs[0][index]
        return self.refs[1][0, index - GAIN1 : index - GAIN1 + 1]

    def pick(self, at):
        return jnp.where(self.core == 0, self.refs[1][at], self.refs[0][at])


def upright(line):
    return jnp.broadcast_to(line, (8, line.shape[1])).T[:, :1]


def hits(slots):
    return lax.broadcasted_iota(jnp.int32, (VIS, S), 0).astype(F32) == slots


def hits_upright(slots):
    return lax.broadcasted_iota(jnp.int32, (S, VIS), 1).astype(F32) == slots


def marks(groups, count):
    lane = lax.broadcasted_iota(jnp.int32, (groups.shape[0], TWO), 1)
    lane = jnp.where(lane < HD, lane, lane - HD).astype(F32)
    same = lane == groups
    key_fill = jnp.where(same, 1.0, 0.0).astype(BF16)
    query_fill = jnp.where(jnp.logical_or(same, lane >= count), 0.0, FAR).astype(BF16)
    return key_fill, query_fill


class Weight:
    def __init__(self, core, refs, dst, sems, cuts):
        self.core, self.refs, self.dst, self.sems, self.cuts = core, refs, dst, sems, cuts

    def start(self, i):
        cut = self.cuts[i]

        def go(ref):
            pltpu.make_async_copy(ref.at[cut], self.dst.at[cut], self.sems.at[i]).start()

        if len(self.refs) == 1:
            go(self.refs[0])
        else:
            pl.when(self.core == 0)(lambda: go(self.refs[1]))
            pl.when(self.core != 0)(lambda: go(self.refs[0]))

    def get(self, i):
        cut = self.cuts[i]
        pltpu.make_async_copy(self.refs[0].at[cut], self.dst.at[cut], self.sems.at[i]).wait()
        return self.dst[cut]


    def take(self, i, cut):
        pltpu.make_async_copy(self.refs[0].at[cut], self.dst.at[cut], self.sems.at[i]).wait()
        return self.dst[cut]


class Either:
    def __init__(self, core, on_first, on_second, dst, sem):
        self.copy = pltpu.make_async_copy(on_first, dst, sem)
        self.dst = dst
        pl.when(core == 0)(self.copy.start)
        pl.when(core != 0)(lambda: pltpu.make_async_copy(on_second, dst, sem).start())

    def get(self):
        self.copy.wait()
        return self.dst[...]


class Out:
    def __init__(self, sems):
        self.sems, self.count, self.going = sems, 0, []

    def send(self, src, dst):
        copy = pltpu.make_async_copy(src, dst, self.sems.at[self.count])
        self.count += 1
        copy.start()
        self.going.append(copy)

    def wait(self):
        for copy in self.going:
            copy.wait()


SMEM, VMEM, HBM = pltpu.SMEM, pltpu.VMEM, pl.ANY


def struct(shape, dtype):
    return jax.ShapeDtypeStruct(shape, dtype)


def size_of(shape):
    return math.prod(shape.shape) * shape.dtype.itemsize


def call(body, ins, outs, scratch, name, flops):
    arrays = [array for array, _ in ins]
    shapes = [shape for shape, _ in outs]
    return pl.pallas_call(
        body,
        in_specs=[pl.BlockSpec(memory_space=space) for _, space in ins],
        out_specs=[pl.BlockSpec(memory_space=space) for _, space in outs],
        out_shape=shapes,
        scratch_shapes=scratch,
        compiler_params=pltpu.CompilerParams(vmem_limit_bytes=60 * 2**20),
        cost_estimate=pl.CostEstimate(flops=1, bytes_accessed=1, transcendentals=0),
        name=name,
    )(*arrays)


def taker(refs):
    refs = list(refs)

    def take(count):
        return [refs.pop(0) for _ in range(count)]

    return take


def columns(i):
    return (slice(None), slice(i * D, (i + 1) * D))


def positions():
    width = D // 2
    frequency = np.exp(np.arange(width) * (-math.log(10000.0) / width))
    angles = np.arange(S)[:, None] * frequency[None, :]
    return jnp.asarray(np.concatenate([np.sin(angles), np.cos(angles)], axis=1), F32)


def section(i):
    return columns(i)


def group_columns(core, decoder, slots_ref, images_ref):
    if decoder:
        return upright(images_ref[pl.ds(core, 1), :].astype(F32)), 2
    parts = []
    for micro in range(MICRO):
        hit = hits(slots_ref[micro : micro + 1, :].astype(F32))
        mark = images_ref[micro : micro + 1, :].astype(F32) + 1.0
        parts.append(jnp.sum(jnp.where(hit, mark, 0.0), axis=1, keepdims=True) + 3.0 * micro)
    return jnp.concatenate(parts, axis=0), 3 * MICRO


def project(params, weight, x_s, h_s, qkv_s, out, h_out, qkv_out):
    unit, _scale = unit_rows(x_s[...])
    h = (unit * params(GAIN1) + params(SHIFT1)).astype(BF16)
    h_s[...] = h
    out.send(h_s, h_out)
    for part, bias in enumerate((QBIAS, None, VBIAS)):
        made = nn(h, weight.get(part))
        if bias is not None:
            made = made + params(bias)
        qkv_s[part] = made.astype(BF16)
        out.send(qkv_s.at[part], qkv_out.at[part])


def attend(n, together, fills, qkv_s, att_s, lse_ref):
    key_fill, query_fill = fills
    scaling = jnp.asarray(HD**-0.5, BF16)

    def pairs(step, _):
        lanes = [
            pl.ds(pl.multiple_of((step * together + i) * TWO, TWO), TWO) for i in range(together)
        ]
        heads = [(i, which) for i in range(together) for which in range(2)]
        qs = [qkv_s[0, :, at] * scaling for at in lanes]
        ks = [qkv_s[1, :, at] for at in lanes]
        vs = [qkv_s[2, :, at].T for at in lanes]
        scores = [
            nt(
                jnp.where(in_head((n, TWO), which), ks[i], key_fill),
                jnp.where(in_head((n, TWO), which), qs[i], query_fill),
            )
            for i, which in heads
        ]
        tops = [jnp.max(score, axis=0, keepdims=True) for score in scores]
        raised = [jnp.exp(score - top) for score, top in zip(scores, tops)]
        totals = [colsum(part) for part in raised]
        found = [
            nn(vs[i][which * HD : (which + 1) * HD, :], part.astype(BF16)) * (1.0 / total)
            for (i, which), part, total in zip(heads, raised, totals)
        ]
        for i in range(together):
            att_s[:, lanes[i]] = jnp.concatenate(found[2 * i : 2 * i + 2], axis=0).T.astype(BF16)
            lse_ref[step * together + i] = jnp.concatenate(
                [tops[at] + jnp.log(totals[at]) for at in (2 * i, 2 * i + 1)], axis=0
            )
        return 0

    lax.fori_loop(0, PAIRS // together, pairs, 0)


def feed(params, weights, x_s, att_s, mid_s, h2_s, act_s, slope_s, sum_s, out, h2_out, act_out):
    out_weight, up, down = weights
    mid = x_s[...] + nn(att_s[...], out_weight.get(0)) + params(OBIAS)
    mid_s[...] = mid
    unit, _scale = unit_rows(mid)
    h2 = (unit * params(GAIN2) + params(SHIFT2)).astype(BF16)
    h2_s[...] = h2
    out.send(h2_s, h2_out)
    sum_s[...] = mid + params(DBIAS)

    def tile(t, _):
        at = (slice(None), pl.ds(pl.multiple_of(t * WIDE, WIDE), WIDE))
        pre = nn(h2_s[...], up.take(t, at)) + params.hidden(t)
        below = 0.5 + 0.5 * lax.erf(pre * math.sqrt(0.5))
        act = (pre * below).astype(BF16)
        act_s[at] = act
        density = jnp.exp(-0.5 * pre * pre) * (1.0 / math.sqrt(2.0 * math.pi))
        slope_s[at] = (below + pre * density).astype(BF16)
        sum_s[...] += nn(act, down.take(t, (at[1], slice(None))))
        return 0

    lax.fori_loop(0, LOADS, tile, 0)
    out.send(act_s, act_out)


def feed_back(
    params, weights, dff, dff_ref, slope, mid, dpre_s, dh2_s, small_ref, out, dpre_out, width
):
    out_weight, up, down = weights
    small_ref[...] = jnp.zeros_like(small_ref)
    small_ref[DBIAS : DBIAS + 1, :] = colsum(dff.astype(F32))
    if dff_ref is not None:
        dff_ref[...] = dff
    dh2_s[...] = jnp.zeros_like(dh2_s)

    def tile(t, _):
        at = (slice(None), pl.ds(pl.multiple_of(t * width, width), width))
        dact = nt(dff_ref[...], down(t, (at[1], slice(None))))
        dpre = (dact * slope(t, at).astype(F32)).astype(BF16)
        dpre_s[at] = dpre
        sums = colsum(dpre.astype(F32))
        for part in range(width // D):
            small_ref[pl.ds(UBIAS + t * (width // D) + part, 1), :] = sums[columns(part)]
        dh2_s[...] += nt(dpre, up(t, at))
        return 0

    lax.fori_loop(0, FF // width, tile, 0)
    out.send(dpre_s, dpre_out)
    dh2 = dh2_s[...]
    unit, scale = unit_rows(mid())
    small_ref[GAIN2 : GAIN2 + 1, :] = colsum(dh2 * unit)
    small_ref[SHIFT2 : SHIFT2 + 1, :] = colsum(dh2)
    dmid = dff.astype(F32) + unit_rows_back(dh2, unit, scale, params(GAIN2))
    dbranch = dmid.astype(BF16)
    small_ref[OBIAS : OBIAS + 1, :] = colsum(dbranch.astype(F32))
    return dmid, dbranch, nt(dbranch, out_weight()).astype(BF16)


def attend_back(n, together, fills, qkv_ref, att_ref, datt_ref, lse_ref, dqkv_ref):
    key_fill, query_fill = fills
    scaling = jnp.asarray(HD**-0.5, BF16)

    def pairs(step, _):
        lanes = [
            pl.ds(pl.multiple_of((step * together + i) * TWO, TWO), TWO) for i in range(together)
        ]
        heads = [(i, which) for i in range(together) for which in range(2)]
        qs = [qkv_ref[0, :, at] * scaling for at in lanes]
        ks = [qkv_ref[1, :, at] for at in lanes]
        vs = [qkv_ref[2, :, at] for at in lanes]
        turned = [k.T for k in ks]
        dos = [datt_ref[:, at] for at in lanes]
        mine = [one_head(dos[i], which) for i, which in heads]
        along = [
            (att_ref[:, at].astype(F32) * do.astype(F32)).T for at, do in zip(lanes, dos)
        ]
        scores = [
            nt(
                jnp.where(in_head((n, TWO), which), ks[i], key_fill),
                jnp.where(in_head((n, TWO), which), qs[i], query_fill),
            )
            for i, which in heads
        ]
        dprobs = [nt(vs[i], do) for (i, which), do in zip(heads, mine)]
        probs = [
            jnp.exp(score - lse_ref[step * together + i, which : which + 1, :])
            for (i, which), score in zip(heads, scores)
        ]
        dscores = [
            (prob * (dprob - colsum(along[i][which * HD : (which + 1) * HD, :]))).astype(BF16)
            for (i, which), prob, dprob in zip(heads, probs, dprobs)
        ]
        for i in range(together):
            a, b = 2 * i, 2 * i + 1
            dv = nn(probs[a].astype(BF16), mine[a]) + nn(probs[b].astype(BF16), mine[b])
            dk = nn(dscores[a], one_head(qs[i], 0)) + nn(dscores[b], one_head(qs[i], 1))
            dq = jnp.concatenate(
                [nn(turned[i][:HD, :], dscores[a]), nn(turned[i][HD:, :], dscores[b])], axis=0
            )
            dqkv_ref[:, pl.ds(0 * D + lanes[i].start, TWO)] = (dq * HD**-0.5).T.astype(BF16)
            dqkv_ref[:, pl.ds(1 * D + lanes[i].start, TWO)] = dk.astype(BF16)
            dqkv_ref[:, pl.ds(2 * D + lanes[i].start, TWO)] = dv.astype(BF16)
        return 0

    lax.fori_loop(0, PAIRS // together, pairs, 0)


def project_back(params, weight, dqkv_ref, x, dmid, small_ref):
    dh = 0.0
    for part in range(3):
        made = dqkv_ref[columns(part)]
        if part != 1:
            bias = QBIAS if part == 0 else VBIAS
            small_ref[bias : bias + 1, :] = colsum(made.astype(F32))
        dh = dh + nt(made, weight.get(part))
    unit, scale = unit_rows(x())
    small_ref[GAIN1 : GAIN1 + 1, :] = colsum(dh * unit)
    small_ref[SHIFT1 : SHIFT1 + 1, :] = colsum(dh)
    return dmid() + unit_rows_back(dh, unit, scale, params(GAIN1))


EVERYTHING = (slice(None), slice(None))


def qkv_loads(core, refs, dst, sems):
    return Weight(core, refs, dst, sems, [columns(part) for part in range(3)])


def feed_loads(core, w_out, w_up, w_down, dsts, sems, width):
    parts = [slice(i, i + width) for i in range(0, FF, width)]
    return (
        Weight(core, w_out, dsts[0], sems[0], [EVERYTHING]),
        Weight(core, w_up, dsts[1], sems[1], [(slice(None), part) for part in parts]),
        Weight(core, w_down, dsts[2], sems[2], [(part, slice(None)) for part in parts]),
    )


def dma(count):
    return pltpu.SemaphoreType.DMA((count,))


FEED_SCRATCH = [VMEM((D, D), BF16), VMEM((D, FF), BF16), VMEM((FF, D), BF16)]
FEED_SEMS = [dma(1), dma(LOADS), dma(LOADS)]
QKV_SCRATCH = [VMEM((D, 3 * D), BF16), dma(3)]


DEC_DPRE, DEC_H2, DEC_SECTIONS = TILES, 2 * TILES, 2 * TILES + 1
LATE_H, LATE_ATT, LATE_DBRANCH, LATE_OUT, LATE_SECTIONS = range(5)
ENC_H, ENC_H2, ENC_ATT, ENC_SECTIONS = range(TILES, TILES + 4)
ENC_DBRANCH, ENC_DQKV, ENC_BACK_SECTIONS = TILES, TILES + 1, TILES + 4


def sections(first, count):
    return (slice(None), slice(first * D, (first + count) * D))


def encoder_forward_body(n, *refs):
    take = taker(refs)
    given = take(3)
    core = lax.axis_index("pipe")
    params = Params(core, given)
    slots_ref, images_ref, section_ref = take(3)
    w_qkv, w_out, w_up, w_down = take(1), take(1), take(1), take(1)
    x_out, factors_out, qkv_out, lse_ref, mid_out, slope_out, sent_ref, params_ref = take(8)
    x_s, h_s, qkv_s, att_s, mid_s, h2_s, act_s, slope_s, sum_s = take(9)
    wq_s, wq_sems = take(2)
    dsts, sems = take(3), take(3)
    (out_sems,) = take(1)
    for i in range(GAIN1):
        params_ref[i : i + 1, :] = given[0][i]
    params_ref[GAIN1:UBIAS, :] = given[1][0]
    for t in range(TILES):
        params_ref[UBIAS + t : UBIAS + t + 1, :] = given[2][columns(t)]

    @pl.when(core != 0)
    def _():
        sent_ref[n:, :] = section_ref[0, 0]

    @pl.when(core == 0)
    def _():
        weight = qkv_loads(core, w_qkv, wq_s, wq_sems)
        weights = feed_loads(core, w_out, w_up, w_down, dsts, sems, WIDE)
        for part in range(3):
            weight.start(part)
        weights[0].start(0)
        for t in range(LOADS):
            weights[1].start(t)
            weights[2].start(t)
        out = Out(out_sems)
        for micro in range(MICRO):
            hit = hits(slots_ref[micro : micro + 1, :].astype(F32))
            x_s[micro * VIS : (micro + 1) * VIS, :] = nn(
                hit.astype(BF16), section_ref[0, micro]
            ) + params(ENTRY)
        out.send(x_s, x_out)
        project(params, weight, x_s, h_s, qkv_s, out, factors_out.at[section(ENC_H)], qkv_out)
        fills = marks(*group_columns(core, False, slots_ref, images_ref))
        attend(n, 3, fills, qkv_s, att_s, lse_ref)
        out.send(att_s, factors_out.at[section(ENC_ATT)])
        feed(
            params, weights, x_s, att_s, mid_s, h2_s, act_s, slope_s, sum_s, out,
            factors_out.at[section(ENC_H2)], factors_out.at[sections(0, TILES)],
        )
        out.send(mid_s, mid_out)
        out.send(slope_s, slope_out)
        sent_ref[:n, :] = sum_s[...].astype(BF16)
        out.wait()


def encoder_forward(n, params, layout, section, weights):
    ins = [(a, VMEM) for a in (*params, *layout, section)]
    ins += [(w, HBM) for w in weights]
    outs = [
        (struct((n, D), F32), HBM),
        (struct((n, ENC_SECTIONS * D), BF16), HBM),
        (struct((3, n, D), BF16), HBM),
        (struct((PAIRS, 2, n), F32), VMEM),
        (struct((n, D), F32), HBM),
        (struct((n, FF), BF16), HBM),
        (struct((n + S, D), BF16), VMEM),
        (struct((ROWS, D), F32), VMEM),
    ]
    scratch = [
        VMEM((n, D), F32),
        VMEM((n, D), BF16),
        VMEM((3, n, D), BF16),
        VMEM((n, D), BF16),
        VMEM((n, D), F32),
        VMEM((n, D), BF16),
        VMEM((n, FF), BF16),
        VMEM((n, FF), BF16),
        VMEM((n, D), F32),
        *QKV_SCRATCH,
        *FEED_SCRATCH,
        *FEED_SEMS,
        dma(10),
    ]
    return call(
        functools.partial(encoder_forward_body, n),
        ins,
        outs,
        scratch,
        "encoder_forward",
        2 * n * (4 * D * D + 2 * D * FF),
    )


def decoder_body(n, *refs):
    take = taker(refs)
    core = lax.axis_index("pipe")
    params = Params(core, take(2))
    slots_ref, images_ref, pos_ref, sent_ref, other_sent_ref, section_ref = take(6)
    w_qkv, w_out, w_up, w_down = take(2), take(2), take(2), take(2)
    x_out, factors_out, late_out, qkv_out, lse_ref, dmid_ref, datt_ref, small_ref = take(8)
    x_s, h_s, qkv_s, att_s, mid_s, h2_s, act_s, slope_s, sum_s, dpre_s, dff_s = take(11)
    dbranch_s, decoded_s = take(2)
    wq_s, wq_sems = take(2)
    dsts, sems = take(3), take(3)
    out_sems, in_sems = take(2)
    rows = MICRO * VIS
    weight = qkv_loads(core, w_qkv, wq_s, wq_sems)
    weights = feed_loads(core, w_out, w_up, w_down, dsts, sems, WIDE)
    for part in range(3):
        weight.start(part)
    weights[0].start(0)
    for t in range(LOADS):
        weights[1].start(t)
        weights[2].start(t)
    dff = Either(core, other_sent_ref.at[rows:], section_ref.at[0, 1], dff_s, in_sems.at[0])
    out = Out(out_sems)
    slots = upright(slots_ref[pl.ds(core, 1), :].astype(F32))
    sent = jnp.where(core == 0, sent_ref[:VIS, :], other_sent_ref[rows - VIS : rows, :])
    x = nn(hits_upright(slots).astype(BF16), sent) + pos_ref[...]
    x_s[...] = x + jnp.where(slots == VIS, params(ENTRY), 0.0)
    out.send(x_s, x_out)
    project(params, weight, x_s, h_s, qkv_s, out, late_out.at[section(LATE_H)], qkv_out)
    fills = marks(*group_columns(core, True, slots_ref, images_ref))
    attend(n, 2, fills, qkv_s, att_s, lse_ref)
    out.send(att_s, late_out.at[section(LATE_ATT)])
    feed(
        params, weights, x_s, att_s, mid_s, h2_s, act_s, slope_s, sum_s, out,
        factors_out.at[section(DEC_H2)], factors_out.at[sections(0, TILES)],
    )
    decoded_s[...] = sum_s[...].astype(BF16)
    out.send(decoded_s, late_out.at[section(LATE_OUT)])
    dmid_ref[...], dbranch_s[...], datt_ref[...] = feed_back(
        params,
        (
            lambda: weights[0].dst[...],
            lambda t, at: weights[1].dst[at],
            lambda t, at: weights[2].dst[at],
        ),
        dff.get(),
        dff_s,
        lambda t, at: slope_s[at],
        lambda: mid_s[...],
        dpre_s,
        sum_s,
        small_ref,
        out,
        factors_out.at[sections(DEC_DPRE, TILES)],
        WIDE,
    )
    out.send(dbranch_s, late_out.at[section(LATE_DBRANCH)])
    out.wait()


def decoder(n, params, other_params, layout, sent, other_sent, section, weights):
    ins = [(a, VMEM) for a in (params, other_params, *layout, positions())]
    ins += [(sent, VMEM), (other_sent, VMEM), (section, HBM)]
    ins += [(w, HBM) for pair in weights for w in pair]
    outs = [
        (struct((n, D), F32), HBM),
        (struct((n, DEC_SECTIONS * D), BF16), HBM),
        (struct((n, LATE_SECTIONS * D), BF16), HBM),
        (struct((3, n, D), BF16), HBM),
        (struct((PAIRS, 2, n), F32), VMEM),
        (struct((n, D), F32), VMEM),
        (struct((n, D), BF16), VMEM),
        (struct((ROWS, D), F32), VMEM),
    ]
    scratch = [
        VMEM((n, D), F32),
        VMEM((n, D), BF16),
        VMEM((3, n, D), BF16),
        VMEM((n, D), BF16),
        VMEM((n, D), F32),
        VMEM((n, D), BF16),
        VMEM((n, FF), BF16),
        VMEM((n, FF), BF16),
        VMEM((n, D), F32),
        VMEM((n, FF), BF16),
        VMEM((n, D), BF16),
        VMEM((n, D), BF16),
        VMEM((n, D), BF16),
        *QKV_SCRATCH,
        *FEED_SCRATCH,
        *FEED_SEMS,
        dma(12),
        dma(1),
    ]
    return call(
        functools.partial(decoder_body, n),
        ins,
        outs,
        scratch,
        "decoder",
        2 * n * (5 * D * D + 4 * D * FF) + 4 * n * n * D,
    )


def decoder_back_body(n, *refs):
    take = taker(refs)
    core = lax.axis_index("pipe")
    params = Params(core, take(2))
    slots_ref, images_ref, qkv_ref, datt_ref, lse_ref, small_in = take(6)
    x_in, dmid_in, factors_in = take(3)
    w_qkv = take(2)
    dqkv_out, back_ref = take(2)
    dqkv_s, x_s, dmid_s, att_s, small_s, wq_s, wq_sems, in_sems, out_sems = take(9)
    att = pltpu.make_async_copy(factors_in.at[section(LATE_ATT)], att_s, in_sems.at[2])
    att.start()
    weight = qkv_loads(core, w_qkv, wq_s, wq_sems)
    x = Weight(core, [x_in], x_s, in_sems, [EVERYTHING])
    dmid = Weight(core, [dmid_in], dmid_s, in_sems.at[pl.ds(1, 1)], [EVERYTHING])
    for part in range(3):
        weight.start(part)
    x.start(0)
    dmid.start(0)
    fills = marks(*group_columns(core, True, slots_ref, images_ref))
    att.wait()
    attend_back(n, 1, fills, qkv_ref, att_s, datt_ref, lse_ref, dqkv_s)
    out = Out(out_sems)
    out.send(dqkv_s, dqkv_out)
    small_s[...] = small_in[...]
    dx = project_back(
        params, weight, dqkv_s, lambda: x.get(0), lambda: dmid.get(0), small_s
    )
    slots = slots_ref[pl.ds(core, 1), :].astype(F32)
    small_s[ENTRY : ENTRY + 1, :] = colsum(jnp.where(upright(slots) == VIS, dx, 0.0))
    back_ref[:VIS, :] = nn(hits(slots).astype(BF16), dx.astype(BF16)).astype(BF16)
    back_ref[VIS:, :] = small_s[...].astype(BF16)
    out.wait()


def decoder_back(
    n, params, other_params, layout, qkv, datt, lse, small, x, dmid, factors, w_qkv
):
    ins = [(a, VMEM) for a in (params, other_params, *layout)]
    ins += [(a, VMEM) for a in (qkv, datt, lse, small)]
    ins += [(a, HBM) for a in (x, dmid, factors, *w_qkv)]
    outs = [
        (struct((n, 3 * D), BF16), HBM),
        (struct((VIS + ROWS, D), BF16), VMEM),
    ]
    scratch = [
        VMEM((n, 3 * D), BF16),
        VMEM((n, D), F32),
        VMEM((n, D), F32),
        VMEM((n, D), BF16),
        VMEM((ROWS, D), F32),
        *QKV_SCRATCH,
        dma(3),
        dma(1),
    ]
    return call(
        functools.partial(decoder_back_body, n),
        ins,
        outs,
        scratch,
        "decoder_back",
        2 * n * D * 3 * D + 10 * n * n * D,
    )


def encoder_back_body(n, *refs):
    take = taker(refs)
    core = lax.axis_index("pipe")
    params = Params(core, take(3))
    slots_ref, images_ref, dy_ref, other_dy_ref, lse_ref = take(5)
    slope_in, mid_in, qkv_in, x_in, enc_in = take(5)
    w_qkv, w_out, w_up, w_down = take(1), take(1), take(1), take(1)
    factors_out, small_ref, results_out = take(3)
    slope_s, mid_s, qkv_s, x_s, att_s, dpre_s, dh2_s, dbranch_s, datt_s, dqkv_s, back_s = take(11)
    wq_s, wq_sems = take(2)
    dsts, sems = take(3), take(3)
    in_sems, out_sems = take(2)

    @pl.when(core == 0)
    def _():
        weight = qkv_loads(core, w_qkv, wq_s, wq_sems)
        weights = feed_loads(core, w_out, w_up, w_down, dsts, sems, D)
        out_weight, up, down = weights
        slope = Weight(core, [slope_in], slope_s, in_sems, [columns(t) for t in range(TILES)])
        mid = Weight(core, [mid_in], mid_s, in_sems.at[pl.ds(TILES, 1)], [EVERYTHING])
        qkv = Weight(
            core, [qkv_in], qkv_s, in_sems.at[pl.ds(TILES + 1, 1)], [(slice(None),) * 3]
        )
        x = Weight(core, [x_in], x_s, in_sems.at[pl.ds(TILES + 2, 1)], [EVERYTHING])
        att = pltpu.make_async_copy(
            enc_in.at[section(ENC_ATT)], att_s, in_sems.at[TILES + 3]
        )
        for t in range(TILES):
            down.start(t)
            slope.start(t)
            up.start(t)
        mid.start(0)
        out_weight.start(0)
        qkv.start(0)
        att.start()
        for part in range(3):
            weight.start(part)
        x.start(0)
        out = Out(out_sems)
        dff = jnp.concatenate([dy_ref[:VIS, :], other_dy_ref[:VIS, :]], axis=0)
        dmid, dbranch, datt = feed_back(
            params, (lambda: out_weight.get(0), up.take, down.take), dff, datt_s, slope.take,
            lambda: mid.get(0), dpre_s, dh2_s, small_ref, out,
            factors_out.at[sections(0, TILES)], D,
        )
        dh2_s[...] = dmid
        dbranch_s[...] = dbranch
        out.send(dbranch_s, factors_out.at[section(ENC_DBRANCH)])
        datt_s[...] = datt
        fills = marks(*group_columns(core, False, slots_ref, images_ref))
        qkv.get(0)
        att.wait()
        attend_back(n, 2, fills, qkv_s, att_s, datt_s, lse_ref, dqkv_s)
        out.send(dqkv_s, factors_out.at[sections(ENC_DQKV, 3)])
        dx = project_back(params, weight, dqkv_s, lambda: x.get(0), lambda: dh2_s[...], small_ref)
        low = dx.astype(BF16)
        small_ref[ENTRY : ENTRY + 1, :] = colsum(dx)
        for micro in range(MICRO):
            slots = upright(slots_ref[micro : micro + 1, :].astype(F32))
            back_s[micro] = nn(
                hits_upright(slots).astype(BF16), low[micro * VIS : (micro + 1) * VIS, :]
            ).astype(BF16)
        out.send(back_s, results_out)
        out.wait()


def encoder_back(
    n, params, layout, dy, other_dy, lse, slope, mid, qkv, x, enc, weights
):
    ins = [(a, VMEM) for a in (*params, *layout, dy, other_dy, lse)]
    ins += [(a, HBM) for a in (slope, mid, qkv, x, enc, *weights)]
    outs = [
        (struct((n, ENC_BACK_SECTIONS * D), BF16), HBM),
        (struct((ROWS, D), F32), VMEM),
        (struct((MICRO, S, D), BF16), HBM),
    ]
    scratch = [
        VMEM((n, FF), BF16),
        VMEM((n, D), F32),
        VMEM((3, n, D), BF16),
        VMEM((n, D), F32),
        VMEM((n, D), BF16),
        VMEM((n, FF), BF16),
        VMEM((n, D), F32),
        VMEM((n, D), BF16),
        VMEM((n, D), BF16),
        VMEM((n, 3 * D), BF16),
        VMEM((MICRO, S, D), BF16),
        *QKV_SCRATCH,
        *FEED_SCRATCH,
        dma(1),
        dma(TILES),
        dma(TILES),
        dma(TILES + 4),
        dma(4),
    ]
    return call(
        functools.partial(encoder_back_body, n),
        ins,
        outs,
        scratch,
        "encoder_back",
        2 * n * (4 * D * D + 2 * D * FF),
    )


def place_body(core_ref, _, dec_in, other_dec_in, results_out, back_s, in_sems, out_sems):
    @pl.when(core_ref[0] != 0)
    def _():
        parts = [
            pltpu.make_async_copy(ref.at[section(LATE_OUT)], back_s.at[at], in_sems.at[at])
            for at, ref in enumerate((other_dec_in, dec_in))
        ]
        out = Out(out_sems)
        for part in parts:
            part.start()
        for at, part in enumerate(parts):
            part.wait()
            out.send(back_s.at[at], results_out.at[at])
        out.wait()


def place_results(core, results, dec, other_dec):
    return pl.pallas_call(
        place_body,
        in_specs=[pl.BlockSpec(memory_space=SMEM)] + [pl.BlockSpec(memory_space=HBM)] * 3,
        out_specs=pl.BlockSpec(memory_space=HBM),
        out_shape=struct(results.shape, BF16),
        scratch_shapes=[VMEM((MICRO, S, D), BF16), dma(2), dma(2)],
        input_output_aliases={1: 0},
        name="place_results",
    )(core, results, dec, other_dec)


def put(core_ref, bit, made, out_refs, at=slice(None)):
    if bit is None:
        out_refs[0][:, at, :] = made
        return
    groups, rows, width = made.shape
    made = made.reshape(groups // 2 ** (bit + 1), 2, 2**bit, rows, width)
    mine = core_ref[1 + bit]
    low, high = made[:, 0], made[:, 1]
    for out_ref, other in zip(out_refs, (True, False)):
        chosen = jnp.where((mine == 0) != other, low, high)
        out_ref[:, at, :] = chosen.reshape(groups // 2, rows, width)


def grad_call(body, core, dec, enc, outs, bits, name):
    def only(wanted, index):
        def place(i, core):
            return tuple(jnp.where(core[0] == wanted, at, 0) for at in index(i))

        return place

    specs = [pl.BlockSpec(block, only(1, index)) for _, block, index in dec]
    specs += [pl.BlockSpec(block, only(0, index)) for _, block, index in enc]
    arrays = [a for a, _, _ in (*dec, *enc)]
    ways = 1 if bits is None else 2
    out_specs, shapes = [], []
    for rows, block, index in outs:
        spec = pl.BlockSpec((block[0] // ways, *block[1:]), lambda i, core, index=index: index(i))
        out_specs += [spec] * ways
        shapes += [struct((GROUPS // ways, rows, D), BF16)] * ways
    made = pl.pallas_call(
        functools.partial(body, bits or (None, None), ways),
        grid_spec=pltpu.PrefetchScalarGridSpec(
            num_scalar_prefetch=1, grid=(TILES,), in_specs=specs, out_specs=out_specs
        ),
        out_shape=shapes,
        compiler_params=pltpu.CompilerParams(
            vmem_limit_bytes=60 * 2**20, dimension_semantics=("arbitrary",)
        ),
        cost_estimate=pl.CostEstimate(flops=1, bytes_accessed=1, transcendentals=0),
        name=name,
    )(core, *arrays)
    return made[:ways], made[ways:]


def on_either(core_ref, dec, enc):
    pl.when(core_ref[0] != 0)(dec)
    pl.when(core_ref[0] == 0)(enc)


def down_grad_body(bits, ways, core_ref, a0, a1, b0, b1, c, d0, d1, *out_refs):
    step = pl.program_id(0)

    def give(made):
        made = made.astype(BF16).reshape(PER, 2, DOWN_ROWS // 2, D)
        for part, bit in enumerate(bits):
            refs = out_refs[part * ways : (part + 1) * ways]
            if bit != 2:
                put(core_ref, bit, made[:, part], refs)
                continue
            stays = lax.rem(step, 2) == core_ref[1 + bit]

            @pl.when(stays)
            def _():
                refs[1][...] = made[:, part]

            @pl.when(jnp.logical_not(stays))
            def _():
                refs[0][...] = made[:, part]

    on_either(
        core_ref,
        lambda: give(tn(a0[...], b0[0]) + tn(a1[...], b1[0])),
        lambda: give(tn(c[...], jnp.concatenate([d0[:VIS, :], d1[:VIS, :]], axis=0))),
    )


def down_grad(core, bits, factors, section, enc, dys):
    tile = lambda i: (0, i)
    zero = lambda i: (0, 0)
    dec = [(a, (a.shape[0], D), tile) for a in factors]
    dec += [(section, (1, S, D), lambda i, m=m: (m, 0, 0)) for m in (1, 0)]
    enc = [(enc, (enc.shape[0], D), tile)] + [(dy, dy.shape, zero) for dy in dys]
    rows = DOWN_ROWS // 2
    outs = []
    for bit in bits or (None, None):
        if bit == 2:
            outs.append((rows, (2 * PER, rows, D), lambda i: (i // 2, 0, 0)))
        else:
            outs.append((rows, (PER, rows, D), lambda i: (i, 0, 0)))
    return grad_call(down_grad_body, core, dec, enc, outs, bits, "down_grad")


def put_slab(core_ref, bits, ways, out_refs, step, made):
    made = made.astype(BF16).reshape(GROUPS, GROUP_ROWS, D)
    for part in range(2):

        @pl.when(step // 2 == part)
        def _():
            put(core_ref, bits[part], made, out_refs[part * ways : (part + 1) * ways])


def up_grad_body(bits, ways, core_ref, a0, a1, b0, b1, c, d, *out_refs):
    give = functools.partial(put_slab, core_ref, bits, ways, out_refs, pl.program_id(0))
    on_either(
        core_ref,
        lambda: give(tn(a0[...], b0[...]) + tn(a1[...], b1[...])),
        lambda: give(tn(c[...], d[...])),
    )


SLABS = (
    (2 * GROUP_ROWS, (GROUPS, GROUP_ROWS, D), lambda i: (0, jnp.minimum(i, 1), 0)),
    (2 * GROUP_ROWS, (GROUPS, GROUP_ROWS, D), lambda i: (0, jnp.maximum(i - 2, 0), 0)),
)


def up_grad(core, bits, factors, enc, enc_back):
    at = lambda place: (lambda i: (0, place))
    after = lambda place: (lambda i: (0, place + i))
    dec = [(a, (a.shape[0], D), at(DEC_H2)) for a in factors]
    dec += [(b, (b.shape[0], D), after(DEC_DPRE)) for b in factors]
    enc = [(enc, (enc.shape[0], D), at(ENC_H2)), (enc_back, (enc.shape[0], D), after(0))]
    return grad_call(up_grad_body, core, dec, enc, SLABS, bits, "up_grad")


def heads_grad_body(bits, ways, core_ref, a0, a1, b0, b1, c0, c1, s0, s1, d, e, small, *out_refs):
    step = pl.program_id(0)
    last = 2 * GROUP_ROWS

    def give(made):
        made = made.astype(BF16).reshape(GROUPS, GROUP_ROWS, D)
        for at in range(4):

            @pl.when(step == at)
            def _():
                part = at // 2
                rows = slice(at % 2 * GROUP_ROWS, (at % 2 + 1) * GROUP_ROWS)
                refs = out_refs[part * ways : (part + 1) * ways]
                if part == 0:
                    put(core_ref, bits[0], made, refs)
                else:
                    put(core_ref, bits[1], made, refs, rows)

    def dec():
        rights = [jnp.where(step == 3, c[...], b[...]) for b, c in ((b0, c0), (b1, c1))]
        give(tn(a0[...], rights[0]) + tn(a1[...], rights[1]))

    on_either(core_ref, dec, lambda: give(tn(d[...], e[...])))

    @pl.when(step == 3)
    def _():
        given = [s[VIS:, :].astype(F32) for s in (s0, s1)]
        extra = jnp.where(core_ref[0] == 0, small[...], given[0] + given[1]).astype(BF16)
        for out_ref in out_refs[ways:]:
            out_ref[:, last:, :] = jnp.broadcast_to(extra, (out_ref.shape[0], ROWS, D))


def heads_grad(core, bits, lates, dqkvs, backs, enc, enc_back, small):
    zero = lambda i: (0, 0)
    n, m = lates[0].shape[0], enc.shape[0]
    dec = [(a, (n, D), lambda i: (0, jnp.where(i < 3, LATE_H, LATE_ATT))) for a in lates]
    dec += [(b, (n, D), lambda i: (0, jnp.minimum(i, 2))) for b in dqkvs]
    dec += [(c, (n, D), lambda i: (0, LATE_DBRANCH)) for c in lates]
    dec += [(s, s.shape, zero) for s in backs]
    enc = [
        (enc, (m, D), lambda i: (0, jnp.where(i < 3, ENC_H, ENC_ATT))),
        (enc_back, (m, D), lambda i: (0, jnp.where(i < 3, ENC_DQKV + i, ENC_DBRANCH))),
        (small, small.shape, zero),
    ]
    rows = 2 * GROUP_ROWS + ROWS
    outs = (SLABS[0], (rows, (GROUPS, rows, D), lambda i: (0, 0, 0)))
    return grad_call(heads_grad_body, core, dec, enc, outs, bits, "heads_grad")


def swapped(value):
    return lax.ppermute(value, "pipe", [(0, 1), (1, 0)])


def across(value, bit):
    size = lax.axis_size("dp")
    return lax.ppermute(value, "dp", [(i, i ^ 2**bit) for i in range(size)])


def dp_bit(bit):
    return lax.rem(lax.axis_index("dp") // 2**bit, 2)


class Order:
    def __init__(self):
        self.last = None

    def __call__(self, step, *operands):
        if self.last is not None:
            operands, _ = lax.optimization_barrier((operands, self.last))
        made = step(*operands)
        self.last = jax.tree.leaves(made)[0]
        return made


def half_sum(stay, got, at, which, left):
    def part(value):
        rest = value.shape[1:]
        value = value.reshape(2**at, 2, left // 2**at, *rest)
        chosen = lax.dynamic_index_in_dim(value, which, 1, keepdims=False)
        return chosen.reshape(left, *rest).astype(F32)

    return (part(stay) + part(got)).astype(BF16)


class Sum:
    def __init__(self, arrays, order):
        go, self.stay = arrays
        self.value = None
        self.order = list(order)
        bit = self.order.pop(0)
        self.bits = [b for b in range(GROUPS.bit_length() - 2, -1, -1) if b != bit]
        self.got = across(go, bit)

    def step(self, run):
        if not self.order:
            self.value = run(
                lambda stay, got: (stay.astype(F32) + got.astype(F32))[0], self.stay, self.got
            )
            return
        bit = self.order.pop(0)
        shape = self.stay.shape
        at = self.bits.index(bit)
        self.bits.remove(bit)
        left = 2 ** len(self.bits)

        def half(which):
            return lambda stay, got: half_sum(stay, got, at, which, left)

        mine = dp_bit(bit)
        go = run(half(1 - mine), self.stay, self.got)
        stay = run(half(mine), self.stay, self.got)
        self.got, self.stay = across(go, bit), stay


class Joined(Sum):
    def __init__(self, one, two):
        self.parts, self.cut = (one, two), one.stay.shape[1]
        self.order, self.bits = one.order, one.bits
        self.value, self.apart = None, True

    def step(self, run):
        if not self.apart:
            super().step(run)
            if self.value is not None:
                self.parts[0].value = self.value[: self.cut]
                self.parts[1].value = self.value[self.cut :]
            return
        self.apart = False
        bit = self.order.pop(0)
        at = self.bits.index(bit)
        self.bits = [b for b in self.bits if b != bit]
        left = 2 ** len(self.bits)

        def both(which):
            def make(*values):
                pairs = zip(values[:2], values[2:])
                return jnp.concatenate(
                    [half_sum(stay, got, at, which, left) for stay, got in pairs], axis=1
                )

            return make

        operands = [one.stay for one in self.parts] + [one.got for one in self.parts]
        mine = dp_bit(bit)
        go = run(both(1 - mine), *operands)
        self.stay = run(both(mine), *operands)
        self.got = across(go, bit)


class PlainSum:
    def __init__(self, parts, slabs):
        whole = jnp.concatenate([part for (part,) in parts], axis=1)
        size = lax.axis_size("dp")
        rows = whole.shape[1] // slabs // ROWS * ROWS
        extra = whole[0, slabs * rows :] if slabs * rows < whole.shape[1] else None
        grad = whole[:, : slabs * rows].reshape(GROUPS, slabs, rows, D).transpose(0, 2, 1, 3)
        grad = grad.reshape(GROUPS * rows, slabs * D).astype(F32)
        mine = lax.psum_scatter(grad, "dp", scatter_dimension=0, tiled=True)
        mine = mine.reshape(-1, slabs, D).transpose(1, 0, 2).reshape(-1, D)
        if extra is not None:
            mine = jnp.concatenate([mine, lax.psum(extra.astype(F32), "dp")])
        self.value = mine

    def step(self, run):
        pass


ORDERS = {
    "down": ((2, 1, 0, 3), (1, 2, 0, 3)),
    "up": ((0, 1, 2, 3), (1, 0, 2, 3)),
    "heads": ((2, 1, 0, 3), (0, 1, 2, 3)),
}
EARLY_STEPS = ()
STEPS = (("down", 0), ("down", 1), ("up", 0), ("up", 1), ("J1", ("down", 0), ("down", 1)), ("heads", 1), ("J1", 0), ("heads", 0), ("J2", ("up", 0), ("up", 1)), ("J2", 0), ("J1", 0), ("heads", 1), ("J2", 0), ("heads", 0), ("J1", 0), ("heads", 1), ("heads", 0), ("J2", 0), ("heads", 1), ("heads", 0),)


def on_device(
    section_input,
    visible_slot,
    image_of_slot,
    qkv_weight,
    out_weight,
    up_weight,
    down_weight,
    norm_gain,
    up_bias,
    vectors,
):
    pipe = lax.axis_index("pipe")
    size = lax.axis_size("dp")
    halving = size == GROUPS
    core = jnp.stack([pipe] + [dp_bit(bit) for bit in range(GROUPS.bit_length() - 1)])
    own = [qkv_weight[0], out_weight[0], up_weight[0], down_weight[0]]
    params = [vectors.transpose(1, 0, 2), norm_gain, up_bias]
    layout = (visible_slot, image_of_slot)
    rows = MICRO * VIS
    run = Order()
    both = [[weight, swapped(weight)] for weight in own]

    enc_x, enc, enc_qkv, enc_lse, enc_mid, enc_slope, sent, packed = run(
        lambda section, *w: encoder_forward(rows, params, layout, section, w),
        section_input, *own,
    )
    other_sent, other_packed = swapped(sent), swapped(packed)
    core, sent = lax.optimization_barrier((core, sent))
    x, dec, late, qkv, lse, dmid, datt, small = run(
        lambda sent, other_sent, packed, other_packed, *w: decoder(
            S, packed, other_packed, layout, sent, other_sent, section_input,
            [w[2 * i : 2 * i + 2] for i in range(4)],
        ),
        sent, other_sent, packed, other_packed, *[w for pair in both for w in pair],
    )
    other_dec = swapped(dec)
    dqkv, back = run(
        lambda *a: decoder_back(S, packed, other_packed, layout, *a, both[0]),
        qkv, datt, lse, small, x, dmid, late,
    )
    other_back = swapped(back)
    (late, dqkv), _ = lax.optimization_barrier(((late, dqkv), other_back))
    other_dqkv, other_late = swapped(dqkv), swapped(late)
    sums = {}

    def begin(name, parts, slabs):
        if halving:
            for i, (arrays, order) in enumerate(zip(parts, ORDERS[name])):
                sums[name, i] = Sum(arrays, order)
        else:
            sums[name, 0] = PlainSum(parts, slabs)

    def bits_of(name):
        return tuple(order[0] for order in ORDERS[name]) if halving else None

    parts = run(
        lambda *a: down_grad(core, bits_of("down"), a[:2], section_input[0], enc, a[2:]),
        dec, other_dec, back, other_back,
    )
    begin("down", parts, 1)
    ready = lax.optimization_barrier((back, other_back, other_dqkv, other_late))
    enc_back, small, results = run(
        lambda dy, other_dy: encoder_back(
            rows, params, layout, dy, other_dy, enc_lse, enc_slope, enc_mid, enc_qkv, enc_x, enc,
            own,
        ),
        *ready[:2],
    )
    other_dqkv, other_late = ready[2:]
    parts = run(
        lambda *a: up_grad(core, bits_of("up"), a[:2], enc, a[2]), dec, other_dec, enc_back
    )
    begin("up", parts, 4)
    if halving:
        for name, i in EARLY_STEPS:
            sums[name, i].step(run)
    parts = run(
        lambda *a: heads_grad(core, bits_of("heads"), a[:2], a[2:4], a[4:6], enc, *a[6:]),
        late, other_late, dqkv, other_dqkv, back, other_back, enc_back, small,
    )
    begin("heads", parts, 4)
    results = run(lambda *a: place_results(core, *a), results, late, other_late)
    width = D // size
    hidden = FF // size

    def wide(slabs):
        return jnp.concatenate(
            [slabs[i * width : (i + 1) * width] for i in range(slabs.shape[0] // width)], axis=1
        )

    def finish(name, *values):
        grad = jnp.concatenate(values) if len(values) > 1 else values[0]
        if name == "down":
            return grad
        if name == "up":
            return wide(grad)
        small = grad[TILES * width :]
        at = lax.axis_index("dp")
        mine = lax.dynamic_slice_in_dim(small, at * width, width, 1)
        bias = lax.dynamic_slice_in_dim(
            small[UBIAS : UBIAS + TILES].reshape(FF), at * hidden, hidden, 0
        )
        return wide(grad[: 3 * width]), grad[3 * width : TILES * width], mine, bias

    finished = {}
    if halving:
        joined = {}
        for step in STEPS:
            if len(step) == 3:
                joined[step[0]] = Joined(sums[step[1]], sums[step[2]])
            elif step[0] in joined:
                joined[step[0]].step(run)
            else:
                sums[step].step(run)
    for name in ORDERS:
        finished[name] = finish(
            name, *[one.value for (kind, _), one in sums.items() if kind == name]
        )
    down, up = finished["down"], finished["up"]
    qkv_grad, out_grad, mine, bias_grad = finished["heads"]
    return (
        results[None],
        qkv_grad[None],
        out_grad[None],
        up[None],
        down[None],
        mine[GAIN1 : GAIN2 + 1][None],
        bias_grad[None],
        mine[:GAIN1][None],
    )


def solution(mesh):
    in_specs = (
        P("pipe", "dp", None, None),
        P("dp", None),
        P("dp", None),
        P("pipe", None, None),
        P("pipe", None, None),
        P("pipe", None, None),
        P("pipe", None, None),
        P("pipe", None, None),
        P("pipe", None),
        P("pipe", None, None),
    )
    out_specs = (
        P("pipe", "dp", None, None),
        P("pipe", "dp", None),
        P("pipe", "dp", None),
        P("pipe", "dp", None),
        P("pipe", "dp", None),
        P("pipe", None, "dp"),
        P("pipe", "dp"),
        P("pipe", None, "dp"),
    )
    return jax.shard_map(
        on_device, mesh=mesh, in_specs=in_specs, out_specs=out_specs, check_vma=False
    )
```
